32 devices in a mesh: group: 2 (over y), rows: 4 (over z), layer: 4 (over x, core).
Axes of the slice: x: 2, y: 2, z: 4, core: 2. Of those that a mesh axis runs over, the one named last changes fastest.
Arguments:
- train_grads: bfloat16 [1024, 8192], P(('group', 'rows'), 'layer'), parts along dimension 0, may hold values from -0.0625 to 0.0625
- query_grads: bfloat16 [4096, 8192], P(('group', 'rows'), 'layer'), parts along dimension 0, may hold values from -6 to 6
- eigenbases: bfloat16 [16, 512, 512], P('layer'), may hold values from -0.25 to 0.25
- eigenvalues: float32 [16, 512], P('layer'), may hold values from 0.05 to 5
- layer_offsets: int32 [16], P('layer'), may hold values from 0 to 7680, as said below
- query_doc_ids: int32 [4096], P(('group', 'rows')), parts along dimension 0, may hold values from 0 to 511
Outputs:
- scores: float32 [4, 512, 1024], P(None, 'layer', ('group', 'rows')), parts along dimension 2
The draws below stay inside these ranges and needn't reach their ends.
There are 2 independent parts, one for each index of `group`. The reference program is written for one: setup_inputs(seed, part) draws one part's arguments, and reference() takes and returns one part's arrays. A program takes and returns all parts, laid end to end along the dimension named above; an argument that names none is the same for every part. Nothing has to cross between parts.
Inputs may be any that keep to these rules, and one draw needn't show every extreme that they name: `layer_offsets`: the layers l with equal l // 4 take the 4 column blocks of width 512 starting at 512 * 4 * (l // 4), in some order.
All inputs are finite; a program needn't handle non-finite values.
Results may differ from the reference program's by a relative error of at most 0.0037.
Values may be sent and summed in bfloat16 or wider, within the bound.
No kernel may reach another device: no remote copies, remote signals or barrier semaphores. Data moves between devices by JAX's collectives and lax.ppermute only.
A program may use at most 64 MiB of HBM per device.

```python
import math
import jax
import jax.numpy as jnp
from jax import lax

LDIM = 512
LAY_DEV = 4
QB = 512
STEPS = 4
DOC_DEV = 128
LAYERS = 16
DIMS = 8192
DOCS = 512
NQ = 2048
N_ROWS = 4


def draw_layer_offsets(key, part):
    key = jax.random.fold_in(key, 7)
    groups = LAYERS // LAY_DEV
    subkeys = jax.random.split(key, groups)
    slot_order = jax.vmap(lambda single: jax.random.permutation(single, LAY_DEV))(subkeys)
    group_base = (jnp.arange(groups, dtype=jnp.int32) * LAY_DEV)[:, None]
    return ((slot_order.astype(jnp.int32) + group_base) * LDIM).reshape(LAYERS).astype(jnp.int32)


def plant(array, rng, least, top_value):
    longest = array.shape.index(max(array.shape))
    spots = []
    for shift in (0, 1):
        where = [jax.random.randint(jax.random.fold_in(rng, axis), (), 0, length) for axis, length in enumerate(array.shape)]
        where[longest] = (where[longest] + shift) % array.shape[longest]
        spots.append(tuple(where))
    return array.at[spots[0]].set(least).at[spots[1]].set(top_value)


def levels(own_key, shape, shards, least, top_value):
    def one(position, blocks):
        steps = jax.random.uniform(jax.random.fold_in(jax.random.fold_in(own_key, 6), position), (blocks,), jnp.float32, least / len(shards), top_value / len(shards))
        return jnp.repeat(jnp.exp(steps), shape[position] // blocks).reshape((-1,) + (1,) * (len(shape) - position - 1))

    gain = one(*shards[0])
    for cut in shards[1:]:
        gain = gain * one(*cut)
    return gain


def centred(key, extent, scale, reach, cuts=(), held_as=jnp.bfloat16):
    values = jax.random.normal(key, extent, jnp.float32) * scale
    if len(cuts) > 0:
        values = levels(key, extent, cuts, -0.22, 0.18) * values
    return jnp.clip(values, min=-reach, max=reach).astype(held_as)


def setup_inputs(seed: int = 0, part: int = 0) -> dict:
    streams_of = jax.random.split(jax.random.key(seed), 7)
    own_keys = jax.random.split(jax.random.fold_in(streams_of[6], part), 7)
    return {
        "train_grads": centred(own_keys[0], (DOCS, DIMS), DIMS ** -0.5, 0.0625, ((0, 4), (1, 4))),
        "query_grads": centred(own_keys[1], (NQ, DIMS), 1.0, 6.0, ((0, 4), (1, 4))),
        "eigenbases": centred(streams_of[2], (LAYERS, LDIM, LDIM), LDIM ** -0.5, 0.25, ((0, 4),)),
        "eigenvalues": jnp.clip(jnp.exp(math.log(5.0) - 4.6051702 * jax.random.uniform(streams_of[3], (LAYERS, LDIM), jnp.float32) ** levels(streams_of[3], (LAYERS, LDIM), ((0, 4),), -0.2, 0.2)), 0.05, 5.0),
        "layer_offsets": draw_layer_offsets(jax.random.fold_in(streams_of[6], 71), part),
        "query_doc_ids": plant(jax.random.randint(own_keys[5], (NQ,), 0, DOCS), jax.random.fold_in(own_keys[5], 1), 0, DOCS - 1).astype(jnp.int32),
    }


DAMPING = 0.05


def precondition(block, basis, values):
    projected = jnp.dot(block, basis, preferred_element_type=jnp.float32)
    scaled = (projected / (values + DAMPING)).astype(jnp.bfloat16)
    return jnp.dot(scaled, basis.T, preferred_element_type=jnp.float32).astype(jnp.bfloat16)


def reference(train_grads, query_grads, eigenbases, eigenvalues, layer_offsets, query_doc_ids):
    columns = []
    for layer in range(LAYERS):
        columns.append(lax.dynamic_slice_in_dim(train_grads, layer_offsets[layer].astype(jnp.int32), LDIM, 1))
    ordered = jnp.concatenate(columns, axis=1)
    conditioned = jnp.concatenate([precondition(query_grads[:, layer * LDIM:(layer + 1) * LDIM], eigenbases[layer], eigenvalues[layer]) for layer in range(LAYERS)], axis=1)
    query_blocks = conditioned.reshape(N_ROWS, QB, DIMS)
    id_blocks = query_doc_ids.reshape(N_ROWS, QB)
    doc_blocks = ordered.reshape(N_ROWS, DOC_DEV, DIMS)

    def one_shard(shard):
        documents = lax.dynamic_index_in_dim(doc_blocks, shard, 0, keepdims=False)
        doc_ids = shard * DOC_DEV + jnp.arange(DOC_DEV, dtype=jnp.int32)
        tile_list = []
        for step in range(STEPS):
            source = ((shard - step) % N_ROWS).astype(jnp.int32)
            queries = lax.dynamic_index_in_dim(query_blocks, source, 0, keepdims=False)
            query_ids = lax.dynamic_index_in_dim(id_blocks, source, 0, keepdims=False)
            tile = lax.dot_general(queries, documents, (((1,), (1,)), ((), ())), preferred_element_type=jnp.float32)
            tile = jnp.where(query_ids[:, None] == doc_ids[None, :], jnp.zeros_like(tile), tile)
            tile_list.append(tile)
        return jnp.stack(tile_list, axis=0)

    stacked = lax.map(one_shard, jnp.arange(N_ROWS, dtype=jnp.int32))
    return jnp.transpose(stacked, (1, 2, 0, 3)).reshape(STEPS, QB, DOCS)
```

```python
import functools

import jax
import jax.numpy as jnp
from jax import lax
from jax.experimental import pallas as pl
from jax.experimental.pallas import tpu as pltpu
from jax.sharding import PartitionSpec as P

LDIM = 512
LAY_DEV = 4
STEPS = 4
DAMPING = 0.05
NT = (((1,), (1,)), ((), ()))
VMEM_LIMIT = 40 * 1024 * 1024


def precondition_kernel(slots, query_ref, basis_ref, values_ref, out_ref):
    layer = pl.program_id(0)
    basis = basis_ref[0]
    projected = jnp.dot(query_ref[...], basis, preferred_element_type=jnp.float32)
    scaled = (projected / (values_ref[pl.ds(layer, 1), :] + DAMPING)).astype(jnp.bfloat16)
    out_ref[...] = lax.dot_general(scaled, basis, NT, preferred_element_type=jnp.float32).astype(jnp.bfloat16)


def precondition(query_grads, eigenbases, eigenvalues, slots):
    rows = query_grads.shape[0]
    return pl.pallas_call(
        precondition_kernel,
        out_shape=jax.ShapeDtypeStruct((rows, LAY_DEV * LDIM), jnp.bfloat16),
        grid_spec=pltpu.PrefetchScalarGridSpec(
            num_scalar_prefetch=1,
            grid=(LAY_DEV,),
            in_specs=[
                pl.BlockSpec((rows, LDIM), lambda layer, slots: (0, layer)),
                pl.BlockSpec((1, LDIM, LDIM), lambda layer, slots: (layer, 0, 0)),
                pl.BlockSpec((LAY_DEV, LDIM), lambda layer, slots: (0, 0)),
            ],
            out_specs=pl.BlockSpec((rows, LDIM), lambda layer, slots: (0, slots[layer])),
        ),
        compiler_params=pltpu.CompilerParams(vmem_limit_bytes=VMEM_LIMIT),
        cost_estimate=pl.CostEstimate(
            flops=4 * rows * LAY_DEV * LDIM * LDIM, bytes_accessed=6 * 1024 * 1024, transcendentals=0
        ),
    )(slots, query_grads, eigenbases, eigenvalues)


def score_kernel(shares, place, queries_ref, documents_ref, ids_ref, *refs):
    *out_refs, held = refs
    tile = lax.dot_general(queries_ref[...], documents_ref[...], NT, preferred_element_type=jnp.float32)
    doc_ids = place[1] + lax.broadcasted_iota(jnp.int32, tile.shape, 1)
    held[...] = jnp.where(ids_ref[...] == doc_ids, 0.0, tile)
    share_rows = tile.shape[0] // shares
    for turn in range(shares):
        share = lax.rem(place[0] + turn, shares)
        first = pl.multiple_of(share * share_rows, share_rows)
        out_refs[turn][...] = held[pl.ds(first, share_rows), :].astype(jnp.bfloat16)


def partial_scores(conditioned, documents, query_ids, place, shares):
    rows, dims = conditioned.shape
    docs = documents.shape[0]
    vmem = pl.BlockSpec(memory_space=pltpu.VMEM)
    return pl.pallas_call(
        functools.partial(score_kernel, shares),
        out_shape=[jax.ShapeDtypeStruct((rows // shares, docs), jnp.bfloat16)] * shares,
        in_specs=[pl.BlockSpec(memory_space=pltpu.SMEM), vmem, vmem, vmem],
        out_specs=[vmem] * shares,
        scratch_shapes=[pltpu.VMEM((rows, docs), jnp.float32)],
        compiler_params=pltpu.CompilerParams(vmem_limit_bytes=VMEM_LIMIT),
        cost_estimate=pl.CostEstimate(
            flops=2 * rows * docs * dims, bytes_accessed=2 * dims * (rows + docs), transcendentals=0
        ),
    )(place, conditioned, documents, query_ids)


def sum_kernel(shares, *refs):
    *in_refs, out_ref = refs
    for step in range(STEPS):
        total = in_refs[step * shares][...].astype(jnp.float32)
        for turn in range(1, shares):
            total += in_refs[step * shares + turn][...].astype(jnp.float32)
        out_ref[step] = total


def sum_shares(blocks, shares):
    vmem = pl.BlockSpec(memory_space=pltpu.VMEM)
    return pl.pallas_call(
        functools.partial(sum_kernel, shares),
        out_shape=jax.ShapeDtypeStruct((STEPS,) + blocks[0].shape, jnp.float32),
        in_specs=[vmem] * len(blocks),
        out_specs=vmem,
    )(*blocks)


def local(train_grads, query_grads, eigenbases, eigenvalues, layer_offsets, query_doc_ids):
    n_rows = lax.axis_size("rows")
    shares = lax.axis_size("layer")
    row_index = lax.axis_index("rows")
    layer_index = lax.axis_index("layer")
    doc_rows = train_grads.shape[0]

    documents = [train_grads]
    for step in range(1, STEPS):
        pairs = [(source, (source - step) % n_rows) for source in range(n_rows)]
        documents.append(lax.ppermute(train_grads, "rows", pairs))

    slots = layer_offsets // LDIM - layer_index * LAY_DEV
    conditioned = precondition(query_grads, eigenbases, eigenvalues, slots)
    query_ids = query_doc_ids[:, None]

    blocks = [None] * (STEPS * shares)
    for step in range(STEPS):
        doc_base = (row_index + step) % n_rows * doc_rows
        place = jnp.stack([layer_index, doc_base]).astype(jnp.int32)
        tiles = partial_scores(conditioned, documents[step], query_ids, place, shares)
        for turn in range(shares):
            pairs = [
                (row * shares + lay, (row + step) % n_rows * shares + (lay + turn) % shares)
                for row in range(n_rows)
                for lay in range(shares)
            ]
            tile = tiles[turn]
            if step or turn:
                tile = lax.ppermute(tile, ("rows", "layer"), pairs)
            blocks[step * shares + turn] = tile
    return sum_shares(blocks, shares)


def solution(mesh):
    in_specs = (
        P(("group", "rows"), "layer"),
        P(("group", "rows"), "layer"),
        P("layer", None, None),
        P("layer", None),
        P("layer"),
        P(("group", "rows")),
    )
    out_specs = P(None, "layer", ("group", "rows"))
    return jax.shard_map(local, mesh=mesh, in_specs=in_specs, out_specs=out_specs, check_vma=False)
```

```python
import functools

import jax
import jax.numpy as jnp
from jax import lax
from jax.experimental import pallas as pl
from jax.experimental.pallas import tpu as pltpu
from jax.sharding import PartitionSpec as P

LDIM = 512
LAY_DEV = 4
STEPS = 4
DAMPING = 0.05
NT = (((1,), (1,)), ((), ()))
VMEM_LIMIT = 40 * 1024 * 1024


def precondition_kernel(slots, query_ref, basis_ref, values_ref, out_ref):
    layer = pl.program_id(0)
    basis = basis_ref[0]
    projected = jnp.dot(query_ref[...], basis, preferred_element_type=jnp.float32)
    scaled = (projected / (values_ref[pl.ds(layer, 1), :] + DAMPING)).astype(jnp.bfloat16)
    out_ref[...] = lax.dot_general(scaled, basis, NT, preferred_element_type=jnp.float32).astype(jnp.bfloat16)


def precondition(query_grads, eigenbases, eigenvalues, slots):
    rows = query_grads.shape[0]
    return pl.pallas_call(
        precondition_kernel,
        out_shape=jax.ShapeDtypeStruct((rows, LAY_DEV * LDIM), jnp.bfloat16),
        grid_spec=pltpu.PrefetchScalarGridSpec(
            num_scalar_prefetch=1,
            grid=(LAY_DEV,),
            in_specs=[
                pl.BlockSpec((rows, LDIM), lambda layer, slots: (0, layer)),
                pl.BlockSpec((1, LDIM, LDIM), lambda layer, slots: (layer, 0, 0)),
                pl.BlockSpec((LAY_DEV, LDIM), lambda layer, slots: (0, 0)),
            ],
            out_specs=pl.BlockSpec((rows, LDIM), lambda layer, slots: (0, slots[layer])),
        ),
        compiler_params=pltpu.CompilerParams(vmem_limit_bytes=VMEM_LIMIT),
        cost_estimate=pl.CostEstimate(
            flops=4 * rows * LAY_DEV * LDIM * LDIM, bytes_accessed=6 * 1024 * 1024, transcendentals=0
        ),
    )(slots, query_grads, eigenbases, eigenvalues)


def score_kernel(shares, row, queries_ref, documents_ref, ids_ref, out_ref):
    tile = lax.dot_general(queries_ref[...], documents_ref[...], NT, preferred_element_type=jnp.float32)
    doc_rows = out_ref.shape[3]
    share_rows = out_ref.shape[2]
    doc_ids = row[0] + lax.broadcasted_iota(jnp.int32, tile.shape, 1)
    tile = jnp.where(ids_ref[...] == doc_ids, 0.0, tile).astype(jnp.bfloat16)
    for owner in range(out_ref.shape[0]):
        for share in range(shares):
            out_ref[owner, share] = tile[
                share * share_rows : (share + 1) * share_rows, owner * doc_rows : (owner + 1) * doc_rows
            ]


def partial_scores(conditioned, documents, query_ids, first_doc, doc_rows, shares):
    rows, dims = conditioned.shape
    docs = documents.shape[0]
    vmem = pl.BlockSpec(memory_space=pltpu.VMEM)
    return pl.pallas_call(
        functools.partial(score_kernel, shares),
        out_shape=jax.ShapeDtypeStruct((docs // doc_rows, shares, rows // shares, doc_rows), jnp.bfloat16),
        in_specs=[pl.BlockSpec(memory_space=pltpu.SMEM), vmem, vmem, vmem],
        out_specs=vmem,
        compiler_params=pltpu.CompilerParams(vmem_limit_bytes=VMEM_LIMIT),
        cost_estimate=pl.CostEstimate(
            flops=2 * rows * docs * dims, bytes_accessed=2 * dims * (rows + docs), transcendentals=0
        ),
    )(first_doc, conditioned, documents, query_ids)


def sum_kernel(row, in_ref, out_ref):
    steps, shares = in_ref.shape[:2]
    for step in range(steps):
        source = lax.rem(row[0] - step + steps, steps)
        total = in_ref[source, 0].astype(jnp.float32)
        for share in range(1, shares):
            total += in_ref[source, share].astype(jnp.float32)
        out_ref[step] = total


def sum_shares(blocks, row):
    vmem = pl.BlockSpec(memory_space=pltpu.VMEM)
    return pl.pallas_call(
        sum_kernel,
        out_shape=jax.ShapeDtypeStruct(blocks.shape[:1] + blocks.shape[2:], jnp.float32),
        in_specs=[pl.BlockSpec(memory_space=pltpu.SMEM), vmem],
        out_specs=vmem,
    )(row, blocks)


def local(train_grads, query_grads, eigenbases, eigenvalues, layer_offsets, query_doc_ids):
    n_rows = lax.axis_size("rows")
    shares = lax.axis_size("layer")
    row = lax.axis_index("rows").astype(jnp.int32)
    layer_index = lax.axis_index("layer")
    doc_rows = train_grads.shape[0]
    query_ids = query_doc_ids[:, None]
    slots = layer_offsets // LDIM - layer_index * LAY_DEV

    if n_rows == STEPS:
        documents = lax.all_gather(train_grads, "rows", tiled=True)
        conditioned = precondition(query_grads, eigenbases, eigenvalues, slots)
        tiles = partial_scores(conditioned, documents, query_ids, jnp.zeros((1,), jnp.int32), doc_rows, shares)
        blocks = tiles.reshape((n_rows * shares,) + tiles.shape[2:])
        blocks = lax.all_to_all(blocks, ("rows", "layer"), 0, 0, tiled=True)
        return sum_shares(blocks.reshape(tiles.shape), row[None])

    conditioned = precondition(query_grads, eigenbases, eigenvalues, slots)
    blocks = []
    for step in range(STEPS):
        back = [(source, (source - step) % n_rows) for source in range(n_rows)]
        documents = lax.ppermute(train_grads, "rows", back) if step else train_grads
        first_doc = (row + step) % n_rows * doc_rows
        tiles = partial_scores(conditioned, documents, query_ids, first_doc[None], doc_rows, shares)
        shared = lax.all_to_all(tiles[0], "layer", 0, 0, tiled=True)
        onward = [(source, (source + step) % n_rows) for source in range(n_rows)]
        blocks.append(lax.ppermute(shared, "rows", onward) if step else shared)
    return jnp.sum(jnp.stack(blocks).astype(jnp.float32), axis=1)


def solution(mesh):
    in_specs = (
        P(("group", "rows"), "layer"),
        P(("group", "rows"), "layer"),
        P("layer", None, None),
        P("layer", None),
        P("layer"),
        P(("group", "rows")),
    )
    out_specs = P(None, "layer", ("group", "rows"))
    return jax.shard_map(local, mesh=mesh, in_specs=in_specs, out_specs=out_specs, check_vma=False)
```

```python
import functools

import jax
import jax.numpy as jnp
from jax import lax
from jax.experimental import pallas as pl
from jax.experimental.pallas import tpu as pltpu
from jax.sharding import PartitionSpec as P

LDIM = 512
LAY_DEV = 4
STEPS = 4
DAMPING = 0.05
NT = (((1,), (1,)), ((), ()))
VMEM_LIMIT = 40 * 1024 * 1024


def precondition_kernel(slots, query_ref, basis_ref, values_ref, out_ref):
    layer = pl.program_id(0)
    basis = basis_ref[0]
    projected = jnp.dot(query_ref[...], basis, preferred_element_type=jnp.float32)
    scaled = (projected / (values_ref[pl.ds(layer, 1), :] + DAMPING)).astype(jnp.bfloat16)
    out_ref[...] = lax.dot_general(scaled, basis, NT, preferred_element_type=jnp.float32).astype(jnp.bfloat16)


def precondition(query_grads, eigenbases, eigenvalues, slots):
    rows = query_grads.shape[0]
    return pl.pallas_call(
        precondition_kernel,
        out_shape=jax.ShapeDtypeStruct((rows, LAY_DEV * LDIM), jnp.bfloat16),
        grid_spec=pltpu.PrefetchScalarGridSpec(
            num_scalar_prefetch=1,
            grid=(LAY_DEV,),
            in_specs=[
                pl.BlockSpec((rows, LDIM), lambda layer, slots: (0, layer)),
                pl.BlockSpec((1, LDIM, LDIM), lambda layer, slots: (layer, 0, 0)),
                pl.BlockSpec((LAY_DEV, LDIM), lambda layer, slots: (0, 0)),
            ],
            out_specs=pl.BlockSpec((rows, LDIM), lambda layer, slots: (0, slots[layer])),
        ),
        compiler_params=pltpu.CompilerParams(vmem_limit_bytes=VMEM_LIMIT),
        cost_estimate=pl.CostEstimate(
            flops=4 * rows * LAY_DEV * LDIM * LDIM, bytes_accessed=6 * 1024 * 1024, transcendentals=0
        ),
    )(slots, query_grads, eigenbases, eigenvalues)


def score_kernel(shares, turned, place, queries_ref, ids_ref, *refs):
    if turned:
        document_refs, out_refs, held = refs[: -1 - shares], refs[-1 - shares : -1], refs[-1]
    else:
        document_refs, out_refs = refs[:-1], refs[-1:]
    doc_rows = document_refs[0].shape[0]
    for spot, document_ref in enumerate(document_refs):
        tile = lax.dot_general(queries_ref[...], document_ref[...], NT, preferred_element_type=jnp.float32)
        doc_ids = place[1 + spot] + lax.broadcasted_iota(jnp.int32, tile.shape, 1)
        tile = jnp.where(ids_ref[...] == doc_ids, 0.0, tile)
        share_rows = tile.shape[0] // shares
        if turned:
            held[...] = tile
            for turn in range(shares):
                first = pl.multiple_of(lax.rem(place[0] + turn, shares) * share_rows, share_rows)
                out_refs[turn][...] = held[pl.ds(first, share_rows), :].astype(jnp.bfloat16)
        else:
            columns = slice(spot * doc_rows, (spot + 1) * doc_rows)
            for share in range(shares):
                part = tile[share * share_rows : (share + 1) * share_rows]
                out_refs[0][share, :, columns] = part.astype(jnp.bfloat16)


def partial_scores(conditioned, query_ids, documents, place, shares, turned=False):
    rows, dims = conditioned.shape
    doc_rows = documents[0].shape[0]
    docs = doc_rows * len(documents)
    vmem = pl.BlockSpec(memory_space=pltpu.VMEM)
    if turned:
        out_shape = [jax.ShapeDtypeStruct((rows // shares, docs), jnp.bfloat16)] * shares
        scratch = [pltpu.VMEM((rows, docs), jnp.float32)]
    else:
        out_shape = jax.ShapeDtypeStruct((shares, rows // shares, docs), jnp.bfloat16)
        scratch = []
    return pl.pallas_call(
        functools.partial(score_kernel, shares, turned),
        out_shape=out_shape,
        in_specs=[pl.BlockSpec(memory_space=pltpu.SMEM)] + [vmem] * (2 + len(documents)),
        out_specs=[vmem] * shares if turned else vmem,
        scratch_shapes=scratch,
        compiler_params=pltpu.CompilerParams(vmem_limit_bytes=VMEM_LIMIT),
        cost_estimate=pl.CostEstimate(
            flops=2 * rows * docs * dims, bytes_accessed=2 * dims * (rows + docs), transcendentals=0
        ),
    )(place, conditioned, query_ids, *documents)


def sum_kernel(in_ref, *out_refs):
    doc_rows = out_refs[0].shape[1]
    for spot, out_ref in enumerate(out_refs):
        columns = slice(spot * doc_rows, (spot + 1) * doc_rows)
        total = in_ref[0, :, columns].astype(jnp.float32)
        for share in range(1, in_ref.shape[0]):
            total += in_ref[share, :, columns].astype(jnp.float32)
        out_ref[...] = total


def sum_shares(tiles, doc_rows):
    tiles = lax.all_to_all(tiles, "layer", 0, 0, tiled=True)
    shares, share_rows, docs = tiles.shape
    vmem = pl.BlockSpec(memory_space=pltpu.VMEM)
    return pl.pallas_call(
        sum_kernel,
        out_shape=[jax.ShapeDtypeStruct((share_rows, doc_rows), jnp.float32)] * (docs // doc_rows),
        in_specs=[vmem],
        out_specs=[vmem] * (docs // doc_rows),
    )(tiles)


def final_kernel(row, own_ref, ahead_ref, behind_ref, across_ref, *refs):
    *last_refs, out_ref = refs
    last = last_refs[0][...].astype(jnp.float32)
    for last_ref in last_refs[1:]:
        last += last_ref[...].astype(jnp.float32)
    out_ref[0] = own_ref[...]
    out_ref[1] = jnp.where(row[0] == 0, last, ahead_ref[...])
    out_ref[2] = across_ref[...]
    out_ref[3] = jnp.where(row[0] == STEPS - 1, last, behind_ref[...])


def final_scores(row, own, ahead, behind, across, last):
    vmem = pl.BlockSpec(memory_space=pltpu.VMEM)
    return pl.pallas_call(
        final_kernel,
        out_shape=jax.ShapeDtypeStruct((STEPS,) + own.shape, jnp.float32),
        in_specs=[pl.BlockSpec(memory_space=pltpu.SMEM)] + [vmem] * (4 + len(last)),
        out_specs=vmem,
    )(row[None], own, ahead, behind, across, *last)


def along_line(documents, conditioned, query_ids, row, layer_index, shares):
    doc_rows = documents.shape[0]

    def hop(value, *pairs):
        return lax.ppermute(value, "rows", pairs)

    def scores(blocks, sources, turned=False):
        place = jnp.stack([layer_index] + [source * doc_rows for source in sources]).astype(jnp.int32)
        return partial_scores(conditioned, query_ids, blocks, place, shares, turned)

    below = hop(documents, (0, 1), (1, 2), (2, 3))
    above = hop(documents, (3, 2), (2, 1), (1, 0))
    below, above, conditioned = lax.optimization_barrier((below, above, conditioned))
    below2 = hop(below, (1, 2), (2, 3))
    above2 = hop(above, (2, 1), (1, 0))

    tiles = scores([documents, below, above], [row, row - 1, row + 1])
    own, lower, upper = sum_shares(tiles, doc_rows)
    behind = hop(lower, (1, 0), (2, 1), (3, 2))
    ahead = hop(upper, (0, 1), (1, 2), (2, 3))

    opposite = below2 + above2
    final = hop(opposite, (2, 3), (1, 0))
    tiles = scores([opposite], [(row + 2) % STEPS])
    (across,) = sum_shares(tiles, doc_rows)
    across = hop(across, (0, 2), (1, 3), (2, 0), (3, 1))

    tiles = scores([final], [STEPS - 1 - row], turned=True)
    last = []
    for turn, tile in enumerate(tiles):
        pairs = [
            (here * shares + lay, there * shares + (lay + turn) % shares)
            for here, there in ((0, 3), (3, 0))
            for lay in range(shares)
        ]
        last.append(lax.ppermute(tile, ("rows", "layer"), pairs))
    return final_scores(row, own, ahead, behind, across, last)


def around_ring(documents, conditioned, query_ids, row, layer_index, shares):
    n_rows = lax.axis_size("rows")
    doc_rows = documents.shape[0]
    result = []
    for step in range(STEPS):
        back = [(source, (source - step) % n_rows) for source in range(n_rows)]
        block = lax.ppermute(documents, "rows", back) if step else documents
        place = jnp.stack([layer_index, (row + step) % n_rows * doc_rows]).astype(jnp.int32)
        (total,) = sum_shares(partial_scores(conditioned, query_ids, [block], place, shares), doc_rows)
        onward = [(source, (source + step) % n_rows) for source in range(n_rows)]
        result.append(lax.ppermute(total, "rows", onward) if step else total)
    return jnp.stack(result)


def local(train_grads, query_grads, eigenbases, eigenvalues, layer_offsets, query_doc_ids):
    row = lax.axis_index("rows").astype(jnp.int32)
    layer_index = lax.axis_index("layer").astype(jnp.int32)
    slots = layer_offsets // LDIM - layer_index * LAY_DEV
    conditioned = precondition(query_grads, eigenbases, eigenvalues, slots)
    plan = along_line if lax.axis_size("rows") == STEPS else around_ring
    return plan(train_grads, conditioned, query_doc_ids[:, None], row, layer_index, lax.axis_size("layer"))


def solution(mesh):
    in_specs = (
        P(("group", "rows"), "layer"),
        P(("group", "rows"), "layer"),
        P("layer", None, None),
        P("layer", None),
        P("layer"),
        P(("group", "rows")),
    )
    out_specs = P(None, "layer", ("group", "rows"))
    return jax.shard_map(local, mesh=mesh, in_specs=in_specs, out_specs=out_specs, check_vma=False)
```

```python
import functools

import jax
import jax.numpy as jnp
from jax import lax
from jax.experimental import pallas as pl
from jax.experimental.pallas import tpu as pltpu
from jax.sharding import PartitionSpec as P

LDIM = 512
LAY_DEV = 4
STEPS = 4
DAMPING = 0.05
NT = (((1,), (1,)), ((), ()))
VMEM_LIMIT = 40 * 1024 * 1024


def precondition_kernel(slots, query_ref, basis_ref, values_ref, out_ref):
    layer = pl.program_id(0)
    basis = basis_ref[0]
    projected = jnp.dot(query_ref[...], basis, preferred_element_type=jnp.float32)
    scaled = (projected / (values_ref[pl.ds(layer, 1), :] + DAMPING)).astype(jnp.bfloat16)
    out_ref[...] = lax.dot_general(scaled, basis, NT, preferred_element_type=jnp.float32).astype(jnp.bfloat16)


def precondition(query_grads, eigenbases, eigenvalues, slots):
    rows = query_grads.shape[0]
    return pl.pallas_call(
        precondition_kernel,
        out_shape=jax.ShapeDtypeStruct((rows, LAY_DEV * LDIM), jnp.bfloat16),
        grid_spec=pltpu.PrefetchScalarGridSpec(
            num_scalar_prefetch=1,
            grid=(LAY_DEV,),
            in_specs=[
                pl.BlockSpec((rows, LDIM), lambda layer, slots: (0, layer)),
                pl.BlockSpec((1, LDIM, LDIM), lambda layer, slots: (layer, 0, 0)),
                pl.BlockSpec((LAY_DEV, LDIM), lambda layer, slots: (0, 0)),
            ],
            out_specs=pl.BlockSpec((rows, LDIM), lambda layer, slots: (0, slots[layer])),
        ),
        compiler_params=pltpu.CompilerParams(vmem_limit_bytes=VMEM_LIMIT),
        cost_estimate=pl.CostEstimate(
            flops=4 * rows * LAY_DEV * LDIM * LDIM, bytes_accessed=6 * 1024 * 1024, transcendentals=0
        ),
    )(slots, query_grads, eigenbases, eigenvalues)


def score_kernel(shares, block_of, turned, place, queries_ref, ids_ref, *refs):
    if turned:
        document_refs, out_refs, held = refs[: -1 - shares], refs[-1 - shares : -1], refs[-1]
    else:
        document_refs, out_refs = refs[:-1], refs[-1:]
    doc_rows = document_refs[0].shape[0]
    for spot, document_ref in enumerate(document_refs):
        tile = lax.dot_general(queries_ref[...], document_ref[...], NT, preferred_element_type=jnp.float32)
        doc_ids = block_of[spot](place[1]) * doc_rows + lax.broadcasted_iota(jnp.int32, tile.shape, 1)
        tile = jnp.where(ids_ref[...] == doc_ids, 0.0, tile)
        share_rows = tile.shape[0] // shares
        if turned:
            held[...] = tile
            for turn in range(shares):
                first = pl.multiple_of(lax.rem(place[0] + turn, shares) * share_rows, share_rows)
                out_refs[turn][...] = held[pl.ds(first, share_rows), :].astype(jnp.bfloat16)
        else:
            columns = slice(spot * doc_rows, (spot + 1) * doc_rows)
            for share in range(shares):
                part = tile[share * share_rows : (share + 1) * share_rows]
                out_refs[0][share, :, columns] = part.astype(jnp.bfloat16)


def partial_scores(conditioned, query_ids, documents, block_of, place, shares, turned=False):
    rows, dims = conditioned.shape
    doc_rows = documents[0].shape[0]
    docs = doc_rows * len(documents)
    vmem = pl.BlockSpec(memory_space=pltpu.VMEM)
    if turned:
        out_shape = [jax.ShapeDtypeStruct((rows // shares, docs), jnp.bfloat16)] * shares
        scratch = [pltpu.VMEM((rows, docs), jnp.float32)]
    else:
        out_shape = jax.ShapeDtypeStruct((shares, rows // shares, docs), jnp.bfloat16)
        scratch = []
    return pl.pallas_call(
        functools.partial(score_kernel, shares, block_of, turned),
        out_shape=out_shape,
        in_specs=[pl.BlockSpec(memory_space=pltpu.SMEM)] + [vmem] * (2 + len(documents)),
        out_specs=[vmem] * shares if turned else vmem,
        scratch_shapes=scratch,
        compiler_params=pltpu.CompilerParams(vmem_limit_bytes=VMEM_LIMIT),
        cost_estimate=pl.CostEstimate(
            flops=2 * rows * docs * dims, bytes_accessed=2 * dims * (rows + docs), transcendentals=0
        ),
    )(place, conditioned, query_ids, *documents)


def sum_kernel(in_ref, *out_refs):
    doc_rows = out_refs[0].shape[1]
    for spot, out_ref in enumerate(out_refs):
        columns = slice(spot * doc_rows, (spot + 1) * doc_rows)
        total = in_ref[0, :, columns].astype(jnp.float32)
        for share in range(1, in_ref.shape[0]):
            total += in_ref[share, :, columns].astype(jnp.float32)
        out_ref[...] = total


def sum_shares(tiles, doc_rows):
    tiles = lax.all_to_all(tiles, "layer", 0, 0, tiled=True)
    shares, share_rows, docs = tiles.shape
    vmem = pl.BlockSpec(memory_space=pltpu.VMEM)
    return pl.pallas_call(
        sum_kernel,
        out_shape=[jax.ShapeDtypeStruct((share_rows, doc_rows), jnp.float32)] * (docs // doc_rows),
        in_specs=[vmem],
        out_specs=[vmem] * (docs // doc_rows),
    )(tiles)


ROUND_ONE = ((0, 2), (3, 1), (2, 3), (1, 0))
ROUND_TWO = ((0, 1), (3, 2), (1, 3), (2, 0))
ROUND_INNER = ((1, 2), (2, 1))
ROUND_OUTER = ((2, 3), (1, 0))
BLOCK_ONE = (1, 3, 0, 2)
BLOCK_TWO = (2, 0, 3, 1)
BLOCK_LAST = (3, 2, 1, 0)


def pick(table):
    def entry(row):
        value = jnp.int32(table[0])
        for index in range(1, len(table)):
            value = jnp.where(row == index, jnp.int32(table[index]), value)
        return value

    return entry


def step_of(table):
    return pick([(block - table.index(block)) % STEPS for block in range(STEPS)])


def final_kernel(place, own_ref, first_ref, *refs):
    *late_refs, out_ref = refs
    out_ref[0] = own_ref[...]
    out_ref[step_of(BLOCK_ONE)(place[1])] = first_ref[...]
    count = len(late_refs) // 2
    for spot, table in enumerate((BLOCK_TWO, BLOCK_LAST)):
        total = late_refs[spot * count][...].astype(jnp.float32)
        for late_ref in late_refs[spot * count + 1 : (spot + 1) * count]:
            total += late_ref[...].astype(jnp.float32)
        out_ref[step_of(table)(place[1])] = total


def final_scores(place, own, first, late):
    vmem = pl.BlockSpec(memory_space=pltpu.VMEM)
    return pl.pallas_call(
        final_kernel,
        out_shape=jax.ShapeDtypeStruct((STEPS,) + own.shape, jnp.float32),
        in_specs=[pl.BlockSpec(memory_space=pltpu.SMEM)] + [vmem] * (2 + len(late)),
        out_specs=vmem,
    )(place, own, first, *late)


def along_line(documents, conditioned, query_ids, place, shares):
    doc_rows = documents.shape[0]

    def straight(block, table):
        tiles = partial_scores(conditioned, query_ids, [block], [pick(table)], place, shares, turned=True)
        arrived = []
        for turn, tile in enumerate(tiles):
            pairs = [
                (here * shares + lay, there * shares + (lay + turn) % shares)
                for here, there in enumerate(table)
                for lay in range(shares)
            ]
            arrived.append(lax.ppermute(tile, ("rows", "layer"), pairs))
        return arrived

    one = lax.ppermute(documents, "rows", ROUND_ONE)
    later, conditioned = lax.optimization_barrier((documents, conditioned))
    two = lax.ppermute(later, "rows", ROUND_TWO)
    later, one = lax.optimization_barrier((later, one))
    outer = lax.ppermute(one, "rows", ROUND_OUTER)
    inner = lax.ppermute(later, "rows", ROUND_INNER)

    both = [lambda row: row, pick(BLOCK_ONE)]
    tiles = partial_scores(conditioned, query_ids, [documents, one], both, place, shares)
    two, tiles = lax.optimization_barrier((two, tiles))
    own, first = sum_shares(tiles, doc_rows)
    first = lax.ppermute(first, "rows", tuple(enumerate(BLOCK_ONE)))
    second = straight(two, BLOCK_TWO)
    last = straight(outer + inner, BLOCK_LAST)
    return final_scores(place, own, first, second + last)


def around_ring(documents, conditioned, query_ids, place, shares):
    n_rows = lax.axis_size("rows")
    result = []
    for step in range(STEPS):
        back = [(source, (source - step) % n_rows) for source in range(n_rows)]
        block = lax.ppermute(documents, "rows", back) if step else documents
        block_of = [lambda row, step=step: lax.rem(row + step, n_rows)]
        tiles = partial_scores(conditioned, query_ids, [block], block_of, place, shares)
        (total,) = sum_shares(tiles, documents.shape[0])
        onward = [(source, (source + step) % n_rows) for source in range(n_rows)]
        result.append(lax.ppermute(total, "rows", onward) if step else total)
    return jnp.stack(result)


def local(train_grads, query_grads, eigenbases, eigenvalues, layer_offsets, query_doc_ids):
    place = jnp.stack([lax.axis_index("layer"), lax.axis_index("rows")]).astype(jnp.int32)
    slots = layer_offsets // LDIM - place[0] * LAY_DEV
    conditioned = precondition(query_grads, eigenbases, eigenvalues, slots)
    plan = along_line if lax.axis_size("rows") == STEPS else around_ring
    return plan(train_grads, conditioned, query_doc_ids[:, None], place, lax.axis_size("layer"))


def solution(mesh):
    in_specs = (
        P(("group", "rows"), "layer"),
        P(("group", "rows"), "layer"),
        P("layer", None, None),
        P("layer", None),
        P("layer"),
        P(("group", "rows")),
    )
    out_specs = P(None, "layer", ("group", "rows"))
    return jax.shard_map(local, mesh=mesh, in_specs=in_specs, out_specs=out_specs, check_vma=False)
```

```python
import functools

import jax
import jax.numpy as jnp
from jax import lax
from jax.experimental import pallas as pl
from jax.experimental.pallas import tpu as pltpu
from jax.sharding import PartitionSpec as P

LDIM = 512
LAY_DEV = 4
STEPS = 4
DAMPING = 0.05
NT = (((1,), (1,)), ((), ()))
MIB = 1024 * 1024


def prepare_kernel(
    place, offsets, documents_hbm, queries_hbm, bases_hbm, values_hbm, ids_ref,
    conditioned_ref, own_ref, documents, queries, bases, values, arrived,
):
    copies = [
        pltpu.make_async_copy(values_hbm, values, arrived.at[0]),
        pltpu.make_async_copy(documents_hbm, documents, arrived.at[1]),
    ]
    for layer in range(LAY_DEV):
        columns = queries_hbm.at[:, layer * LDIM : (layer + 1) * LDIM]
        copies.append(pltpu.make_async_copy(columns, queries.at[layer], arrived.at[2 + 2 * layer]))
        copies.append(pltpu.make_async_copy(bases_hbm.at[layer], bases.at[layer], arrived.at[3 + 2 * layer]))
    for copy in copies:
        copy.start()
    copies[0].wait()
    for layer in range(LAY_DEV):
        copies[2 + 2 * layer].wait()
        copies[3 + 2 * layer].wait()
        basis = bases[layer]
        projected = jnp.dot(queries[layer], basis, preferred_element_type=jnp.float32)
        scaled = (projected / (values[layer : layer + 1, :] + DAMPING)).astype(jnp.bfloat16)
        restored = lax.dot_general(scaled, basis, NT, preferred_element_type=jnp.float32)
        first = pl.multiple_of(offsets[layer] - place[0] * (LAY_DEV * LDIM), LDIM)
        conditioned_ref[:, pl.ds(first, LDIM)] = restored.astype(jnp.bfloat16)
    copies[1].wait()
    tile = masked_tile(conditioned_ref, documents, ids_ref, place[1])
    shares, share_rows = own_ref.shape[:2]
    for share in range(shares):
        own_ref[share] = tile[share * share_rows : (share + 1) * share_rows].astype(jnp.bfloat16)


def prepare(documents, queries, bases, values, offsets, query_ids, place, shares):
    rows, dims = queries.shape
    docs = documents.shape[0]
    smem = pl.BlockSpec(memory_space=pltpu.SMEM)
    hbm = pl.BlockSpec(memory_space=pltpu.HBM)
    vmem = pl.BlockSpec(memory_space=pltpu.VMEM)
    return pl.pallas_call(
        prepare_kernel,
        out_shape=[
            jax.ShapeDtypeStruct((rows, dims), jnp.bfloat16),
            jax.ShapeDtypeStruct((shares, rows // shares, docs), jnp.bfloat16),
        ],
        in_specs=[smem, smem, hbm, hbm, hbm, hbm, vmem],
        out_specs=[vmem, vmem],
        scratch_shapes=[
            pltpu.VMEM(documents.shape, jnp.bfloat16),
            pltpu.VMEM((LAY_DEV, rows, LDIM), jnp.bfloat16),
            pltpu.VMEM(bases.shape, jnp.bfloat16),
            pltpu.VMEM(values.shape, jnp.float32),
            pltpu.SemaphoreType.DMA((2 + 2 * LAY_DEV,)),
        ],
        compiler_params=pltpu.CompilerParams(vmem_limit_bytes=62 * MIB),
        cost_estimate=pl.CostEstimate(
            flops=2 * rows * dims * (2 * LDIM + docs), bytes_accessed=6 * MIB, transcendentals=0
        ),
    )(place, offsets, documents, queries, bases, values, query_ids)


def masked_tile(queries_ref, documents, ids_ref, block):
    tile = lax.dot_general(queries_ref[...], documents[...], NT, preferred_element_type=jnp.float32)
    doc_ids = block * tile.shape[1] + lax.broadcasted_iota(jnp.int32, tile.shape, 1)
    return jnp.where(ids_ref[...] == doc_ids, 0.0, tile)


def score_kernel(shares, block_of, place, queries_ref, ids_ref, *refs):
    *document_refs, held = refs[: -1 - shares] + refs[-1:]
    out_refs = refs[-1 - shares : -1]
    documents = document_refs[0][...]
    for document_ref in document_refs[1:]:
        documents = documents + document_ref[...]
    held[...] = masked_tile(queries_ref, documents, ids_ref, block_of(place[1]))
    share_rows = out_refs[0].shape[0]
    for turn in range(shares):
        first = pl.multiple_of(lax.rem(place[0] + turn, shares) * share_rows, share_rows)
        out_refs[turn][...] = held[pl.ds(first, share_rows), :].astype(jnp.bfloat16)


def partial_scores(conditioned, query_ids, documents, block_of, place, shares):
    rows, dims = conditioned.shape
    docs = documents[0].shape[0]
    vmem = pl.BlockSpec(memory_space=pltpu.VMEM)
    return pl.pallas_call(
        functools.partial(score_kernel, shares, block_of),
        out_shape=[jax.ShapeDtypeStruct((rows // shares, docs), jnp.bfloat16)] * shares,
        in_specs=[pl.BlockSpec(memory_space=pltpu.SMEM)] + [vmem] * (2 + len(documents)),
        out_specs=[vmem] * shares,
        scratch_shapes=[pltpu.VMEM((rows, docs), jnp.float32)],
        compiler_params=pltpu.CompilerParams(vmem_limit_bytes=12 * MIB),
        cost_estimate=pl.CostEstimate(
            flops=2 * rows * docs * dims, bytes_accessed=2 * dims * (rows + docs), transcendentals=0
        ),
    )(place, conditioned, query_ids, *documents)


ROUND_ONE = ((0, 2), (3, 1), (2, 3), (1, 0))
ROUND_TWO = ((0, 1), (3, 2), (1, 3), (2, 0))
ROUND_INNER = ((1, 2), (2, 1))
ROUND_OUTER = ((2, 3), (1, 0))
BLOCK_ONE = (1, 3, 0, 2)
BLOCK_TWO = (2, 0, 3, 1)
BLOCK_LAST = (3, 2, 1, 0)


def pick(table):
    def entry(row):
        value = jnp.int32(table[0])
        for index in range(1, len(table)):
            value = jnp.where(row == index, jnp.int32(table[index]), value)
        return value

    return entry


def step_of(table):
    return pick([(block - table.index(block)) % STEPS for block in range(STEPS)])


def final_kernel(tables, place, own_ref, *refs):
    *late_refs, out_ref = refs
    shares = own_ref.shape[0]
    total = own_ref[0].astype(jnp.float32)
    for share in range(1, shares):
        total += own_ref[share].astype(jnp.float32)
    out_ref[0] = total
    for spot, step_at in enumerate(tables):
        total = late_refs[spot * shares][...].astype(jnp.float32)
        for late_ref in late_refs[spot * shares + 1 : (spot + 1) * shares]:
            total += late_ref[...].astype(jnp.float32)
        out_ref[step_at(place[1])] = total


def final_scores(place, own, late, tables):
    vmem = pl.BlockSpec(memory_space=pltpu.VMEM)
    return pl.pallas_call(
        functools.partial(final_kernel, tables),
        out_shape=jax.ShapeDtypeStruct((STEPS,) + own.shape[1:], jnp.float32),
        in_specs=[pl.BlockSpec(memory_space=pltpu.SMEM)] + [vmem] * (1 + len(late)),
        out_specs=vmem,
        compiler_params=pltpu.CompilerParams(vmem_limit_bytes=4 * MIB),
    )(place, own, *late)


def exchange(tiles, target_of):
    n_rows, shares = lax.axis_size("rows"), lax.axis_size("layer")
    arrived = []
    for turn, tile in enumerate(tiles):
        pairs = [
            (row * shares + lay, target_of(row) * shares + (lay + turn) % shares)
            for row in range(n_rows)
            for lay in range(shares)
        ]
        arrived.append(lax.ppermute(tile, ("rows", "layer"), pairs))
    return arrived


def along_line(documents, conditioned, own, query_ids, place, shares):
    def scored(blocks, table):
        return partial_scores(conditioned, query_ids, blocks, pick(table), place, shares)

    one = lax.ppermute(documents, "rows", ROUND_ONE)
    later, conditioned = lax.optimization_barrier((documents, conditioned))
    two = lax.ppermute(later, "rows", ROUND_TWO)
    later, one, own = lax.optimization_barrier((later, one, own))
    outer = lax.ppermute(one, "rows", ROUND_OUTER)
    inner = lax.ppermute(later, "rows", ROUND_INNER)

    first = exchange(scored([one], BLOCK_ONE), BLOCK_ONE.__getitem__)
    second = exchange(scored([two], BLOCK_TWO), BLOCK_TWO.__getitem__)
    last = exchange(scored([outer, inner], BLOCK_LAST), BLOCK_LAST.__getitem__)
    return own, first + second + last, [step_of(table) for table in (BLOCK_ONE, BLOCK_TWO, BLOCK_LAST)]


def around_ring(documents, conditioned, own, query_ids, place, shares):
    n_rows = lax.axis_size("rows")
    late = []
    for step in range(1, STEPS):
        back = [(row, (row - step) % n_rows) for row in range(n_rows)]
        block = lax.ppermute(documents, "rows", back)

        def ahead(row, step=step):
            return lax.rem(row + step, n_rows)

        tiles = partial_scores(conditioned, query_ids, [block], ahead, place, shares)
        late += exchange(tiles, lambda row, step=step: (row + step) % n_rows)
    return own, late, [lambda row, step=step: step for step in range(1, STEPS)]


def local(train_grads, query_grads, eigenbases, eigenvalues, layer_offsets, query_doc_ids):
    shares = lax.axis_size("layer")
    place = jnp.stack([lax.axis_index("layer"), lax.axis_index("rows")]).astype(jnp.int32)
    query_ids = query_doc_ids[:, None]
    conditioned, own = prepare(
        train_grads, query_grads, eigenbases, eigenvalues, layer_offsets, query_ids, place, shares
    )
    own = lax.all_to_all(own, "layer", 0, 0, tiled=True)
    plan = along_line if lax.axis_size("rows") == STEPS else around_ring
    own, late, tables = plan(train_grads, conditioned, own, query_ids, place, shares)
    return final_scores(place, own, late, tables)


def solution(mesh):
    in_specs = (
        P(("group", "rows"), "layer"),
        P(("group", "rows"), "layer"),
        P("layer", None, None),
        P("layer", None),
        P("layer"),
        P(("group", "rows")),
    )
    out_specs = P(None, "layer", ("group", "rows"))
    return jax.shard_map(local, mesh=mesh, in_specs=in_specs, out_specs=out_specs, check_vma=False)
```

```python
import functools

import jax
import jax.numpy as jnp
from jax import lax
from jax.experimental import pallas as pl
from jax.experimental.pallas import tpu as pltpu
from jax.sharding import PartitionSpec as P

LDIM = 512
LAY_DEV = 4
STEPS = 4
DAMPING = 0.05
NT = (((1,), (1,)), ((), ()))
MIB = 1024 * 1024


def prepare_kernel(
    offsets, queries_hbm, bases_hbm, values_hbm, conditioned_ref, queries, bases, values, arrived
):
    copies = [pltpu.make_async_copy(values_hbm, values, arrived.at[0])]
    for layer in range(LAY_DEV):
        columns = queries_hbm.at[:, layer * LDIM : (layer + 1) * LDIM]
        copies.append(pltpu.make_async_copy(columns, queries.at[layer], arrived.at[1 + 2 * layer]))
        copies.append(pltpu.make_async_copy(bases_hbm.at[layer], bases.at[layer], arrived.at[2 + 2 * layer]))
    for copy in copies:
        copy.start()
    base_column = lax.axis_index("layer") * (LAY_DEV * LDIM)
    copies[0].wait()
    for layer in range(LAY_DEV):
        copies[1 + 2 * layer].wait()
        copies[2 + 2 * layer].wait()
        basis = bases[layer]
        projected = jnp.dot(queries[layer], basis, preferred_element_type=jnp.float32)
        scaled = (projected / (values[layer : layer + 1, :] + DAMPING)).astype(jnp.bfloat16)
        restored = lax.dot_general(scaled, basis, NT, preferred_element_type=jnp.float32)
        first = pl.multiple_of(offsets[layer] - base_column, LDIM)
        conditioned_ref[:, pl.ds(first, LDIM)] = restored.astype(jnp.bfloat16)


def prepare(queries, bases, values, offsets):
    rows, dims = queries.shape
    hbm = pl.BlockSpec(memory_space=pltpu.HBM)
    return pl.pallas_call(
        prepare_kernel,
        out_shape=jax.ShapeDtypeStruct((rows, dims), jnp.bfloat16),
        in_specs=[pl.BlockSpec(memory_space=pltpu.SMEM), hbm, hbm, hbm],
        out_specs=pl.BlockSpec(memory_space=pltpu.VMEM),
        scratch_shapes=[
            pltpu.VMEM((LAY_DEV, rows, LDIM), jnp.bfloat16),
            pltpu.VMEM(bases.shape, jnp.bfloat16),
            pltpu.VMEM(values.shape, jnp.float32),
            pltpu.SemaphoreType.DMA((1 + 2 * LAY_DEV,)),
        ],
        compiler_params=pltpu.CompilerParams(vmem_limit_bytes=62 * MIB),
        cost_estimate=pl.CostEstimate(
            flops=4 * rows * dims * LDIM, bytes_accessed=6 * MIB, transcendentals=0
        ),
    )(offsets, queries, bases, values)


def masked_tile(queries_ref, documents, ids_ref, block):
    tile = lax.dot_general(queries_ref[...], documents[...], NT, preferred_element_type=jnp.float32)
    doc_ids = block * tile.shape[1] + lax.broadcasted_iota(jnp.int32, tile.shape, 1)
    return jnp.where(ids_ref[...] == doc_ids, 0.0, tile)


def score_kernel(shares, block_of, place, queries_ref, ids_ref, documents_ref, *refs):
    front_refs, out_refs, held = refs[: -1 - shares], refs[-1 - shares : -1], refs[-1]
    held[...] = masked_tile(queries_ref, documents_ref, ids_ref, block_of(place[1]))
    docs = documents_ref.shape[0]
    for turn, out_ref in enumerate(out_refs):
        share_rows, width = out_ref.shape
        first = pl.multiple_of(lax.rem(place[0] + turn, shares) * share_rows, share_rows)
        if front_refs:
            out_ref[:, : width - docs] = front_refs[turn][...]
        out_ref[:, width - docs :] = held[pl.ds(first, share_rows), :].astype(jnp.bfloat16)


def partial_scores(conditioned, query_ids, documents, block_of, place, shares, front=()):
    rows, dims = conditioned.shape
    docs = documents.shape[0]
    width = docs + (front[0].shape[1] if front else 0)
    vmem = pl.BlockSpec(memory_space=pltpu.VMEM)
    return pl.pallas_call(
        functools.partial(score_kernel, shares, block_of),
        out_shape=[jax.ShapeDtypeStruct((rows // shares, width), jnp.bfloat16)] * shares,
        in_specs=[pl.BlockSpec(memory_space=pltpu.SMEM)] + [vmem] * (3 + len(front)),
        out_specs=[vmem] * shares,
        scratch_shapes=[pltpu.VMEM((rows, docs), jnp.float32)],
        compiler_params=pltpu.CompilerParams(vmem_limit_bytes=12 * MIB),
        cost_estimate=pl.CostEstimate(
            flops=2 * rows * docs * dims, bytes_accessed=2 * dims * (rows + docs), transcendentals=0
        ),
    )(place, conditioned, query_ids, documents, *front)


def total_of(refs):
    total = refs[0][...].astype(jnp.float32)
    for ref in refs[1:]:
        total += ref[...].astype(jnp.float32)
    return total


def sum_kernel(shares, *refs):
    in_refs, out_refs = refs[:shares], refs[shares:]
    total = total_of(in_refs)
    docs = out_refs[0].shape[1]
    for spot, out_ref in enumerate(out_refs):
        out_ref[...] = total[:, spot * docs : (spot + 1) * docs]


def row_exchange(tiles):
    shares = len(tiles)
    arrived = [tiles[0]]
    for turn in range(1, shares):
        pairs = [(lay, (lay + turn) % shares) for lay in range(shares)]
        arrived.append(lax.ppermute(tiles[turn], "layer", pairs))
    return arrived


def row_sums(tiles, docs):
    shares = len(tiles)
    rows, width = tiles[0].shape
    vmem = pl.BlockSpec(memory_space=pltpu.VMEM)
    return pl.pallas_call(
        functools.partial(sum_kernel, shares),
        out_shape=[jax.ShapeDtypeStruct((rows, docs), jnp.float32)] * (width // docs),
        in_specs=[vmem] * shares,
        out_specs=[vmem] * (width // docs),
        compiler_params=pltpu.CompilerParams(vmem_limit_bytes=4 * MIB),
    )(*tiles)


ROUND_ONE = ((0, 2), (2, 3), (3, 1), (1, 0))
ROUND_TWO = ((0, 1), (1, 3), (3, 2), (2, 0))
BLOCK_ONE = (1, 3, 0, 2)
BLOCK_TWO = (2, 0, 3, 1)
BLOCK_LAST = (3, 2, 1, 0)


def pick(table):
    def entry(row):
        value = jnp.int32(table[0])
        for index in range(1, len(table)):
            value = jnp.where(row == index, jnp.int32(table[index]), value)
        return value

    return entry


def step_of(table):
    return pick([(block - table.index(block)) % STEPS for block in range(STEPS)])


def final_kernel(tables, place, own_ref, *refs):
    *round_refs, out_ref = refs
    out_ref[0] = own_ref[...]
    for spot, step_at in enumerate(tables):
        parts = round_refs[spot:] if spot == len(tables) - 1 else round_refs[spot : spot + 1]
        out_ref[step_at(place[1])] = total_of(parts)


def final_scores(place, own, rounds, last, tables):
    vmem = pl.BlockSpec(memory_space=pltpu.VMEM)
    return pl.pallas_call(
        functools.partial(final_kernel, tables),
        out_shape=jax.ShapeDtypeStruct((STEPS,) + own.shape, jnp.float32),
        in_specs=[pl.BlockSpec(memory_space=pltpu.SMEM)] + [vmem] * (1 + len(rounds) + len(last)),
        out_specs=vmem,
        compiler_params=pltpu.CompilerParams(vmem_limit_bytes=4 * MIB),
    )(place, own, *rounds, *last)


def exchange(tiles, target_of):
    n_rows, shares = lax.axis_size("rows"), lax.axis_size("layer")
    arrived = []
    for turn, tile in enumerate(tiles):
        pairs = [
            (row * shares + lay, target_of(row) * shares + (lay + turn) % shares)
            for row in range(n_rows)
            for lay in range(shares)
        ]
        arrived.append(lax.ppermute(tile, ("rows", "layer"), pairs))
    return arrived


def along_line(documents, conditioned, query_ids, place, shares):
    docs = documents.shape[0]

    def scored(block, block_of, front=()):
        return partial_scores(conditioned, query_ids, block, block_of, place, shares, front)

    one = lax.ppermute(documents, "rows", ROUND_ONE)
    later, conditioned = lax.optimization_barrier((documents, conditioned))
    two = lax.ppermute(later, "rows", ROUND_TWO)
    tiles = scored(later, lambda row: row)
    one, tiles = lax.optimization_barrier((one, tiles))
    three = lax.ppermute(one, "rows", ROUND_ONE)

    tiles = row_exchange(scored(one, pick(BLOCK_ONE), tiles))
    two, tiles[1] = lax.optimization_barrier((two, tiles[1]))
    own, first = row_sums(tiles, docs)
    first = lax.ppermute(first, "rows", tuple(enumerate(BLOCK_ONE)))
    (second,) = row_sums(row_exchange(scored(two, pick(BLOCK_TWO))), docs)
    second = lax.ppermute(second, "rows", tuple(enumerate(BLOCK_TWO)))
    last = exchange(scored(three, pick(BLOCK_LAST)), BLOCK_LAST.__getitem__)
    tables = [step_of(table) for table in (BLOCK_ONE, BLOCK_TWO, BLOCK_LAST)]
    return final_scores(place, own, [first, second], last, tables)


def around_ring(documents, conditioned, query_ids, place, shares):
    n_rows = lax.axis_size("rows")
    docs = documents.shape[0]
    result = []
    for step in range(STEPS):
        back = [(row, (row - step) % n_rows) for row in range(n_rows)]
        block = lax.ppermute(documents, "rows", back) if step else documents

        def ahead(row, step=step):
            return lax.rem(row + step, n_rows)

        tiles = partial_scores(conditioned, query_ids, block, ahead, place, shares)
        (total,) = row_sums(row_exchange(tiles), docs)
        onward = [(row, (row + step) % n_rows) for row in range(n_rows)]
        result.append(lax.ppermute(total, "rows", onward) if step else total)
    return jnp.stack(result)


def local(train_grads, query_grads, eigenbases, eigenvalues, layer_offsets, query_doc_ids):
    place = jnp.stack([lax.axis_index("layer"), lax.axis_index("rows")]).astype(jnp.int32)
    conditioned = prepare(query_grads, eigenbases, eigenvalues, layer_offsets)
    plan = along_line if lax.axis_size("rows") == STEPS else around_ring
    return plan(train_grads, conditioned, query_doc_ids[:, None], place, lax.axis_size("layer"))


def solution(mesh):
    in_specs = (
        P(("group", "rows"), "layer"),
        P(("group", "rows"), "layer"),
        P("layer", None, None),
        P("layer", None),
        P("layer"),
        P(("group", "rows")),
    )
    out_specs = P(None, "layer", ("group", "rows"))
    return jax.shard_map(local, mesh=mesh, in_specs=in_specs, out_specs=out_specs, check_vma=False)
```

```python
import functools

import jax
import jax.numpy as jnp
from jax import lax
from jax.experimental import pallas as pl
from jax.experimental.pallas import tpu as pltpu
from jax.sharding import PartitionSpec as P

LDIM = 512
LAY_DEV = 4
STEPS = 4
DAMPING = 0.05
NT = (((1,), (1,)), ((), ()))
MIB = 1024 * 1024


def prepare_kernel(
    offsets, queries_hbm, bases_hbm, values_hbm, conditioned_ref, queries, bases, values, arrived
):
    copies = [pltpu.make_async_copy(values_hbm, values, arrived.at[0])]
    for layer in range(LAY_DEV):
        columns = queries_hbm.at[:, layer * LDIM : (layer + 1) * LDIM]
        copies.append(pltpu.make_async_copy(columns, queries.at[layer], arrived.at[1 + 2 * layer]))
        copies.append(pltpu.make_async_copy(bases_hbm.at[layer], bases.at[layer], arrived.at[2 + 2 * layer]))
    for copy in copies:
        copy.start()
    base_column = lax.axis_index("layer") * (LAY_DEV * LDIM)
    copies[0].wait()
    for layer in range(LAY_DEV):
        copies[1 + 2 * layer].wait()
        copies[2 + 2 * layer].wait()
        basis = bases[layer]
        projected = jnp.dot(queries[layer], basis, preferred_element_type=jnp.float32)
        scaled = (projected / (values[layer : layer + 1, :] + DAMPING)).astype(jnp.bfloat16)
        restored = lax.dot_general(scaled, basis, NT, preferred_element_type=jnp.float32)
        first = pl.multiple_of(offsets[layer] - base_column, LDIM)
        conditioned_ref[:, pl.ds(first, LDIM)] = restored.astype(jnp.bfloat16)


def prepare(queries, bases, values, offsets):
    rows, dims = queries.shape
    hbm = pl.BlockSpec(memory_space=pltpu.HBM)
    return pl.pallas_call(
        prepare_kernel,
        out_shape=jax.ShapeDtypeStruct((rows, dims), jnp.bfloat16),
        in_specs=[pl.BlockSpec(memory_space=pltpu.SMEM), hbm, hbm, hbm],
        out_specs=pl.BlockSpec(memory_space=pltpu.VMEM),
        scratch_shapes=[
            pltpu.VMEM((LAY_DEV, rows, LDIM), jnp.bfloat16),
            pltpu.VMEM(bases.shape, jnp.bfloat16),
            pltpu.VMEM(values.shape, jnp.float32),
            pltpu.SemaphoreType.DMA((1 + 2 * LAY_DEV,)),
        ],
        compiler_params=pltpu.CompilerParams(vmem_limit_bytes=62 * MIB),
        cost_estimate=pl.CostEstimate(
            flops=4 * rows * dims * LDIM, bytes_accessed=6 * MIB, transcendentals=0
        ),
    )(offsets, queries, bases, values)


def masked_tile(queries_ref, documents, ids_ref, block):
    tile = lax.dot_general(queries_ref[...], documents[...], NT, preferred_element_type=jnp.float32)
    doc_ids = block * tile.shape[1] + lax.broadcasted_iota(jnp.int32, tile.shape, 1)
    return jnp.where(ids_ref[...] == doc_ids, 0.0, tile)


def score_kernel(shares, block_of, place, queries_ref, ids_ref, documents_ref, *refs):
    *out_refs, held = refs
    held[...] = masked_tile(queries_ref, documents_ref, ids_ref, block_of(place[1]))
    for turn, out_ref in enumerate(out_refs):
        share_rows = out_ref.shape[0]
        first = pl.multiple_of(lax.rem(place[0] + turn, shares) * share_rows, share_rows)
        out_ref[...] = held[pl.ds(first, share_rows), :].astype(jnp.bfloat16)


def own_kernel(shares, place, queries_ref, ids_ref, documents_ref, out_ref):
    tile = masked_tile(queries_ref, documents_ref, ids_ref, place[1])
    out_ref[...] = tile.astype(jnp.bfloat16).reshape(out_ref.shape)


def pair_kernel(shares, place, queries_ref, ids_ref, documents_ref, own_ref, out_ref):
    tile = masked_tile(queries_ref, documents_ref, ids_ref, STEPS - 1 - place[1])
    spot = own_spot(place[1])
    out_ref[spot] = own_ref[...]
    out_ref[1 - spot] = tile.astype(jnp.bfloat16).reshape(own_ref.shape)


def own_spot(row):
    return jnp.where(row < STEPS - 1 - row, 0, 1)


def partial_scores(kernel, out_shape, conditioned, query_ids, documents, place, extra=(), scratch=()):
    rows, dims = conditioned.shape
    docs = documents.shape[0]
    vmem = pl.BlockSpec(memory_space=pltpu.VMEM)
    return pl.pallas_call(
        kernel,
        out_shape=out_shape,
        in_specs=[pl.BlockSpec(memory_space=pltpu.SMEM)] + [vmem] * (3 + len(extra)),
        out_specs=jax.tree.map(lambda _: vmem, out_shape),
        scratch_shapes=scratch,
        compiler_params=pltpu.CompilerParams(vmem_limit_bytes=12 * MIB),
        cost_estimate=pl.CostEstimate(
            flops=2 * rows * docs * dims, bytes_accessed=2 * dims * (rows + docs), transcendentals=0
        ),
    )(place, conditioned, query_ids, documents, *extra)


def turned_scores(conditioned, query_ids, documents, block_of, place, shares):
    rows, docs = conditioned.shape[0], documents.shape[0]
    out_shape = [jax.ShapeDtypeStruct((rows // shares, docs), jnp.bfloat16)] * shares
    kernel = functools.partial(score_kernel, shares, block_of)
    scratch = [pltpu.VMEM((rows, docs), jnp.float32)]
    return partial_scores(kernel, out_shape, conditioned, query_ids, documents, place, (), scratch)


def total_of(refs):
    total = refs[0][...].astype(jnp.float32)
    for ref in refs[1:]:
        total += ref[...].astype(jnp.float32)
    return total


def sum_kernel(*refs):
    refs[-1][...] = total_of(refs[:-1])


def row_exchange(tiles):
    shares = len(tiles)
    arrived = [tiles[0]]
    for turn in range(1, shares):
        pairs = [(lay, (lay + turn) % shares) for lay in range(shares)]
        arrived.append(lax.ppermute(tiles[turn], "layer", pairs))
    return arrived


def row_sum(tiles):
    vmem = pl.BlockSpec(memory_space=pltpu.VMEM)
    return pl.pallas_call(
        sum_kernel,
        out_shape=jax.ShapeDtypeStruct(tiles[0].shape, jnp.float32),
        in_specs=[vmem] * len(tiles),
        out_specs=vmem,
        compiler_params=pltpu.CompilerParams(vmem_limit_bytes=4 * MIB),
    )(*tiles)


ROUND_ONE = ((0, 2), (2, 3), (3, 1), (1, 0))
ROUND_TWO = ((0, 1), (1, 3), (3, 2), (2, 0))
BLOCK_ONE = (1, 3, 0, 2)
BLOCK_TWO = (2, 0, 3, 1)
BLOCK_LAST = (3, 2, 1, 0)


def pick(table):
    def entry(row):
        value = jnp.int32(table[0])
        for index in range(1, len(table)):
            value = jnp.where(row == index, jnp.int32(table[index]), value)
        return value

    return entry


def step_of(table):
    return pick([(block - table.index(block)) % STEPS for block in range(STEPS)])


def final_kernel(place, first_ref, second_ref, pair_ref, out_ref):
    row = place[1]
    spot = own_spot(row)
    shares = pair_ref.shape[1]
    out_ref[0] = total_of([pair_ref.at[spot, share] for share in range(shares)])
    out_ref[step_of(BLOCK_ONE)(row)] = first_ref[...]
    out_ref[step_of(BLOCK_TWO)(row)] = second_ref[...]
    out_ref[step_of(BLOCK_LAST)(row)] = total_of([pair_ref.at[1 - spot, share] for share in range(shares)])


def final_scores(place, first, second, pair):
    vmem = pl.BlockSpec(memory_space=pltpu.VMEM)
    return pl.pallas_call(
        final_kernel,
        out_shape=jax.ShapeDtypeStruct((STEPS,) + first.shape, jnp.float32),
        in_specs=[pl.BlockSpec(memory_space=pltpu.SMEM)] + [vmem] * 3,
        out_specs=vmem,
        compiler_params=pltpu.CompilerParams(vmem_limit_bytes=4 * MIB),
    )(place, first, second, pair)


def along_line(documents, conditioned, query_ids, place, shares):
    docs = documents.shape[0]
    own_shape = (shares, conditioned.shape[0] // shares, docs)

    def row_scores(block, table):
        tiles = turned_scores(conditioned, query_ids, block, pick(table), place, shares)
        return row_exchange(tiles)

    def back(total, table):
        return lax.ppermute(total, "rows", tuple(enumerate(table)))

    one = lax.ppermute(documents, "rows", ROUND_ONE)
    later, conditioned = lax.optimization_barrier((documents, conditioned))
    two = lax.ppermute(later, "rows", ROUND_TWO)
    own = partial_scores(
        functools.partial(own_kernel, shares),
        jax.ShapeDtypeStruct(own_shape, jnp.bfloat16),
        conditioned, query_ids, later, place,
    )
    one, own = lax.optimization_barrier((one, own))
    three = lax.ppermute(one, "rows", ROUND_ONE)

    tiles = row_scores(one, BLOCK_ONE)
    two, tiles[1] = lax.optimization_barrier((two, tiles[1]))
    first = back(row_sum(tiles), BLOCK_ONE)
    second = back(row_sum(row_scores(two, BLOCK_TWO)), BLOCK_TWO)

    pair = partial_scores(
        functools.partial(pair_kernel, shares),
        jax.ShapeDtypeStruct((2,) + own_shape, jnp.bfloat16),
        conditioned, query_ids, three, place, (own,),
    )
    groups = [
        [row * shares + lay for row in (low, STEPS - 1 - low) for lay in range(shares)]
        for low in range(STEPS // 2)
    ]
    blocks = pair.reshape((2 * shares,) + own_shape[1:])
    blocks = lax.all_to_all(blocks, ("rows", "layer"), 0, 0, axis_index_groups=groups, tiled=True)
    return final_scores(place, first, second, blocks.reshape(pair.shape))


def around_ring(documents, conditioned, query_ids, place, shares):
    n_rows = lax.axis_size("rows")
    result = []
    for step in range(STEPS):
        behind = [(row, (row - step) % n_rows) for row in range(n_rows)]
        block = lax.ppermute(documents, "rows", behind) if step else documents

        def ahead(row, step=step):
            return lax.rem(row + step, n_rows)

        tiles = turned_scores(conditioned, query_ids, block, ahead, place, shares)
        total = row_sum(row_exchange(tiles))
        onward = [(row, (row + step) % n_rows) for row in range(n_rows)]
        result.append(lax.ppermute(total, "rows", onward) if step else total)
    return jnp.stack(result)


def local(train_grads, query_grads, eigenbases, eigenvalues, layer_offsets, query_doc_ids):
    place = jnp.stack([lax.axis_index("layer"), lax.axis_index("rows")]).astype(jnp.int32)
    conditioned = prepare(query_grads, eigenbases, eigenvalues, layer_offsets)
    plan = along_line if lax.axis_size("rows") == STEPS else around_ring
    return plan(train_grads, conditioned, query_doc_ids[:, None], place, lax.axis_size("layer"))


def solution(mesh):
    in_specs = (
        P(("group", "rows"), "layer"),
        P(("group", "rows"), "layer"),
        P("layer", None, None),
        P("layer", None),
        P("layer"),
        P(("group", "rows")),
    )
    out_specs = P(None, "layer", ("group", "rows"))
    return jax.shard_map(local, mesh=mesh, in_specs=in_specs, out_specs=out_specs, check_vma=False)
```

```python
import functools

import jax
import jax.numpy as jnp
from jax import lax
from jax.experimental import pallas as pl
from jax.experimental.pallas import tpu as pltpu
from jax.sharding import PartitionSpec as P

LDIM = 512
LAY_DEV = 4
STEPS = 4
DAMPING = 0.05
NT = (((1,), (1,)), ((), ()))
MIB = 1024 * 1024


def prepare_kernel(
    offsets, queries_hbm, bases_hbm, values_hbm, conditioned_ref, queries, bases, values, arrived
):
    copies = [pltpu.make_async_copy(values_hbm, values, arrived.at[0])]
    for layer in range(LAY_DEV):
        columns = queries_hbm.at[:, layer * LDIM : (layer + 1) * LDIM]
        copies.append(pltpu.make_async_copy(columns, queries.at[layer], arrived.at[1 + 2 * layer]))
        copies.append(pltpu.make_async_copy(bases_hbm.at[layer], bases.at[layer], arrived.at[2 + 2 * layer]))
    for copy in copies:
        copy.start()
    base_column = lax.axis_index("layer") * (LAY_DEV * LDIM)
    copies[0].wait()
    for layer in range(LAY_DEV):
        copies[1 + 2 * layer].wait()
        copies[2 + 2 * layer].wait()
        basis = bases[layer]
        projected = jnp.dot(queries[layer], basis, preferred_element_type=jnp.float32)
        scaled = (projected / (values[layer : layer + 1, :] + DAMPING)).astype(jnp.bfloat16)
        restored = lax.dot_general(scaled, basis, NT, preferred_element_type=jnp.float32)
        first = pl.multiple_of(offsets[layer] - base_column, LDIM)
        conditioned_ref[:, pl.ds(first, LDIM)] = restored.astype(jnp.bfloat16)


def prepare(queries, bases, values, offsets):
    rows, dims = queries.shape
    hbm = pl.BlockSpec(memory_space=pltpu.HBM)
    return pl.pallas_call(
        prepare_kernel,
        out_shape=jax.ShapeDtypeStruct((rows, dims), jnp.bfloat16),
        in_specs=[pl.BlockSpec(memory_space=pltpu.SMEM), hbm, hbm, hbm],
        out_specs=pl.BlockSpec(memory_space=pltpu.VMEM),
        scratch_shapes=[
            pltpu.VMEM((LAY_DEV, rows, LDIM), jnp.bfloat16),
            pltpu.VMEM(bases.shape, jnp.bfloat16),
            pltpu.VMEM(values.shape, jnp.float32),
            pltpu.SemaphoreType.DMA((1 + 2 * LAY_DEV,)),
        ],
        compiler_params=pltpu.CompilerParams(vmem_limit_bytes=62 * MIB),
        cost_estimate=pl.CostEstimate(
            flops=4 * rows * dims * LDIM, bytes_accessed=6 * MIB, transcendentals=0
        ),
    )(offsets, queries, bases, values)


def masked_tile(queries_ref, documents, ids_ref, block):
    tile = lax.dot_general(queries_ref[...], documents[...], NT, preferred_element_type=jnp.float32)
    doc_ids = block * tile.shape[1] + lax.broadcasted_iota(jnp.int32, tile.shape, 1)
    return jnp.where(ids_ref[...] == doc_ids, 0.0, tile)


def score_kernel(shares, block_of, place, queries_ref, ids_ref, documents_ref, *refs):
    front_refs, out_refs, held = refs[: -1 - shares], refs[-1 - shares : -1], refs[-1]
    held[...] = masked_tile(queries_ref, documents_ref, ids_ref, block_of(place[1]))
    docs = documents_ref.shape[0]
    for turn, out_ref in enumerate(out_refs):
        share_rows, width = out_ref.shape
        first = pl.multiple_of(lax.rem(place[0] + turn, shares) * share_rows, share_rows)
        if front_refs:
            out_ref[:, : width - docs] = front_refs[turn][...]
        out_ref[:, width - docs :] = held[pl.ds(first, share_rows), :].astype(jnp.bfloat16)


def partial_scores(conditioned, query_ids, documents, block_of, place, shares, front=()):
    rows, dims = conditioned.shape
    docs = documents.shape[0]
    width = docs + (front[0].shape[1] if front else 0)
    vmem = pl.BlockSpec(memory_space=pltpu.VMEM)
    return pl.pallas_call(
        functools.partial(score_kernel, shares, block_of),
        out_shape=[jax.ShapeDtypeStruct((rows // shares, width), jnp.bfloat16)] * shares,
        in_specs=[pl.BlockSpec(memory_space=pltpu.SMEM)] + [vmem] * (3 + len(front)),
        out_specs=[vmem] * shares,
        scratch_shapes=[pltpu.VMEM((rows, docs), jnp.float32)],
        compiler_params=pltpu.CompilerParams(vmem_limit_bytes=12 * MIB),
        cost_estimate=pl.CostEstimate(
            flops=2 * rows * docs * dims, bytes_accessed=2 * dims * (rows + docs), transcendentals=0
        ),
    )(place, conditioned, query_ids, documents, *front)


def total_of(refs):
    total = refs[0][...].astype(jnp.float32)
    for ref in refs[1:]:
        total += ref[...].astype(jnp.float32)
    return total


def sum_kernel(shares, *refs):
    in_refs, out_refs = refs[:shares], refs[shares:]
    total = total_of(in_refs)
    docs = out_refs[0].shape[1]
    for spot, out_ref in enumerate(out_refs):
        out_ref[...] = total[:, spot * docs : (spot + 1) * docs]


def row_exchange(tiles):
    shares = len(tiles)
    arrived = [tiles[0]]
    for turn in range(1, shares):
        pairs = [(lay, (lay + turn) % shares) for lay in range(shares)]
        arrived.append(lax.ppermute(tiles[turn], "layer", pairs))
    return arrived


def row_sums(tiles, docs):
    shares = len(tiles)
    rows, width = tiles[0].shape
    vmem = pl.BlockSpec(memory_space=pltpu.VMEM)
    return pl.pallas_call(
        functools.partial(sum_kernel, shares),
        out_shape=[jax.ShapeDtypeStruct((rows, docs), jnp.float32)] * (width // docs),
        in_specs=[vmem] * shares,
        out_specs=[vmem] * (width // docs),
        compiler_params=pltpu.CompilerParams(vmem_limit_bytes=4 * MIB),
    )(*tiles)


ROUND_ONE = ((0, 2), (2, 3), (3, 1), (1, 0))
ROUND_TWO = ((0, 1), (1, 3), (3, 2), (2, 0))
BLOCK_ONE = (1, 3, 0, 2)
BLOCK_TWO = (2, 0, 3, 1)
BLOCK_LAST = (3, 2, 1, 0)


def pick(table):
    def entry(row):
        value = jnp.int32(table[0])
        for index in range(1, len(table)):
            value = jnp.where(row == index, jnp.int32(table[index]), value)
        return value

    return entry


def step_of(table):
    return pick([(block - table.index(block)) % STEPS for block in range(STEPS)])


def final_kernel(place, own_ref, *refs):
    *round_refs, out_ref = refs
    out_ref[0] = own_ref[...]
    for round_ref, table in zip(round_refs, (BLOCK_ONE, BLOCK_TWO, BLOCK_LAST)):
        out_ref[step_of(table)(place[1])] = round_ref[...]


def final_scores(place, own, rounds):
    vmem = pl.BlockSpec(memory_space=pltpu.VMEM)
    return pl.pallas_call(
        final_kernel,
        out_shape=jax.ShapeDtypeStruct((STEPS,) + own.shape, jnp.float32),
        in_specs=[pl.BlockSpec(memory_space=pltpu.SMEM)] + [vmem] * (1 + len(rounds)),
        out_specs=vmem,
        compiler_params=pltpu.CompilerParams(vmem_limit_bytes=4 * MIB),
    )(place, own, *rounds)


def along_line(documents, conditioned, query_ids, place, shares):
    docs = documents.shape[0]

    def scored(block, block_of, front=()):
        return partial_scores(conditioned, query_ids, block, block_of, place, shares, front)

    def back(total, table):
        return lax.ppermute(total, "rows", tuple(enumerate(table)))

    one = lax.ppermute(documents, "rows", ROUND_ONE)
    later, conditioned = lax.optimization_barrier((documents, conditioned))
    two = lax.ppermute(later, "rows", ROUND_TWO)
    tiles = scored(later, lambda row: row)
    one, tiles = lax.optimization_barrier((one, tiles))
    three = lax.ppermute(one, "rows", ROUND_ONE)

    tiles = row_exchange(scored(one, pick(BLOCK_ONE), tiles))
    two, tiles[1] = lax.optimization_barrier((two, tiles[1]))
    own, first = row_sums(tiles, docs)
    first = back(first, BLOCK_ONE)
    (second,) = row_sums(row_exchange(scored(two, pick(BLOCK_TWO))), docs)
    second = back(second, BLOCK_TWO)
    three, first, second = lax.optimization_barrier((three, first, second))
    (last,) = row_sums(row_exchange(scored(three, pick(BLOCK_LAST))), docs)
    last = back(last, BLOCK_LAST)
    return final_scores(place, own, [first, second, last])


def around_ring(documents, conditioned, query_ids, place, shares):
    n_rows = lax.axis_size("rows")
    docs = documents.shape[0]
    result = []
    for step in range(STEPS):
        back = [(row, (row - step) % n_rows) for row in range(n_rows)]
        block = lax.ppermute(documents, "rows", back) if step else documents

        def ahead(row, step=step):
            return lax.rem(row + step, n_rows)

        tiles = partial_scores(conditioned, query_ids, block, ahead, place, shares)
        (total,) = row_sums(row_exchange(tiles), docs)
        onward = [(row, (row + step) % n_rows) for row in range(n_rows)]
        result.append(lax.ppermute(total, "rows", onward) if step else total)
    return jnp.stack(result)


def local(train_grads, query_grads, eigenbases, eigenvalues, layer_offsets, query_doc_ids):
    place = jnp.stack([lax.axis_index("layer"), lax.axis_index("rows")]).astype(jnp.int32)
    conditioned = prepare(query_grads, eigenbases, eigenvalues, layer_offsets)
    plan = along_line if lax.axis_size("rows") == STEPS else around_ring
    return plan(train_grads, conditioned, query_doc_ids[:, None], place, lax.axis_size("layer"))


def solution(mesh):
    in_specs = (
        P(("group", "rows"), "layer"),
        P(("group", "rows"), "layer"),
        P("layer", None, None),
        P("layer", None),
        P("layer"),
        P(("group", "rows")),
    )
    out_specs = P(None, "layer", ("group", "rows"))
    return jax.shard_map(local, mesh=mesh, in_specs=in_specs, out_specs=out_specs, check_vma=False)
```

```python
import functools

import jax
import jax.numpy as jnp
from jax import lax
from jax.experimental import pallas as pl
from jax.experimental.pallas import tpu as pltpu
from jax.sharding import PartitionSpec as P

LDIM = 512
LAY_DEV = 4
STEPS = 4
DAMPING = 0.05
NT = (((1,), (1,)), ((), ()))
MIB = 1024 * 1024


def prepare_kernel(
    offsets, queries_hbm, bases_hbm, values_hbm, conditioned_ref, queries, bases, values, arrived
):
    copies = [pltpu.make_async_copy(values_hbm, values, arrived.at[0])]
    for layer in range(LAY_DEV):
        columns = queries_hbm.at[:, layer * LDIM : (layer + 1) * LDIM]
        copies.append(pltpu.make_async_copy(columns, queries.at[layer], arrived.at[1 + 2 * layer]))
        copies.append(pltpu.make_async_copy(bases_hbm.at[layer], bases.at[layer], arrived.at[2 + 2 * layer]))
    for copy in copies:
        copy.start()
    base_column = lax.axis_index("layer") * (LAY_DEV * LDIM)
    copies[0].wait()
    for layer in range(LAY_DEV):
        copies[1 + 2 * layer].wait()
        copies[2 + 2 * layer].wait()
        basis = bases[layer]
        projected = jnp.dot(queries[layer], basis, preferred_element_type=jnp.float32)
        scaled = (projected / (values[layer : layer + 1, :] + DAMPING)).astype(jnp.bfloat16)
        restored = lax.dot_general(scaled, basis, NT, preferred_element_type=jnp.float32)
        first = pl.multiple_of(offsets[layer] - base_column, LDIM)
        conditioned_ref[:, pl.ds(first, LDIM)] = restored.astype(jnp.bfloat16)


def prepare(queries, bases, values, offsets):
    rows, dims = queries.shape
    hbm = pl.BlockSpec(memory_space=pltpu.HBM)
    return pl.pallas_call(
        prepare_kernel,
        out_shape=jax.ShapeDtypeStruct((rows, dims), jnp.bfloat16),
        in_specs=[pl.BlockSpec(memory_space=pltpu.SMEM), hbm, hbm, hbm],
        out_specs=pl.BlockSpec(memory_space=pltpu.VMEM),
        scratch_shapes=[
            pltpu.VMEM((LAY_DEV, rows, LDIM), jnp.bfloat16),
            pltpu.VMEM(bases.shape, jnp.bfloat16),
            pltpu.VMEM(values.shape, jnp.float32),
            pltpu.SemaphoreType.DMA((1 + 2 * LAY_DEV,)),
        ],
        compiler_params=pltpu.CompilerParams(vmem_limit_bytes=62 * MIB),
        cost_estimate=pl.CostEstimate(
            flops=4 * rows * dims * LDIM, bytes_accessed=6 * MIB, transcendentals=0
        ),
    )(offsets, queries, bases, values)


def masked_tile(queries, documents, query_ids, block):
    tile = lax.dot_general(queries, documents, NT, preferred_element_type=jnp.float32)
    doc_ids = block * tile.shape[1] + lax.broadcasted_iota(jnp.int32, tile.shape, 1)
    return jnp.where(query_ids == doc_ids, 0.0, tile)


def scoring(kernel, out_shape, place, conditioned, query_ids, documents, extra=(), scratch=()):
    dims = conditioned.shape[1]
    docs = documents.shape[0]
    rows = sum(shape.shape[0] for shape in out_shape)
    vmem = pl.BlockSpec(memory_space=pltpu.VMEM)
    return pl.pallas_call(
        kernel,
        out_shape=out_shape,
        in_specs=[pl.BlockSpec(memory_space=pltpu.SMEM)] + [vmem] * (3 + len(extra)),
        out_specs=[vmem] * len(out_shape),
        scratch_shapes=scratch,
        compiler_params=pltpu.CompilerParams(vmem_limit_bytes=12 * MIB),
        cost_estimate=pl.CostEstimate(
            flops=2 * rows * docs * dims, bytes_accessed=2 * dims * (rows + docs), transcendentals=0
        ),
    )(place, conditioned, query_ids, documents, *extra)


def turned_kernel(shares, block_of, place, queries_ref, ids_ref, documents_ref, *refs):
    *out_refs, held = refs
    held[...] = masked_tile(queries_ref[...], documents_ref[...], ids_ref[...], block_of(place[1]))
    for turn, out_ref in enumerate(out_refs):
        share_rows = out_ref.shape[0]
        first = pl.multiple_of(lax.rem(place[0] + turn, shares) * share_rows, share_rows)
        out_ref[...] = held[pl.ds(first, share_rows), :].astype(jnp.bfloat16)


def half_shares(layer, share_rows, kept):
    core = lax.rem(layer, 2)
    core = core if kept else 1 - core
    return [pl.multiple_of((2 * chip + core) * share_rows, share_rows) for chip in range(2)]


def halves_kernel(block_of, place, queries_ref, ids_ref, documents_ref, *refs):
    front_refs, out_refs, held = refs[:-3], refs[-3:-1], refs[-1]
    held[...] = masked_tile(queries_ref[...], documents_ref[...], ids_ref[...], block_of(place[1]))
    docs = documents_ref.shape[0]
    rows, width = out_refs[0].shape
    for side, kept in enumerate((True, False)):
        if front_refs:
            out_refs[side][:, : width - docs] = front_refs[side][...]
        for chip, first in enumerate(half_shares(place[0], rows // 2, kept)):
            spot = slice(chip * (rows // 2), (chip + 1) * (rows // 2))
            out_refs[side][spot, width - docs :] = held[pl.ds(first, rows // 2), :]


def half_kernel(block_of, kept, place, queries_ref, ids_ref, documents_ref, out_ref):
    share_rows = out_ref.shape[0] // 2
    firsts = half_shares(place[0], share_rows, kept)
    queries = jnp.concatenate([queries_ref[pl.ds(first, share_rows), :] for first in firsts], axis=0)
    query_ids = jnp.concatenate([ids_ref[pl.ds(first, share_rows), :] for first in firsts], axis=0)
    out_ref[...] = masked_tile(queries, documents_ref[...], query_ids, block_of(place[1]))


def total_of(refs):
    total = refs[0][...].astype(jnp.float32)
    for ref in refs[1:]:
        total += ref[...].astype(jnp.float32)
    return total


def sum_kernel(*refs):
    refs[-1][...] = total_of(refs[:-1])


def small_call(kernel, out_shape, *args, place=None):
    vmem = pl.BlockSpec(memory_space=pltpu.VMEM)
    scalars = [] if place is None else [place]
    return pl.pallas_call(
        kernel,
        out_shape=out_shape,
        in_specs=[pl.BlockSpec(memory_space=pltpu.SMEM)] * len(scalars) + [vmem] * len(args),
        out_specs=[vmem] * len(out_shape),
        compiler_params=pltpu.CompilerParams(vmem_limit_bytes=4 * MIB),
    )(*scalars, *args)


def direct_sum(tiles):
    shares = len(tiles)
    arrived = [tiles[0]]
    for turn in range(1, shares):
        pairs = [(lay, (lay + turn) % shares) for lay in range(shares)]
        arrived.append(lax.ppermute(tiles[turn], "layer", pairs))
    (total,) = small_call(sum_kernel, [jax.ShapeDtypeStruct(tiles[0].shape, jnp.float32)], *arrived)
    return total


def core_sum_kernel(place, kept_ref, arrived_ref, mine_ref, other_ref):
    rows = mine_ref.shape[0]
    chip = place[0] // 2
    mine = pl.ds(pl.multiple_of(chip * rows, rows), rows)
    other = pl.ds(pl.multiple_of((1 - chip) * rows, rows), rows)
    mine_ref[...] = kept_ref[mine, :] + arrived_ref[mine, :]
    other_ref[...] = (kept_ref[other, :] + arrived_ref[other, :]).astype(other_ref.dtype)


def chip_sum_kernel(mine_ref, arrived_ref, *out_refs):
    docs = out_refs[0].shape[1]
    for spot, out_ref in enumerate(out_refs):
        columns = slice(spot * docs, (spot + 1) * docs)
        total = mine_ref[:, columns] + arrived_ref[:, columns].astype(jnp.float32)
        out_ref[...] = total.astype(out_ref.dtype)


def swap(value, distance):
    count = lax.axis_size("layer")
    return lax.ppermute(value, "layer", [(lay, lay ^ distance) for lay in range(count)])


def layer_sum(kept, sent, place, out_types):
    rows, width = kept.shape[0] // 2, kept.shape[1]
    mine, other = small_call(
        core_sum_kernel,
        [jax.ShapeDtypeStruct((rows, width), jnp.float32), jax.ShapeDtypeStruct((rows, width), jnp.bfloat16)],
        kept, swap(sent, 1), place=place,
    )
    docs = width // len(out_types)
    out_shape = [jax.ShapeDtypeStruct((rows, docs), out_type) for out_type in out_types]
    return small_call(chip_sum_kernel, out_shape, mine, swap(other, 2))


ROUND_ONE = ((0, 2), (2, 3), (3, 1), (1, 0))
ROUND_TWO = ((0, 1), (1, 3), (3, 2), (2, 0))
BLOCK_ONE = (1, 3, 0, 2)
BLOCK_TWO = (2, 0, 3, 1)
BLOCK_LAST = (3, 2, 1, 0)


def pick(table):
    def entry(row):
        value = jnp.int32(table[0])
        for index in range(1, len(table)):
            value = jnp.where(row == index, jnp.int32(table[index]), value)
        return value

    return entry


def step_of(table):
    return pick([(block - table.index(block)) % STEPS for block in range(STEPS)])


def assemble_kernel(place, own_ref, first_ref, second_ref, out_ref):
    out_ref[0] = own_ref[...]
    for ref, table in ((first_ref, BLOCK_ONE), (second_ref, BLOCK_TWO)):
        out_ref[step_of(table)(place[1])] = ref[...].astype(jnp.float32)


def finish_kernel(place, last_ref, scores_hbm, out_hbm, wide, copied):
    del scores_hbm
    wide[...] = last_ref[...].astype(jnp.float32)
    copy = pltpu.make_async_copy(wide, out_hbm.at[step_of(BLOCK_LAST)(place[1])], copied)
    copy.start()
    copy.wait()


def finish(place, last, scores):
    hbm = pl.BlockSpec(memory_space=pltpu.HBM)
    return pl.pallas_call(
        finish_kernel,
        out_shape=jax.ShapeDtypeStruct(scores.shape, scores.dtype),
        in_specs=[pl.BlockSpec(memory_space=pltpu.SMEM), pl.BlockSpec(memory_space=pltpu.VMEM), hbm],
        out_specs=hbm,
        scratch_shapes=[pltpu.VMEM(last.shape, jnp.float32), pltpu.SemaphoreType.DMA],
        input_output_aliases={2: 0},
        compiler_params=pltpu.CompilerParams(vmem_limit_bytes=4 * MIB),
    )(place, last, scores)


def along_line(documents, conditioned, query_ids, place):
    docs = documents.shape[0]
    half = (conditioned.shape[0] // 2, docs)

    def halves(block, block_of, front=()):
        width = docs * (1 + bool(front))
        out_shape = [jax.ShapeDtypeStruct((half[0], width), jnp.float32)] * 2
        scratch = [pltpu.VMEM((2 * half[0], docs), jnp.float32)]
        kernel = functools.partial(halves_kernel, block_of)
        return scoring(kernel, out_shape, place, conditioned, query_ids, block, front, scratch)

    def one_half(block, block_of, kept):
        kernel = functools.partial(half_kernel, block_of, kept)
        out_shape = [jax.ShapeDtypeStruct(half, jnp.float32)]
        return scoring(kernel, out_shape, place, conditioned, query_ids, block)[0]

    def back(total, table):
        return lax.ppermute(total, "rows", tuple(enumerate(table)))

    one = lax.ppermute(documents, "rows", ROUND_ONE)
    later, conditioned = lax.optimization_barrier((documents, conditioned))
    two = lax.ppermute(later, "rows", ROUND_TWO)
    own = halves(later, lambda row: row)
    one, own = lax.optimization_barrier((one, own))
    three = lax.ppermute(one, "rows", ROUND_ONE)

    own, first = layer_sum(*halves(one, pick(BLOCK_ONE), own), place, (jnp.float32, jnp.bfloat16))
    two, first = lax.optimization_barrier((two, first))
    first = back(first, BLOCK_ONE)
    (second,) = layer_sum(*halves(two, pick(BLOCK_TWO)), place, (jnp.bfloat16,))
    second = back(second, BLOCK_TWO)
    three, first, second = lax.optimization_barrier((three, first, second))

    sent = one_half(three, pick(BLOCK_LAST), False)
    kept = one_half(three, pick(BLOCK_LAST), True)
    (last,) = layer_sum(kept, sent, place, (jnp.bfloat16,))
    last = back(last, BLOCK_LAST)
    out_shape = [jax.ShapeDtypeStruct((STEPS,) + own.shape, jnp.float32)]
    (scores,) = small_call(assemble_kernel, out_shape, own, first, second, place=place)
    return finish(place, last, scores)


def around_ring(documents, conditioned, query_ids, place):
    n_rows, shares = lax.axis_size("rows"), lax.axis_size("layer")
    rows, docs = conditioned.shape[0], documents.shape[0]
    result = []
    for step in range(STEPS):
        behind = [(row, (row - step) % n_rows) for row in range(n_rows)]
        block = lax.ppermute(documents, "rows", behind) if step else documents

        def ahead(row, step=step):
            return lax.rem(row + step, n_rows)

        kernel = functools.partial(turned_kernel, shares, ahead)
        out_shape = [jax.ShapeDtypeStruct((rows // shares, docs), jnp.bfloat16)] * shares
        scratch = [pltpu.VMEM((rows, docs), jnp.float32)]
        total = direct_sum(scoring(kernel, out_shape, place, conditioned, query_ids, block, (), scratch))
        onward = [(row, (row + step) % n_rows) for row in range(n_rows)]
        result.append(lax.ppermute(total, "rows", onward) if step else total)
    return jnp.stack(result)


def local(train_grads, query_grads, eigenbases, eigenvalues, layer_offsets, query_doc_ids):
    place = jnp.stack([lax.axis_index("layer"), lax.axis_index("rows")]).astype(jnp.int32)
    conditioned = prepare(query_grads, eigenbases, eigenvalues, layer_offsets)
    on_line = lax.axis_size("rows") == 4 and lax.axis_size("layer") == 4
    plan = along_line if on_line else around_ring
    return plan(train_grads, conditioned, query_doc_ids[:, None], place)


def solution(mesh):
    in_specs = (
        P(("group", "rows"), "layer"),
        P(("group", "rows"), "layer"),
        P("layer", None, None),
        P("layer", None),
        P("layer"),
        P(("group", "rows")),
    )
    out_specs = P(None, "layer", ("group", "rows"))
    return jax.shard_map(local, mesh=mesh, in_specs=in_specs, out_specs=out_specs, check_vma=False)
```

```python
import functools

import jax
import jax.numpy as jnp
from jax import lax
from jax.experimental import pallas as pl
from jax.experimental.pallas import tpu as pltpu
from jax.sharding import PartitionSpec as P

LDIM = 512
LAY_DEV = 4
STEPS = 4
DAMPING = 0.05
NT = (((1,), (1,)), ((), ()))
MIB = 1024 * 1024


def layer_index():
    return lax.axis_index("layer").astype(jnp.int32)


def row_index():
    return lax.axis_index("rows").astype(jnp.int32)


def prepare_kernel(
    offsets, queries_hbm, bases_hbm, values_hbm, conditioned_ref, queries, bases, values, arrived
):
    copies = [pltpu.make_async_copy(values_hbm, values, arrived.at[0])]
    for layer in range(LAY_DEV):
        columns = queries_hbm.at[:, layer * LDIM : (layer + 1) * LDIM]
        copies.append(pltpu.make_async_copy(columns, queries.at[layer], arrived.at[1 + 2 * layer]))
        copies.append(pltpu.make_async_copy(bases_hbm.at[layer], bases.at[layer], arrived.at[2 + 2 * layer]))
    for copy in copies:
        copy.start()
    base_column = layer_index() * (LAY_DEV * LDIM)
    copies[0].wait()
    for layer in range(LAY_DEV):
        copies[1 + 2 * layer].wait()
        copies[2 + 2 * layer].wait()
        basis = bases[layer]
        projected = jnp.dot(queries[layer], basis, preferred_element_type=jnp.float32)
        scaled = (projected / (values[layer : layer + 1, :] + DAMPING)).astype(jnp.bfloat16)
        restored = lax.dot_general(scaled, basis, NT, preferred_element_type=jnp.float32)
        first = pl.multiple_of(offsets[layer] - base_column, LDIM)
        conditioned_ref[:, pl.ds(first, LDIM)] = restored.astype(jnp.bfloat16)


def prepare(queries, bases, values, offsets):
    rows, dims = queries.shape
    hbm = pl.BlockSpec(memory_space=pltpu.HBM)
    return pl.pallas_call(
        prepare_kernel,
        out_shape=jax.ShapeDtypeStruct((rows, dims), jnp.bfloat16),
        in_specs=[pl.BlockSpec(memory_space=pltpu.SMEM), hbm, hbm, hbm],
        out_specs=pl.BlockSpec(memory_space=pltpu.VMEM),
        scratch_shapes=[
            pltpu.VMEM((LAY_DEV, rows, LDIM), jnp.bfloat16),
            pltpu.VMEM(bases.shape, jnp.bfloat16),
            pltpu.VMEM(values.shape, jnp.float32),
            pltpu.SemaphoreType.DMA((1 + 2 * LAY_DEV,)),
        ],
        compiler_params=pltpu.CompilerParams(vmem_limit_bytes=62 * MIB),
        cost_estimate=pl.CostEstimate(
            flops=4 * rows * dims * LDIM, bytes_accessed=6 * MIB, transcendentals=0
        ),
    )(offsets, queries, bases, values)


def masked_tile(queries, documents, query_ids, block):
    tile = lax.dot_general(queries, documents, NT, preferred_element_type=jnp.float32)
    doc_ids = block * tile.shape[1] + lax.broadcasted_iota(jnp.int32, tile.shape, 1)
    return jnp.where(query_ids == doc_ids, 0.0, tile)


def scoring(kernel, out_shape, conditioned, query_ids, documents, extra=(), scratch=()):
    dims = conditioned.shape[1]
    docs = documents.shape[0]
    rows = sum(shape.shape[0] for shape in out_shape)
    vmem = pl.BlockSpec(memory_space=pltpu.VMEM)
    return pl.pallas_call(
        kernel,
        out_shape=out_shape,
        in_specs=[vmem] * (3 + len(extra)),
        out_specs=[vmem] * len(out_shape),
        scratch_shapes=scratch,
        compiler_params=pltpu.CompilerParams(vmem_limit_bytes=12 * MIB),
        cost_estimate=pl.CostEstimate(
            flops=2 * rows * docs * dims, bytes_accessed=2 * dims * (rows + docs), transcendentals=0
        ),
    )(conditioned, query_ids, documents, *extra)


def turned_kernel(shares, block_of, queries_ref, ids_ref, documents_ref, *refs):
    *out_refs, held = refs
    held[...] = masked_tile(queries_ref[...], documents_ref[...], ids_ref[...], block_of(row_index()))
    for turn, out_ref in enumerate(out_refs):
        share_rows = out_ref.shape[0]
        first = pl.multiple_of(lax.rem(layer_index() + turn, shares) * share_rows, share_rows)
        out_ref[...] = held[pl.ds(first, share_rows), :].astype(jnp.bfloat16)


def half_shares(share_rows, kept):
    core = lax.rem(layer_index(), 2)
    core = core if kept else 1 - core
    return [pl.multiple_of((2 * chip + core) * share_rows, share_rows) for chip in range(2)]


def halves_kernel(block_of, queries_ref, ids_ref, documents_ref, *refs):
    front_refs, out_refs, held = refs[:-3], refs[-3:-1], refs[-1]
    held[...] = masked_tile(queries_ref[...], documents_ref[...], ids_ref[...], block_of(row_index()))
    docs = documents_ref.shape[0]
    rows, width = out_refs[0].shape
    for side, kept in enumerate((True, False)):
        if front_refs:
            out_refs[side][:, : width - docs] = front_refs[side][...]
        for chip, first in enumerate(half_shares(rows // 2, kept)):
            spot = slice(chip * (rows // 2), (chip + 1) * (rows // 2))
            out_refs[side][spot, width - docs :] = held[pl.ds(first, rows // 2), :]


def half_kernel(block_of, kept, queries_ref, ids_ref, documents_ref, out_ref):
    share_rows = out_ref.shape[0] // 2
    firsts = half_shares(share_rows, kept)
    queries = jnp.concatenate([queries_ref[pl.ds(first, share_rows), :] for first in firsts], axis=0)
    query_ids = jnp.concatenate([ids_ref[pl.ds(first, share_rows), :] for first in firsts], axis=0)
    out_ref[...] = masked_tile(queries, documents_ref[...], query_ids, block_of(row_index()))


def total_of(refs):
    total = refs[0][...].astype(jnp.float32)
    for ref in refs[1:]:
        total += ref[...].astype(jnp.float32)
    return total


def sum_kernel(*refs):
    refs[-1][...] = total_of(refs[:-1])


def small_call(kernel, out_shape, *args):
    vmem = pl.BlockSpec(memory_space=pltpu.VMEM)
    return pl.pallas_call(
        kernel,
        out_shape=out_shape,
        in_specs=[vmem] * len(args),
        out_specs=[vmem] * len(out_shape),
        compiler_params=pltpu.CompilerParams(vmem_limit_bytes=4 * MIB),
    )(*args)


def direct_sum(tiles):
    shares = len(tiles)
    arrived = [tiles[0]]
    for turn in range(1, shares):
        pairs = [(lay, (lay + turn) % shares) for lay in range(shares)]
        arrived.append(lax.ppermute(tiles[turn], "layer", pairs))
    (total,) = small_call(sum_kernel, [jax.ShapeDtypeStruct(tiles[0].shape, jnp.float32)], *arrived)
    return total


def core_sum_kernel(kept_ref, arrived_ref, mine_ref, other_ref):
    rows = mine_ref.shape[0]
    chip = lax.div(layer_index(), 2)
    mine = pl.ds(pl.multiple_of(chip * rows, rows), rows)
    other = pl.ds(pl.multiple_of((1 - chip) * rows, rows), rows)
    mine_ref[...] = (kept_ref[mine, :] + arrived_ref[mine, :]).astype(mine_ref.dtype)
    other_ref[...] = (kept_ref[other, :] + arrived_ref[other, :]).astype(other_ref.dtype)


def chip_sum_kernel(mine_ref, arrived_ref, *out_refs):
    docs = out_refs[0].shape[1]
    for spot, out_ref in enumerate(out_refs):
        columns = slice(spot * docs, (spot + 1) * docs)
        total = mine_ref[:, columns] + arrived_ref[:, columns].astype(jnp.float32)
        out_ref[...] = total.astype(out_ref.dtype)


def swap(value, distance):
    count = lax.axis_size("layer")
    return lax.ppermute(value, "layer", [(lay, lay ^ distance) for lay in range(count)])


def core_sum(kept, arrived, mine_type):
    rows, width = kept.shape[0] // 2, kept.shape[1]
    out_shape = [jax.ShapeDtypeStruct((rows, width), out_type) for out_type in (mine_type, jnp.bfloat16)]
    return small_call(core_sum_kernel, out_shape, kept, arrived)


def layer_sum(kept, sent, out_types):
    mine, other = core_sum(kept, swap(sent, 1), jnp.float32)
    rows, docs = mine.shape[0], mine.shape[1] // len(out_types)
    out_shape = [jax.ShapeDtypeStruct((rows, docs), out_type) for out_type in out_types]
    return small_call(chip_sum_kernel, out_shape, mine, swap(other, 2))


ROUND_ONE = ((0, 2), (2, 3), (3, 1), (1, 0))
ROUND_TWO = ((0, 1), (1, 3), (3, 2), (2, 0))
BLOCK_ONE = (1, 3, 0, 2)
BLOCK_TWO = (2, 0, 3, 1)
BLOCK_LAST = (3, 2, 1, 0)


def pick(table):
    def entry(row):
        value = jnp.int32(table[0])
        for index in range(1, len(table)):
            value = jnp.where(row == index, jnp.int32(table[index]), value)
        return value

    return entry


def step_of(table):
    return pick([(block - table.index(block)) % STEPS for block in range(STEPS)])


def assemble_kernel(own_ref, first_ref, second_ref, out_ref):
    out_ref[0] = own_ref[...]
    for ref, table in ((first_ref, BLOCK_ONE), (second_ref, BLOCK_TWO)):
        out_ref[step_of(table)(row_index())] = ref[...].astype(jnp.float32)


def finish_kernel(mine_ref, other_ref, scores_hbm, out_hbm, total, copied):
    del scores_hbm
    total[...] = total_of([mine_ref, other_ref])
    copy = pltpu.make_async_copy(total, out_hbm.at[step_of(BLOCK_LAST)(row_index())], copied)
    copy.start()
    copy.wait()


def finish(mine, other, scores):
    hbm = pl.BlockSpec(memory_space=pltpu.HBM)
    vmem = pl.BlockSpec(memory_space=pltpu.VMEM)
    return pl.pallas_call(
        finish_kernel,
        out_shape=jax.ShapeDtypeStruct(scores.shape, scores.dtype),
        in_specs=[vmem, vmem, hbm],
        out_specs=hbm,
        scratch_shapes=[pltpu.VMEM(mine.shape, jnp.float32), pltpu.SemaphoreType.DMA],
        input_output_aliases={2: 0},
        compiler_params=pltpu.CompilerParams(vmem_limit_bytes=4 * MIB),
    )(mine, other, scores)


def along_line(documents, conditioned, query_ids):
    docs = documents.shape[0]
    half = (conditioned.shape[0] // 2, docs)

    def halves(block, block_of, front=()):
        width = docs * (1 + bool(front))
        out_shape = [jax.ShapeDtypeStruct((half[0], width), jnp.float32)] * 2
        scratch = [pltpu.VMEM((2 * half[0], docs), jnp.float32)]
        kernel = functools.partial(halves_kernel, block_of)
        return scoring(kernel, out_shape, conditioned, query_ids, block, front, scratch)

    def one_half(block, block_of, kept):
        kernel = functools.partial(half_kernel, block_of, kept)
        out_shape = [jax.ShapeDtypeStruct(half, jnp.float32)]
        return scoring(kernel, out_shape, conditioned, query_ids, block)[0]

    def back(total, table):
        return lax.ppermute(total, "rows", tuple(enumerate(table)))

    one = lax.ppermute(documents, "rows", ROUND_ONE)
    later, conditioned = lax.optimization_barrier((documents, conditioned))
    two = lax.ppermute(later, "rows", ROUND_TWO)
    own = halves(later, lambda row: row)
    one, own = lax.optimization_barrier((one, own))
    three = lax.ppermute(one, "rows", ROUND_ONE)

    own, first = layer_sum(*halves(one, pick(BLOCK_ONE), own), (jnp.float32, jnp.bfloat16))
    two, first = lax.optimization_barrier((two, first))
    first = back(first, BLOCK_ONE)
    (second,) = layer_sum(*halves(two, pick(BLOCK_TWO)), (jnp.bfloat16,))
    second = back(second, BLOCK_TWO)
    three, first, second = lax.optimization_barrier((three, first, second))

    arrived = swap(one_half(three, pick(BLOCK_LAST), False), 1)
    kept = one_half(three, pick(BLOCK_LAST), True)
    mine, other = core_sum(kept, arrived, jnp.bfloat16)
    mine = back(mine, BLOCK_LAST)
    shares = lax.axis_size("layer")
    pairs = [
        (row * shares + lay, BLOCK_LAST[row] * shares + (lay ^ 2))
        for row in range(len(BLOCK_LAST))
        for lay in range(shares)
    ]
    other = lax.ppermute(other, ("rows", "layer"), pairs)
    out_shape = [jax.ShapeDtypeStruct((STEPS,) + own.shape, jnp.float32)]
    (scores,) = small_call(assemble_kernel, out_shape, own, first, second)
    return finish(mine, other, scores)


def around_ring(documents, conditioned, query_ids):
    n_rows, shares = lax.axis_size("rows"), lax.axis_size("layer")
    rows, docs = conditioned.shape[0], documents.shape[0]
    result = []
    for step in range(STEPS):
        behind = [(row, (row - step) % n_rows) for row in range(n_rows)]
        block = lax.ppermute(documents, "rows", behind) if step else documents

        def ahead(row, step=step):
            return lax.rem(row + step, n_rows)

        kernel = functools.partial(turned_kernel, shares, ahead)
        out_shape = [jax.ShapeDtypeStruct((rows // shares, docs), jnp.bfloat16)] * shares
        scratch = [pltpu.VMEM((rows, docs), jnp.float32)]
        total = direct_sum(scoring(kernel, out_shape, conditioned, query_ids, block, (), scratch))
        onward = [(row, (row + step) % n_rows) for row in range(n_rows)]
        result.append(lax.ppermute(total, "rows", onward) if step else total)
    return jnp.stack(result)


def local(train_grads, query_grads, eigenbases, eigenvalues, layer_offsets, query_doc_ids):
    conditioned = prepare(query_grads, eigenbases, eigenvalues, layer_offsets)
    on_line = lax.axis_size("rows") == 4 and lax.axis_size("layer") == 4
    plan = along_line if on_line else around_ring
    return plan(train_grads, conditioned, query_doc_ids[:, None])


def solution(mesh):
    in_specs = (
        P(("group", "rows"), "layer"),
        P(("group", "rows"), "layer"),
        P("layer", None, None),
        P("layer", None),
        P("layer"),
        P(("group", "rows")),
    )
    out_specs = P(None, "layer", ("group", "rows"))
    return jax.shard_map(local, mesh=mesh, in_specs=in_specs, out_specs=out_specs, check_vma=False)
```

```python
import functools

import jax
import jax.numpy as jnp
from jax import lax
from jax.experimental import pallas as pl
from jax.experimental.pallas import tpu as pltpu
from jax.sharding import PartitionSpec as P

LDIM = 512
LAY_DEV = 4
STEPS = 4
DAMPING = 0.05
NT = (((1,), (1,)), ((), ()))
MIB = 1024 * 1024


def layer_index():
    return lax.axis_index("layer").astype(jnp.int32)


def row_index():
    return lax.axis_index("rows").astype(jnp.int32)


def prepare_kernel(
    offsets, queries_hbm, bases_hbm, values_hbm, conditioned_ref, queries, bases, values, arrived
):
    copies = [pltpu.make_async_copy(values_hbm, values, arrived.at[0])]
    for layer in range(LAY_DEV):
        columns = queries_hbm.at[:, layer * LDIM : (layer + 1) * LDIM]
        copies.append(pltpu.make_async_copy(columns, queries.at[layer], arrived.at[1 + 2 * layer]))
        copies.append(pltpu.make_async_copy(bases_hbm.at[layer], bases.at[layer], arrived.at[2 + 2 * layer]))
    for copy in copies:
        copy.start()
    base_column = layer_index() * (LAY_DEV * LDIM)
    copies[0].wait()
    for layer in range(LAY_DEV):
        copies[1 + 2 * layer].wait()
        copies[2 + 2 * layer].wait()
        basis = bases[layer]
        projected = jnp.dot(queries[layer], basis, preferred_element_type=jnp.float32)
        scaled = (projected / (values[layer : layer + 1, :] + DAMPING)).astype(jnp.bfloat16)
        restored = lax.dot_general(scaled, basis, NT, preferred_element_type=jnp.float32)
        first = pl.multiple_of(offsets[layer] - base_column, LDIM)
        conditioned_ref[:, pl.ds(first, LDIM)] = restored.astype(jnp.bfloat16)


def prepare(queries, bases, values, offsets):
    rows, dims = queries.shape
    hbm = pl.BlockSpec(memory_space=pltpu.HBM)
    return pl.pallas_call(
        prepare_kernel,
        out_shape=jax.ShapeDtypeStruct((rows, dims), jnp.bfloat16),
        in_specs=[pl.BlockSpec(memory_space=pltpu.SMEM), hbm, hbm, hbm],
        out_specs=pl.BlockSpec(memory_space=pltpu.VMEM),
        scratch_shapes=[
            pltpu.VMEM((LAY_DEV, rows, LDIM), jnp.bfloat16),
            pltpu.VMEM(bases.shape, jnp.bfloat16),
            pltpu.VMEM(values.shape, jnp.float32),
            pltpu.SemaphoreType.DMA((1 + 2 * LAY_DEV,)),
        ],
        compiler_params=pltpu.CompilerParams(vmem_limit_bytes=62 * MIB),
        cost_estimate=pl.CostEstimate(
            flops=4 * rows * dims * LDIM, bytes_accessed=6 * MIB, transcendentals=0
        ),
    )(offsets, queries, bases, values)


def masked_tile(queries, documents, query_ids, block):
    tile = lax.dot_general(queries, documents, NT, preferred_element_type=jnp.float32)
    doc_ids = block * tile.shape[1] + lax.broadcasted_iota(jnp.int32, tile.shape, 1)
    return jnp.where(query_ids == doc_ids, 0.0, tile)


def scoring(kernel, out_shape, conditioned, query_ids, documents, extra=(), scratch=()):
    dims = conditioned.shape[1]
    docs = documents.shape[0]
    rows = sum(shape.shape[0] for shape in out_shape)
    vmem = pl.BlockSpec(memory_space=pltpu.VMEM)
    return pl.pallas_call(
        kernel,
        out_shape=out_shape,
        in_specs=[vmem] * (3 + len(extra)),
        out_specs=[vmem] * len(out_shape),
        scratch_shapes=scratch,
        compiler_params=pltpu.CompilerParams(vmem_limit_bytes=12 * MIB),
        cost_estimate=pl.CostEstimate(
            flops=2 * rows * docs * dims, bytes_accessed=2 * dims * (rows + docs), transcendentals=0
        ),
    )(conditioned, query_ids, documents, *extra)


def turned_kernel(shares, block_of, queries_ref, ids_ref, documents_ref, *refs):
    *out_refs, held = refs
    held[...] = masked_tile(queries_ref[...], documents_ref[...], ids_ref[...], block_of(row_index()))
    for turn, out_ref in enumerate(out_refs):
        share_rows = out_ref.shape[0]
        first = pl.multiple_of(lax.rem(layer_index() + turn, shares) * share_rows, share_rows)
        out_ref[...] = held[pl.ds(first, share_rows), :].astype(jnp.bfloat16)


def half_shares(share_rows, kept):
    core = lax.rem(layer_index(), 2)
    core = core if kept else 1 - core
    return [pl.multiple_of((2 * chip + core) * share_rows, share_rows) for chip in range(2)]


def halves_kernel(block_of, queries_ref, ids_ref, documents_ref, *refs):
    front_refs, out_refs, held = refs[:-3], refs[-3:-1], refs[-1]
    held[...] = masked_tile(queries_ref[...], documents_ref[...], ids_ref[...], block_of(row_index()))
    docs = documents_ref.shape[0]
    rows, width = out_refs[0].shape
    for side, kept in enumerate((True, False)):
        if front_refs:
            out_refs[side][:, : width - docs] = front_refs[side][...]
        for chip, first in enumerate(half_shares(rows // 2, kept)):
            spot = slice(chip * (rows // 2), (chip + 1) * (rows // 2))
            out_refs[side][spot, width - docs :] = held[pl.ds(first, rows // 2), :]


def half_kernel(block_of, kept, queries_ref, ids_ref, documents_ref, out_ref):
    share_rows = out_ref.shape[0] // 2
    firsts = half_shares(share_rows, kept)
    queries = jnp.concatenate([queries_ref[pl.ds(first, share_rows), :] for first in firsts], axis=0)
    query_ids = jnp.concatenate([ids_ref[pl.ds(first, share_rows), :] for first in firsts], axis=0)
    out_ref[...] = masked_tile(queries, documents_ref[...], query_ids, block_of(row_index()))


def total_of(refs):
    total = refs[0][...].astype(jnp.float32)
    for ref in refs[1:]:
        total += ref[...].astype(jnp.float32)
    return total


def sum_kernel(*refs):
    refs[-1][...] = total_of(refs[:-1])


def small_call(kernel, out_shape, *args):
    vmem = pl.BlockSpec(memory_space=pltpu.VMEM)
    return pl.pallas_call(
        kernel,
        out_shape=out_shape,
        in_specs=[vmem] * len(args),
        out_specs=[vmem] * len(out_shape),
        compiler_params=pltpu.CompilerParams(vmem_limit_bytes=4 * MIB),
    )(*args)


def direct_sum(tiles):
    shares = len(tiles)
    arrived = [tiles[0]]
    for turn in range(1, shares):
        pairs = [(lay, (lay + turn) % shares) for lay in range(shares)]
        arrived.append(lax.ppermute(tiles[turn], "layer", pairs))
    (total,) = small_call(sum_kernel, [jax.ShapeDtypeStruct(tiles[0].shape, jnp.float32)], *arrived)
    return total


def core_sum_kernel(kept_ref, arrived_ref, mine_ref, other_ref):
    rows = mine_ref.shape[0]
    chip = lax.div(layer_index(), 2)
    mine = pl.ds(pl.multiple_of(chip * rows, rows), rows)
    other = pl.ds(pl.multiple_of((1 - chip) * rows, rows), rows)
    mine_ref[...] = (kept_ref[mine, :] + arrived_ref[mine, :]).astype(mine_ref.dtype)
    other_ref[...] = (kept_ref[other, :] + arrived_ref[other, :]).astype(other_ref.dtype)


def chip_sum_kernel(mine_ref, arrived_ref, *out_refs):
    docs = out_refs[0].shape[1]
    for spot, out_ref in enumerate(out_refs):
        columns = slice(spot * docs, (spot + 1) * docs)
        total = mine_ref[:, columns] + arrived_ref[:, columns].astype(jnp.float32)
        out_ref[...] = total.astype(out_ref.dtype)


def swap(value, distance):
    count = lax.axis_size("layer")
    return lax.ppermute(value, "layer", [(lay, lay ^ distance) for lay in range(count)])


def core_sum(kept, arrived, mine_type):
    rows, width = kept.shape[0] // 2, kept.shape[1]
    out_shape = [jax.ShapeDtypeStruct((rows, width), out_type) for out_type in (mine_type, jnp.bfloat16)]
    return small_call(core_sum_kernel, out_shape, kept, arrived)


def layer_sum(kept, sent, out_types):
    mine, other = core_sum(kept, swap(sent, 1), jnp.float32)
    rows, docs = mine.shape[0], mine.shape[1] // len(out_types)
    out_shape = [jax.ShapeDtypeStruct((rows, docs), out_type) for out_type in out_types]
    return small_call(chip_sum_kernel, out_shape, mine, swap(other, 2))


ROUND_ONE = ((0, 1), (1, 2), (2, 3), (3, 0))
ROUND_TWO = ((0, 3), (1, 0), (2, 1), (3, 2))
BLOCK_ONE = (3, 0, 1, 2)
BLOCK_TWO = (1, 2, 3, 0)
BLOCK_LAST = (2, 3, 0, 1)


def pick(table):
    def entry(row):
        value = jnp.int32(table[0])
        for index in range(1, len(table)):
            value = jnp.where(row == index, jnp.int32(table[index]), value)
        return value

    return entry


def step_of(table):
    return pick([(block - table.index(block)) % STEPS for block in range(STEPS)])


def assemble_kernel(own_ref, first_ref, second_ref, out_ref):
    out_ref[0] = own_ref[...]
    for ref, table in ((first_ref, BLOCK_ONE), (second_ref, BLOCK_TWO)):
        out_ref[step_of(table)(row_index())] = ref[...].astype(jnp.float32)


def finish_kernel(mine_ref, other_ref, scores_hbm, out_hbm, total, copied):
    del scores_hbm
    total[...] = total_of([mine_ref, other_ref])
    copy = pltpu.make_async_copy(total, out_hbm.at[step_of(BLOCK_LAST)(row_index())], copied)
    copy.start()
    copy.wait()


def finish(mine, other, scores):
    hbm = pl.BlockSpec(memory_space=pltpu.HBM)
    vmem = pl.BlockSpec(memory_space=pltpu.VMEM)
    return pl.pallas_call(
        finish_kernel,
        out_shape=jax.ShapeDtypeStruct(scores.shape, scores.dtype),
        in_specs=[vmem, vmem, hbm],
        out_specs=hbm,
        scratch_shapes=[pltpu.VMEM(mine.shape, jnp.float32), pltpu.SemaphoreType.DMA],
        input_output_aliases={2: 0},
        compiler_params=pltpu.CompilerParams(vmem_limit_bytes=4 * MIB),
    )(mine, other, scores)


def along_line(documents, conditioned, query_ids):
    docs = documents.shape[0]
    half = (conditioned.shape[0] // 2, docs)

    def halves(block, block_of, front=()):
        width = docs * (1 + bool(front))
        out_shape = [jax.ShapeDtypeStruct((half[0], width), jnp.float32)] * 2
        scratch = [pltpu.VMEM((2 * half[0], docs), jnp.float32)]
        kernel = functools.partial(halves_kernel, block_of)
        return scoring(kernel, out_shape, conditioned, query_ids, block, front, scratch)

    def one_half(block, block_of, kept):
        kernel = functools.partial(half_kernel, block_of, kept)
        out_shape = [jax.ShapeDtypeStruct(half, jnp.float32)]
        return scoring(kernel, out_shape, conditioned, query_ids, block)[0]

    def back(total, table):
        return lax.ppermute(total, "rows", tuple(enumerate(table)))

    one = lax.ppermute(documents, "rows", ROUND_ONE)
    later, conditioned = lax.optimization_barrier((documents, conditioned))
    two = lax.ppermute(later, "rows", ROUND_TWO)
    own = halves(later, lambda row: row)
    one, own = lax.optimization_barrier((one, own))
    three = lax.ppermute(one, "rows", ROUND_ONE)

    own, first = layer_sum(*halves(one, pick(BLOCK_ONE), own), (jnp.float32, jnp.bfloat16))
    two, first = lax.optimization_barrier((two, first))
    first = back(first, BLOCK_ONE)
    (second,) = layer_sum(*halves(two, pick(BLOCK_TWO)), (jnp.bfloat16,))
    second = back(second, BLOCK_TWO)
    three, first, second = lax.optimization_barrier((three, first, second))

    arrived = swap(one_half(three, pick(BLOCK_LAST), False), 1)
    kept = one_half(three, pick(BLOCK_LAST), True)
    mine, other = core_sum(kept, arrived, jnp.bfloat16)
    shares = lax.axis_size("layer")
    pairs = [
        (row * shares + lay, BLOCK_LAST[row] * shares + (lay ^ 2))
        for row in range(len(BLOCK_LAST))
        for lay in range(shares)
    ]
    other = lax.ppermute(other, ("rows", "layer"), pairs)
    mine = back(mine, BLOCK_LAST)
    out_shape = [jax.ShapeDtypeStruct((STEPS,) + own.shape, jnp.float32)]
    (scores,) = small_call(assemble_kernel, out_shape, own, first, second)
    return finish(mine, other, scores)


def around_ring(documents, conditioned, query_ids):
    n_rows, shares = lax.axis_size("rows"), lax.axis_size("layer")
    rows, docs = conditioned.shape[0], documents.shape[0]
    result = []
    for step in range(STEPS):
        behind = [(row, (row - step) % n_rows) for row in range(n_rows)]
        block = lax.ppermute(documents, "rows", behind) if step else documents

        def ahead(row, step=step):
            return lax.rem(row + step, n_rows)

        kernel = functools.partial(turned_kernel, shares, ahead)
        out_shape = [jax.ShapeDtypeStruct((rows // shares, docs), jnp.bfloat16)] * shares
        scratch = [pltpu.VMEM((rows, docs), jnp.float32)]
        total = direct_sum(scoring(kernel, out_shape, conditioned, query_ids, block, (), scratch))
        onward = [(row, (row + step) % n_rows) for row in range(n_rows)]
        result.append(lax.ppermute(total, "rows", onward) if step else total)
    return jnp.stack(result)


def local(train_grads, query_grads, eigenbases, eigenvalues, layer_offsets, query_doc_ids):
    conditioned = prepare(query_grads, eigenbases, eigenvalues, layer_offsets)
    on_line = lax.axis_size("rows") == 4 and lax.axis_size("layer") == 4
    plan = along_line if on_line else around_ring
    return plan(train_grads, conditioned, query_doc_ids[:, None])


def solution(mesh):
    in_specs = (
        P(("group", "rows"), "layer"),
        P(("group", "rows"), "layer"),
        P("layer", None, None),
        P("layer", None),
        P("layer"),
        P(("group", "rows")),
    )
    out_specs = P(None, "layer", ("group", "rows"))
    return jax.shard_map(local, mesh=mesh, in_specs=in_specs, out_specs=out_specs, check_vma=False)
```

```python
import functools

import jax
import jax.numpy as jnp
from jax import lax
from jax.experimental import pallas as pl
from jax.experimental.pallas import tpu as pltpu
from jax.sharding import PartitionSpec as P

LDIM = 512
LAY_DEV = 4
STEPS = 4
DAMPING = 0.05
NT = (((1,), (1,)), ((), ()))
MIB = 1024 * 1024


def layer_index():
    return lax.axis_index("layer").astype(jnp.int32)


def row_index():
    return lax.axis_index("rows").astype(jnp.int32)


def prepare_kernel(
    offsets, queries_hbm, bases_hbm, values_hbm, conditioned_ref, queries, bases, values, arrived
):
    copies = [pltpu.make_async_copy(values_hbm, values, arrived.at[0])]
    for layer in range(LAY_DEV):
        columns = queries_hbm.at[:, layer * LDIM : (layer + 1) * LDIM]
        copies.append(pltpu.make_async_copy(columns, queries.at[layer], arrived.at[1 + 2 * layer]))
        copies.append(pltpu.make_async_copy(bases_hbm.at[layer], bases.at[layer], arrived.at[2 + 2 * layer]))
    for copy in copies:
        copy.start()
    base_column = layer_index() * (LAY_DEV * LDIM)
    copies[0].wait()
    for layer in range(LAY_DEV):
        copies[1 + 2 * layer].wait()
        copies[2 + 2 * layer].wait()
        basis = bases[layer]
        projected = jnp.dot(queries[layer], basis, preferred_element_type=jnp.float32)
        scaled = (projected / (values[layer : layer + 1, :] + DAMPING)).astype(jnp.bfloat16)
        restored = lax.dot_general(scaled, basis, NT, preferred_element_type=jnp.float32)
        first = pl.multiple_of(offsets[layer] - base_column, LDIM)
        conditioned_ref[:, pl.ds(first, LDIM)] = restored.astype(jnp.bfloat16)


def prepare(queries, bases, values, offsets):
    rows, dims = queries.shape
    hbm = pl.BlockSpec(memory_space=pltpu.HBM)
    return pl.pallas_call(
        prepare_kernel,
        out_shape=jax.ShapeDtypeStruct((rows, dims), jnp.bfloat16),
        in_specs=[pl.BlockSpec(memory_space=pltpu.SMEM), hbm, hbm, hbm],
        out_specs=pl.BlockSpec(memory_space=pltpu.VMEM),
        scratch_shapes=[
            pltpu.VMEM((LAY_DEV, rows, LDIM), jnp.bfloat16),
            pltpu.VMEM(bases.shape, jnp.bfloat16),
            pltpu.VMEM(values.shape, jnp.float32),
            pltpu.SemaphoreType.DMA((1 + 2 * LAY_DEV,)),
        ],
        compiler_params=pltpu.CompilerParams(vmem_limit_bytes=62 * MIB),
        cost_estimate=pl.CostEstimate(
            flops=4 * rows * dims * LDIM, bytes_accessed=6 * MIB, transcendentals=0
        ),
    )(offsets, queries, bases, values)


def masked_tile(queries, documents, query_ids, block):
    tile = lax.dot_general(queries, documents, NT, preferred_element_type=jnp.float32)
    doc_ids = block * tile.shape[1] + lax.broadcasted_iota(jnp.int32, tile.shape, 1)
    return jnp.where(query_ids == doc_ids, 0.0, tile)


def scoring(kernel, out_shape, conditioned, query_ids, documents, extra=(), scratch=()):
    dims = conditioned.shape[1]
    docs = documents.shape[0]
    rows = sum(shape.shape[0] for shape in out_shape)
    vmem = pl.BlockSpec(memory_space=pltpu.VMEM)
    return pl.pallas_call(
        kernel,
        out_shape=out_shape,
        in_specs=[vmem] * (3 + len(extra)),
        out_specs=[vmem] * len(out_shape),
        scratch_shapes=scratch,
        compiler_params=pltpu.CompilerParams(vmem_limit_bytes=12 * MIB),
        cost_estimate=pl.CostEstimate(
            flops=2 * rows * docs * dims, bytes_accessed=2 * dims * (rows + docs), transcendentals=0
        ),
    )(conditioned, query_ids, documents, *extra)


def turned_kernel(shares, block_of, queries_ref, ids_ref, documents_ref, *refs):
    *out_refs, held = refs
    held[...] = masked_tile(queries_ref[...], documents_ref[...], ids_ref[...], block_of(row_index()))
    for turn, out_ref in enumerate(out_refs):
        share_rows = out_ref.shape[0]
        first = pl.multiple_of(lax.rem(layer_index() + turn, shares) * share_rows, share_rows)
        out_ref[...] = held[pl.ds(first, share_rows), :].astype(jnp.bfloat16)


def half_shares(share_rows, kept):
    core = lax.rem(layer_index(), 2)
    core = core if kept else 1 - core
    return [pl.multiple_of((2 * chip + core) * share_rows, share_rows) for chip in range(2)]


def halves_kernel(block_of, queries_ref, ids_ref, documents_ref, *refs):
    front_refs, out_refs, held = refs[:-3], refs[-3:-1], refs[-1]
    held[...] = masked_tile(queries_ref[...], documents_ref[...], ids_ref[...], block_of(row_index()))
    docs = documents_ref.shape[0]
    rows, width = out_refs[0].shape
    for side, kept in enumerate((True, False)):
        if front_refs:
            out_refs[side][:, : width - docs] = front_refs[side][...]
        for chip, first in enumerate(half_shares(rows // 2, kept)):
            spot = slice(chip * (rows // 2), (chip + 1) * (rows // 2))
            out_refs[side][spot, width - docs :] = held[pl.ds(first, rows // 2), :]


def half_kernel(block_of, kept, queries_ref, ids_ref, documents_ref, out_ref):
    share_rows = out_ref.shape[0] // 2
    firsts = half_shares(share_rows, kept)
    queries = jnp.concatenate([queries_ref[pl.ds(first, share_rows), :] for first in firsts], axis=0)
    query_ids = jnp.concatenate([ids_ref[pl.ds(first, share_rows), :] for first in firsts], axis=0)
    out_ref[...] = masked_tile(queries, documents_ref[...], query_ids, block_of(row_index()))


def total_of(refs):
    total = refs[0][...].astype(jnp.float32)
    for ref in refs[1:]:
        total += ref[...].astype(jnp.float32)
    return total


def sum_kernel(*refs):
    refs[-1][...] = total_of(refs[:-1])


def small_call(kernel, out_shape, *args):
    vmem = pl.BlockSpec(memory_space=pltpu.VMEM)
    return pl.pallas_call(
        kernel,
        out_shape=out_shape,
        in_specs=[vmem] * len(args),
        out_specs=[vmem] * len(out_shape),
        compiler_params=pltpu.CompilerParams(vmem_limit_bytes=4 * MIB),
    )(*args)


def direct_sum(tiles):
    shares = len(tiles)
    arrived = [tiles[0]]
    for turn in range(1, shares):
        pairs = [(lay, (lay + turn) % shares) for lay in range(shares)]
        arrived.append(lax.ppermute(tiles[turn], "layer", pairs))
    (total,) = small_call(sum_kernel, [jax.ShapeDtypeStruct(tiles[0].shape, jnp.float32)], *arrived)
    return total


def core_sum_kernel(kept_ref, arrived_ref, mine_ref, other_ref):
    rows = mine_ref.shape[0]
    chip = lax.div(layer_index(), 2)
    mine = pl.ds(pl.multiple_of(chip * rows, rows), rows)
    other = pl.ds(pl.multiple_of((1 - chip) * rows, rows), rows)
    mine_ref[...] = (kept_ref[mine, :] + arrived_ref[mine, :]).astype(mine_ref.dtype)
    other_ref[...] = (kept_ref[other, :] + arrived_ref[other, :]).astype(other_ref.dtype)


def chip_sum_kernel(mine_ref, arrived_ref, *out_refs):
    docs = out_refs[0].shape[1]
    for spot, out_ref in enumerate(out_refs):
        columns = slice(spot * docs, (spot + 1) * docs)
        total = mine_ref[:, columns] + arrived_ref[:, columns].astype(jnp.float32)
        out_ref[...] = total.astype(out_ref.dtype)


def swap(value, distance):
    count = lax.axis_size("layer")
    return lax.ppermute(value, "layer", [(lay, lay ^ distance) for lay in range(count)])


def core_sum(kept, arrived, mine_type):
    rows, width = kept.shape[0] // 2, kept.shape[1]
    out_shape = [jax.ShapeDtypeStruct((rows, width), out_type) for out_type in (mine_type, jnp.bfloat16)]
    return small_call(core_sum_kernel, out_shape, kept, arrived)


def layer_sum(kept, sent, out_types):
    mine, other = core_sum(kept, swap(sent, 1), jnp.float32)
    rows, docs = mine.shape[0], mine.shape[1] // len(out_types)
    out_shape = [jax.ShapeDtypeStruct((rows, docs), out_type) for out_type in out_types]
    return small_call(chip_sum_kernel, out_shape, mine, swap(other, 2))


ROUND_ONE = ((0, 2), (2, 3), (3, 1), (1, 0))
ROUND_TWO = ((0, 1), (1, 3), (3, 2), (2, 0))
BLOCK_ONE = (1, 3, 0, 2)
BLOCK_TWO = (2, 0, 3, 1)
BLOCK_LAST = (3, 2, 1, 0)


def pick(table):
    def entry(row):
        value = jnp.int32(table[0])
        for index in range(1, len(table)):
            value = jnp.where(row == index, jnp.int32(table[index]), value)
        return value

    return entry


def step_of(table):
    return pick([(block - table.index(block)) % STEPS for block in range(STEPS)])


def assemble_kernel(own_ref, first_ref, second_ref, out_ref):
    out_ref[0] = own_ref[...]
    for ref, table in ((first_ref, BLOCK_ONE), (second_ref, BLOCK_TWO)):
        out_ref[step_of(table)(row_index())] = ref[...].astype(jnp.float32)


def finish_kernel(mine_ref, other_ref, scores_hbm, out_hbm, total, copied):
    del scores_hbm
    total[...] = total_of([mine_ref, other_ref])
    copy = pltpu.make_async_copy(total, out_hbm.at[step_of(BLOCK_LAST)(row_index())], copied)
    copy.start()
    copy.wait()


def finish(mine, other, scores):
    hbm = pl.BlockSpec(memory_space=pltpu.HBM)
    vmem = pl.BlockSpec(memory_space=pltpu.VMEM)
    return pl.pallas_call(
        finish_kernel,
        out_shape=jax.ShapeDtypeStruct(scores.shape, scores.dtype),
        in_specs=[vmem, vmem, hbm],
        out_specs=hbm,
        scratch_shapes=[pltpu.VMEM(mine.shape, jnp.float32), pltpu.SemaphoreType.DMA],
        input_output_aliases={2: 0},
        compiler_params=pltpu.CompilerParams(vmem_limit_bytes=4 * MIB),
    )(mine, other, scores)


def along_line(documents, conditioned, query_ids):
    docs = documents.shape[0]
    half = (conditioned.shape[0] // 2, docs)

    def halves(block, block_of, front=()):
        width = docs * (1 + bool(front))
        out_shape = [jax.ShapeDtypeStruct((half[0], width), jnp.float32)] * 2
        scratch = [pltpu.VMEM((2 * half[0], docs), jnp.float32)]
        kernel = functools.partial(halves_kernel, block_of)
        return scoring(kernel, out_shape, conditioned, query_ids, block, front, scratch)

    def one_half(block, block_of, kept):
        kernel = functools.partial(half_kernel, block_of, kept)
        out_shape = [jax.ShapeDtypeStruct(half, jnp.float32)]
        return scoring(kernel, out_shape, conditioned, query_ids, block)[0]

    def back(total, table):
        return lax.ppermute(total, "rows", tuple(enumerate(table)))

    one = lax.ppermute(documents, "rows", ROUND_ONE)
    two = lax.ppermute(documents, "rows", ROUND_TWO)
    own = halves(documents, lambda row: row)
    one, own = lax.optimization_barrier((one, own))
    three = lax.ppermute(one, "rows", ROUND_ONE)

    own, first = layer_sum(*halves(one, pick(BLOCK_ONE), own), (jnp.float32, jnp.bfloat16))
    two, first = lax.optimization_barrier((two, first))
    first = back(first, BLOCK_ONE)
    (second,) = layer_sum(*halves(two, pick(BLOCK_TWO)), (jnp.bfloat16,))
    second = back(second, BLOCK_TWO)
    three, first, second = lax.optimization_barrier((three, first, second))

    arrived = swap(one_half(three, pick(BLOCK_LAST), False), 1)
    kept = one_half(three, pick(BLOCK_LAST), True)
    mine, other = core_sum(kept, arrived, jnp.bfloat16)
    shares = lax.axis_size("layer")
    pairs = [
        (row * shares + lay, BLOCK_LAST[row] * shares + (lay ^ 2))
        for row in range(len(BLOCK_LAST))
        for lay in range(shares)
    ]
    other = lax.ppermute(other, ("rows", "layer"), pairs)
    mine = back(mine, BLOCK_LAST)
    out_shape = [jax.ShapeDtypeStruct((STEPS,) + own.shape, jnp.float32)]
    (scores,) = small_call(assemble_kernel, out_shape, own, first, second)
    return finish(mine, other, scores)


def around_ring(documents, conditioned, query_ids):
    n_rows, shares = lax.axis_size("rows"), lax.axis_size("layer")
    rows, docs = conditioned.shape[0], documents.shape[0]
    result = []
    for step in range(STEPS):
        behind = [(row, (row - step) % n_rows) for row in range(n_rows)]
        block = lax.ppermute(documents, "rows", behind) if step else documents

        def ahead(row, step=step):
            return lax.rem(row + step, n_rows)

        kernel = functools.partial(turned_kernel, shares, ahead)
        out_shape = [jax.ShapeDtypeStruct((rows // shares, docs), jnp.bfloat16)] * shares
        scratch = [pltpu.VMEM((rows, docs), jnp.float32)]
        total = direct_sum(scoring(kernel, out_shape, conditioned, query_ids, block, (), scratch))
        onward = [(row, (row + step) % n_rows) for row in range(n_rows)]
        result.append(lax.ppermute(total, "rows", onward) if step else total)
    return jnp.stack(result)


def local(train_grads, query_grads, eigenbases, eigenvalues, layer_offsets, query_doc_ids):
    conditioned = prepare(query_grads, eigenbases, eigenvalues, layer_offsets)
    on_line = lax.axis_size("rows") == 4 and lax.axis_size("layer") == 4
    plan = along_line if on_line else around_ring
    return plan(train_grads, conditioned, query_doc_ids[:, None])


def solution(mesh):
    in_specs = (
        P(("group", "rows"), "layer"),
        P(("group", "rows"), "layer"),
        P("layer", None, None),
        P("layer", None),
        P("layer"),
        P(("group", "rows")),
    )
    out_specs = P(None, "layer", ("group", "rows"))
    return jax.shard_map(local, mesh=mesh, in_specs=in_specs, out_specs=out_specs, check_vma=False)
```

```python
import functools

import jax
import jax.numpy as jnp
from jax import lax
from jax.experimental import pallas as pl
from jax.experimental.pallas import tpu as pltpu
from jax.sharding import PartitionSpec as P

LDIM = 512
LAY_DEV = 4
STEPS = 4
DAMPING = 0.05
NT = (((1,), (1,)), ((), ()))
MIB = 1024 * 1024


def layer_index():
    return lax.axis_index("layer").astype(jnp.int32)


def row_index():
    return lax.axis_index("rows").astype(jnp.int32)


def prepare_kernel(
    offsets, queries_hbm, bases_hbm, values_hbm, conditioned_ref, queries, bases, values, arrived
):
    copies = [pltpu.make_async_copy(values_hbm, values, arrived.at[0])]
    for layer in range(LAY_DEV):
        columns = queries_hbm.at[:, layer * LDIM : (layer + 1) * LDIM]
        copies.append(pltpu.make_async_copy(columns, queries.at[layer], arrived.at[1 + 2 * layer]))
        copies.append(pltpu.make_async_copy(bases_hbm.at[layer], bases.at[layer], arrived.at[2 + 2 * layer]))
    for copy in copies:
        copy.start()
    base_column = layer_index() * (LAY_DEV * LDIM)
    copies[0].wait()
    for layer in range(LAY_DEV):
        copies[1 + 2 * layer].wait()
        copies[2 + 2 * layer].wait()
        basis = bases[layer]
        projected = jnp.dot(queries[layer], basis, preferred_element_type=jnp.float32)
        scaled = (projected / (values[layer : layer + 1, :] + DAMPING)).astype(jnp.bfloat16)
        restored = lax.dot_general(scaled, basis, NT, preferred_element_type=jnp.float32)
        first = pl.multiple_of(offsets[layer] - base_column, LDIM)
        conditioned_ref[:, pl.ds(first, LDIM)] = restored.astype(jnp.bfloat16)


def prepare(queries, bases, values, offsets):
    rows, dims = queries.shape
    hbm = pl.BlockSpec(memory_space=pltpu.HBM)
    return pl.pallas_call(
        prepare_kernel,
        out_shape=jax.ShapeDtypeStruct((rows, dims), jnp.bfloat16),
        in_specs=[pl.BlockSpec(memory_space=pltpu.SMEM), hbm, hbm, hbm],
        out_specs=pl.BlockSpec(memory_space=pltpu.VMEM),
        scratch_shapes=[
            pltpu.VMEM((LAY_DEV, rows, LDIM), jnp.bfloat16),
            pltpu.VMEM(bases.shape, jnp.bfloat16),
            pltpu.VMEM(values.shape, jnp.float32),
            pltpu.SemaphoreType.DMA((1 + 2 * LAY_DEV,)),
        ],
        compiler_params=pltpu.CompilerParams(vmem_limit_bytes=62 * MIB),
        cost_estimate=pl.CostEstimate(
            flops=4 * rows * dims * LDIM, bytes_accessed=6 * MIB, transcendentals=0
        ),
    )(offsets, queries, bases, values)


def masked_tile(queries, documents, query_ids, block):
    tile = lax.dot_general(queries, documents, NT, preferred_element_type=jnp.float32)
    doc_ids = block * tile.shape[1] + lax.broadcasted_iota(jnp.int32, tile.shape, 1)
    return jnp.where(query_ids == doc_ids, 0.0, tile)


def scoring(kernel, out_shape, conditioned, query_ids, documents, extra=(), scratch=()):
    dims = conditioned.shape[1]
    docs = documents.shape[0]
    rows = sum(shape.shape[0] for shape in out_shape)
    vmem = pl.BlockSpec(memory_space=pltpu.VMEM)
    return pl.pallas_call(
        kernel,
        out_shape=out_shape,
        in_specs=[vmem] * (3 + len(extra)),
        out_specs=[vmem] * len(out_shape),
        scratch_shapes=scratch,
        compiler_params=pltpu.CompilerParams(vmem_limit_bytes=12 * MIB),
        cost_estimate=pl.CostEstimate(
            flops=2 * rows * docs * dims, bytes_accessed=2 * dims * (rows + docs), transcendentals=0
        ),
    )(conditioned, query_ids, documents, *extra)


def turned_kernel(shares, block_of, queries_ref, ids_ref, documents_ref, *refs):
    *out_refs, held = refs
    held[...] = masked_tile(queries_ref[...], documents_ref[...], ids_ref[...], block_of(row_index()))
    for turn, out_ref in enumerate(out_refs):
        share_rows = out_ref.shape[0]
        first = pl.multiple_of(lax.rem(layer_index() + turn, shares) * share_rows, share_rows)
        out_ref[...] = held[pl.ds(first, share_rows), :].astype(jnp.bfloat16)


def half_shares(share_rows, kept):
    core = lax.rem(layer_index(), 2)
    core = core if kept else 1 - core
    return [pl.multiple_of((2 * chip + core) * share_rows, share_rows) for chip in range(2)]


def halves_kernel(block_of, queries_ref, ids_ref, documents_ref, *refs):
    front_refs, out_refs, held = refs[:-3], refs[-3:-1], refs[-1]
    held[...] = masked_tile(queries_ref[...], documents_ref[...], ids_ref[...], block_of(row_index()))
    docs = documents_ref.shape[0]
    rows, width = out_refs[0].shape
    for side, kept in enumerate((True, False)):
        if front_refs:
            out_refs[side][:, : width - docs] = front_refs[side][...]
        for chip, first in enumerate(half_shares(rows // 2, kept)):
            spot = slice(chip * (rows // 2), (chip + 1) * (rows // 2))
            out_refs[side][spot, width - docs :] = held[pl.ds(first, rows // 2), :]


def half_kernel(block_of, kept, queries_ref, ids_ref, documents_ref, out_ref):
    share_rows = out_ref.shape[0] // 2
    firsts = half_shares(share_rows, kept)
    queries = jnp.concatenate([queries_ref[pl.ds(first, share_rows), :] for first in firsts], axis=0)
    query_ids = jnp.concatenate([ids_ref[pl.ds(first, share_rows), :] for first in firsts], axis=0)
    out_ref[...] = masked_tile(queries, documents_ref[...], query_ids, block_of(row_index()))


def total_of(refs):
    total = refs[0][...].astype(jnp.float32)
    for ref in refs[1:]:
        total += ref[...].astype(jnp.float32)
    return total


def sum_kernel(*refs):
    refs[-1][...] = total_of(refs[:-1])


def small_call(kernel, out_shape, *args):
    vmem = pl.BlockSpec(memory_space=pltpu.VMEM)
    return pl.pallas_call(
        kernel,
        out_shape=out_shape,
        in_specs=[vmem] * len(args),
        out_specs=[vmem] * len(out_shape),
        compiler_params=pltpu.CompilerParams(vmem_limit_bytes=4 * MIB),
    )(*args)


def direct_sum(tiles):
    shares = len(tiles)
    arrived = [tiles[0]]
    for turn in range(1, shares):
        pairs = [(lay, (lay + turn) % shares) for lay in range(shares)]
        arrived.append(lax.ppermute(tiles[turn], "layer", pairs))
    (total,) = small_call(sum_kernel, [jax.ShapeDtypeStruct(tiles[0].shape, jnp.float32)], *arrived)
    return total


def core_sum_kernel(kept_ref, arrived_ref, mine_ref, other_ref):
    rows = mine_ref.shape[0]
    chip = lax.div(layer_index(), 2)
    mine = pl.ds(pl.multiple_of(chip * rows, rows), rows)
    other = pl.ds(pl.multiple_of((1 - chip) * rows, rows), rows)
    mine_ref[...] = (kept_ref[mine, :] + arrived_ref[mine, :]).astype(mine_ref.dtype)
    other_ref[...] = (kept_ref[other, :] + arrived_ref[other, :]).astype(other_ref.dtype)


def chip_sum_kernel(mine_ref, arrived_ref, *out_refs):
    docs = out_refs[0].shape[1]
    for spot, out_ref in enumerate(out_refs):
        columns = slice(spot * docs, (spot + 1) * docs)
        total = mine_ref[:, columns] + arrived_ref[:, columns].astype(jnp.float32)
        out_ref[...] = total.astype(out_ref.dtype)


def swap(value, distance):
    count = lax.axis_size("layer")
    return lax.ppermute(value, "layer", [(lay, lay ^ distance) for lay in range(count)])


def core_sum(kept, arrived, mine_type):
    rows, width = kept.shape[0] // 2, kept.shape[1]
    out_shape = [jax.ShapeDtypeStruct((rows, width), out_type) for out_type in (mine_type, jnp.bfloat16)]
    return small_call(core_sum_kernel, out_shape, kept, arrived)


def layer_sum(kept, sent, out_types):
    mine, other = core_sum(kept, swap(sent, 1), jnp.float32)
    rows, docs = mine.shape[0], mine.shape[1] // len(out_types)
    out_shape = [jax.ShapeDtypeStruct((rows, docs), out_type) for out_type in out_types]
    return small_call(chip_sum_kernel, out_shape, mine, swap(other, 2))


ROUND_ONE = ((0, 2), (2, 3), (3, 1), (1, 0))
ROUND_TWO = ((0, 1), (1, 3), (3, 2), (2, 0))
BLOCK_ONE = (1, 3, 0, 2)
BLOCK_TWO = (2, 0, 3, 1)
BLOCK_LAST = (3, 2, 1, 0)


def pick(table):
    def entry(row):
        value = jnp.int32(table[0])
        for index in range(1, len(table)):
            value = jnp.where(row == index, jnp.int32(table[index]), value)
        return value

    return entry


def step_of(table):
    return pick([(block - table.index(block)) % STEPS for block in range(STEPS)])


def assemble_kernel(own_ref, first_ref, second_ref, out_ref):
    out_ref[0] = own_ref[...]
    for ref, table in ((first_ref, BLOCK_ONE), (second_ref, BLOCK_TWO)):
        out_ref[step_of(table)(row_index())] = ref[...].astype(jnp.float32)


def own_side():
    row = row_index()
    return jnp.where(row < pick(BLOCK_LAST)(row), 0, 1)


def pair_sum_kernel(kept_ref, arrived_ref, out_ref):
    side = own_side()
    rows = out_ref.shape[2]
    out_ref[side] = jnp.zeros(out_ref.shape[1:], out_ref.dtype)
    for chip in range(2):
        share = slice(chip * rows, (chip + 1) * rows)
        out_ref[1 - side, chip] = (kept_ref[share, :] + arrived_ref[share, :]).astype(out_ref.dtype)


def finish_kernel(pair_ref, scores_hbm, out_hbm, total, copied):
    del scores_hbm
    side = 1 - own_side()
    total[...] = total_of([pair_ref.at[side, chip] for chip in range(2)])
    copy = pltpu.make_async_copy(total, out_hbm.at[step_of(BLOCK_LAST)(row_index())], copied)
    copy.start()
    copy.wait()


def finish(pair, scores):
    hbm = pl.BlockSpec(memory_space=pltpu.HBM)
    vmem = pl.BlockSpec(memory_space=pltpu.VMEM)
    return pl.pallas_call(
        finish_kernel,
        out_shape=jax.ShapeDtypeStruct(scores.shape, scores.dtype),
        in_specs=[vmem, hbm],
        out_specs=hbm,
        scratch_shapes=[pltpu.VMEM(pair.shape[2:], jnp.float32), pltpu.SemaphoreType.DMA],
        input_output_aliases={1: 0},
        compiler_params=pltpu.CompilerParams(vmem_limit_bytes=4 * MIB),
    )(pair, scores)


def along_line(documents, conditioned, query_ids):
    docs = documents.shape[0]
    half = (conditioned.shape[0] // 2, docs)

    def halves(block, block_of, front=()):
        width = docs * (1 + bool(front))
        out_shape = [jax.ShapeDtypeStruct((half[0], width), jnp.float32)] * 2
        scratch = [pltpu.VMEM((2 * half[0], docs), jnp.float32)]
        kernel = functools.partial(halves_kernel, block_of)
        return scoring(kernel, out_shape, conditioned, query_ids, block, front, scratch)

    def one_half(block, block_of, kept):
        kernel = functools.partial(half_kernel, block_of, kept)
        out_shape = [jax.ShapeDtypeStruct(half, jnp.float32)]
        return scoring(kernel, out_shape, conditioned, query_ids, block)[0]

    def back(total, table):
        return lax.ppermute(total, "rows", tuple(enumerate(table)))

    one = lax.ppermute(documents, "rows", ROUND_ONE)
    later, conditioned = lax.optimization_barrier((documents, conditioned))
    two = lax.ppermute(later, "rows", ROUND_TWO)
    own = halves(later, lambda row: row)
    one, own = lax.optimization_barrier((one, own))
    three = lax.ppermute(one, "rows", ROUND_ONE)

    own, first = layer_sum(*halves(one, pick(BLOCK_ONE), own), (jnp.float32, jnp.bfloat16))
    two, first = lax.optimization_barrier((two, first))
    first = back(first, BLOCK_ONE)
    (second,) = layer_sum(*halves(two, pick(BLOCK_TWO)), (jnp.bfloat16,))
    second = back(second, BLOCK_TWO)
    three, first, second = lax.optimization_barrier((three, first, second))

    arrived = swap(one_half(three, pick(BLOCK_LAST), False), 1)
    kept = one_half(three, pick(BLOCK_LAST), True)
    pair_shape = (2, 2) + own.shape
    (pair,) = small_call(pair_sum_kernel, [jax.ShapeDtypeStruct(pair_shape, jnp.bfloat16)], kept, arrived)
    shares = lax.axis_size("layer")
    groups = [
        [row * shares + 2 * chip + core for row in (low, BLOCK_LAST[low]) for chip in range(2)]
        for low in range(STEPS // 2)
        for core in range(2)
    ]
    blocks = pair.reshape((4,) + own.shape)
    blocks = lax.all_to_all(blocks, ("rows", "layer"), 0, 0, axis_index_groups=groups, tiled=True)
    out_shape = [jax.ShapeDtypeStruct((STEPS,) + own.shape, jnp.float32)]
    (scores,) = small_call(assemble_kernel, out_shape, own, first, second)
    return finish(blocks.reshape(pair_shape), scores)


def around_ring(documents, conditioned, query_ids):
    n_rows, shares = lax.axis_size("rows"), lax.axis_size("layer")
    rows, docs = conditioned.shape[0], documents.shape[0]
    result = []
    for step in range(STEPS):
        behind = [(row, (row - step) % n_rows) for row in range(n_rows)]
        block = lax.ppermute(documents, "rows", behind) if step else documents

        def ahead(row, step=step):
            return lax.rem(row + step, n_rows)

        kernel = functools.partial(turned_kernel, shares, ahead)
        out_shape = [jax.ShapeDtypeStruct((rows // shares, docs), jnp.bfloat16)] * shares
        scratch = [pltpu.VMEM((rows, docs), jnp.float32)]
        total = direct_sum(scoring(kernel, out_shape, conditioned, query_ids, block, (), scratch))
        onward = [(row, (row + step) % n_rows) for row in range(n_rows)]
        result.append(lax.ppermute(total, "rows", onward) if step else total)
    return jnp.stack(result)


def local(train_grads, query_grads, eigenbases, eigenvalues, layer_offsets, query_doc_ids):
    conditioned = prepare(query_grads, eigenbases, eigenvalues, layer_offsets)
    on_line = lax.axis_size("rows") == 4 and lax.axis_size("layer") == 4
    plan = along_line if on_line else around_ring
    return plan(train_grads, conditioned, query_doc_ids[:, None])


def solution(mesh):
    in_specs = (
        P(("group", "rows"), "layer"),
        P(("group", "rows"), "layer"),
        P("layer", None, None),
        P("layer", None),
        P("layer"),
        P(("group", "rows")),
    )
    out_specs = P(None, "layer", ("group", "rows"))
    return jax.shard_map(local, mesh=mesh, in_specs=in_specs, out_specs=out_specs, check_vma=False)
```

```python
import functools

import jax
import jax.numpy as jnp
from jax import lax
from jax.experimental import pallas as pl
from jax.experimental.pallas import tpu as pltpu
from jax.sharding import PartitionSpec as P

LDIM = 512
LAY_DEV = 4
STEPS = 4
DAMPING = 0.05
NT = (((1,), (1,)), ((), ()))
MIB = 1024 * 1024


def layer_index():
    return lax.axis_index("layer").astype(jnp.int32)


def row_index():
    return lax.axis_index("rows").astype(jnp.int32)


def prepare_kernel(
    offsets, queries_hbm, bases_hbm, values_hbm, conditioned_ref, queries, bases, values, arrived
):
    copies = [pltpu.make_async_copy(values_hbm, values, arrived.at[0])]
    for layer in range(LAY_DEV):
        columns = queries_hbm.at[:, layer * LDIM : (layer + 1) * LDIM]
        copies.append(pltpu.make_async_copy(columns, queries.at[layer], arrived.at[1 + 2 * layer]))
        copies.append(pltpu.make_async_copy(bases_hbm.at[layer], bases.at[layer], arrived.at[2 + 2 * layer]))
    for copy in copies:
        copy.start()
    base_column = layer_index() * (LAY_DEV * LDIM)
    copies[0].wait()
    for layer in range(LAY_DEV):
        copies[1 + 2 * layer].wait()
        copies[2 + 2 * layer].wait()
        basis = bases[layer]
        projected = jnp.dot(queries[layer], basis, preferred_element_type=jnp.float32)
        scaled = (projected / (values[layer : layer + 1, :] + DAMPING)).astype(jnp.bfloat16)
        restored = lax.dot_general(scaled, basis, NT, preferred_element_type=jnp.float32)
        first = pl.multiple_of(offsets[layer] - base_column, LDIM)
        conditioned_ref[:, pl.ds(first, LDIM)] = restored.astype(jnp.bfloat16)


def prepare(queries, bases, values, offsets):
    rows, dims = queries.shape
    hbm = pl.BlockSpec(memory_space=pltpu.HBM)
    return pl.pallas_call(
        prepare_kernel,
        out_shape=jax.ShapeDtypeStruct((rows, dims), jnp.bfloat16),
        in_specs=[pl.BlockSpec(memory_space=pltpu.SMEM), hbm, hbm, hbm],
        out_specs=pl.BlockSpec(memory_space=pltpu.VMEM),
        scratch_shapes=[
            pltpu.VMEM((LAY_DEV, rows, LDIM), jnp.bfloat16),
            pltpu.VMEM(bases.shape, jnp.bfloat16),
            pltpu.VMEM(values.shape, jnp.float32),
            pltpu.SemaphoreType.DMA((1 + 2 * LAY_DEV,)),
        ],
        compiler_params=pltpu.CompilerParams(vmem_limit_bytes=62 * MIB),
        cost_estimate=pl.CostEstimate(
            flops=4 * rows * dims * LDIM, bytes_accessed=6 * MIB, transcendentals=0
        ),
    )(offsets, queries, bases, values)


def masked_tile(queries, documents, query_ids, block):
    tile = lax.dot_general(queries, documents, NT, preferred_element_type=jnp.float32)
    doc_ids = block * tile.shape[1] + lax.broadcasted_iota(jnp.int32, tile.shape, 1)
    return jnp.where(query_ids == doc_ids, 0.0, tile)


def scoring(kernel, out_shape, conditioned, query_ids, documents, extra=(), scratch=()):
    dims = conditioned.shape[1]
    docs = documents.shape[0]
    rows = sum(shape.shape[0] for shape in out_shape)
    vmem = pl.BlockSpec(memory_space=pltpu.VMEM)
    return pl.pallas_call(
        kernel,
        out_shape=out_shape,
        in_specs=[vmem] * (3 + len(extra)),
        out_specs=[vmem] * len(out_shape),
        scratch_shapes=scratch,
        compiler_params=pltpu.CompilerParams(vmem_limit_bytes=12 * MIB),
        cost_estimate=pl.CostEstimate(
            flops=2 * rows * docs * dims, bytes_accessed=2 * dims * (rows + docs), transcendentals=0
        ),
    )(conditioned, query_ids, documents, *extra)


def turned_kernel(shares, block_of, queries_ref, ids_ref, documents_ref, *refs):
    *out_refs, held = refs
    held[...] = masked_tile(queries_ref[...], documents_ref[...], ids_ref[...], block_of(row_index()))
    for turn, out_ref in enumerate(out_refs):
        share_rows = out_ref.shape[0]
        first = pl.multiple_of(lax.rem(layer_index() + turn, shares) * share_rows, share_rows)
        out_ref[...] = held[pl.ds(first, share_rows), :].astype(jnp.bfloat16)


def half_shares(share_rows, kept):
    core = lax.rem(layer_index(), 2)
    core = core if kept else 1 - core
    return [pl.multiple_of((2 * chip + core) * share_rows, share_rows) for chip in range(2)]


def halves_kernel(block_of, queries_ref, ids_ref, documents_ref, *refs):
    front_refs, out_refs, held = refs[:-3], refs[-3:-1], refs[-1]
    held[...] = masked_tile(queries_ref[...], documents_ref[...], ids_ref[...], block_of(row_index()))
    docs = documents_ref.shape[0]
    rows, width = out_refs[0].shape
    for side, kept in enumerate((True, False)):
        if front_refs:
            out_refs[side][:, : width - docs] = front_refs[side][...]
        for chip, first in enumerate(half_shares(rows // 2, kept)):
            spot = slice(chip * (rows // 2), (chip + 1) * (rows // 2))
            out_refs[side][spot, width - docs :] = held[pl.ds(first, rows // 2), :]


def target_chip():
    chip, core = lax.div(layer_index(), 2), lax.rem(layer_index(), 2)
    return jnp.where(chip == core, 0, 1)


def half_kernel(block_of, kept, queries_ref, ids_ref, documents_ref, out_ref):
    rows = out_ref.shape[0]
    chip = target_chip() if kept else 1 - target_chip()
    spot = pl.ds(pl.multiple_of(chip * rows, rows), rows)
    out_ref[...] = masked_tile(queries_ref[spot, :], documents_ref[...], ids_ref[spot, :], block_of(row_index()))


def total_of(refs):
    total = refs[0][...].astype(jnp.float32)
    for ref in refs[1:]:
        total += ref[...].astype(jnp.float32)
    return total


def sum_kernel(*refs):
    refs[-1][...] = total_of(refs[:-1]).astype(refs[-1].dtype)


def small_call(kernel, out_shape, *args):
    vmem = pl.BlockSpec(memory_space=pltpu.VMEM)
    return pl.pallas_call(
        kernel,
        out_shape=out_shape,
        in_specs=[vmem] * len(args),
        out_specs=[vmem] * len(out_shape),
        compiler_params=pltpu.CompilerParams(vmem_limit_bytes=4 * MIB),
    )(*args)


def direct_sum(tiles):
    shares = len(tiles)
    arrived = [tiles[0]]
    for turn in range(1, shares):
        pairs = [(lay, (lay + turn) % shares) for lay in range(shares)]
        arrived.append(lax.ppermute(tiles[turn], "layer", pairs))
    (total,) = small_call(sum_kernel, [jax.ShapeDtypeStruct(tiles[0].shape, jnp.float32)], *arrived)
    return total


def core_sum_kernel(kept_ref, arrived_ref, mine_ref, other_ref):
    rows = mine_ref.shape[0]
    chip = lax.div(layer_index(), 2)
    mine = pl.ds(pl.multiple_of(chip * rows, rows), rows)
    other = pl.ds(pl.multiple_of((1 - chip) * rows, rows), rows)
    mine_ref[...] = (kept_ref[mine, :] + arrived_ref[mine, :]).astype(mine_ref.dtype)
    other_ref[...] = (kept_ref[other, :] + arrived_ref[other, :]).astype(other_ref.dtype)


def chip_sum_kernel(mine_ref, arrived_ref, *out_refs):
    docs = out_refs[0].shape[1]
    for spot, out_ref in enumerate(out_refs):
        columns = slice(spot * docs, (spot + 1) * docs)
        total = mine_ref[:, columns] + arrived_ref[:, columns].astype(jnp.float32)
        out_ref[...] = total.astype(out_ref.dtype)


def swap(value, distance):
    count = lax.axis_size("layer")
    return lax.ppermute(value, "layer", [(lay, lay ^ distance) for lay in range(count)])


def core_sum(kept, arrived, mine_type):
    rows, width = kept.shape[0] // 2, kept.shape[1]
    out_shape = [jax.ShapeDtypeStruct((rows, width), out_type) for out_type in (mine_type, jnp.bfloat16)]
    return small_call(core_sum_kernel, out_shape, kept, arrived)


def layer_sum(kept, sent, out_types):
    mine, other = core_sum(kept, swap(sent, 1), jnp.float32)
    rows, docs = mine.shape[0], mine.shape[1] // len(out_types)
    out_shape = [jax.ShapeDtypeStruct((rows, docs), out_type) for out_type in out_types]
    return small_call(chip_sum_kernel, out_shape, mine, swap(other, 2))


ROUND_ONE = ((0, 2), (2, 3), (3, 1), (1, 0))
ROUND_TWO = ((0, 1), (1, 3), (3, 2), (2, 0))
BLOCK_ONE = (1, 3, 0, 2)
BLOCK_TWO = (2, 0, 3, 1)
BLOCK_LAST = (3, 2, 1, 0)


def pick(table):
    def entry(row):
        value = jnp.int32(table[0])
        for index in range(1, len(table)):
            value = jnp.where(row == index, jnp.int32(table[index]), value)
        return value

    return entry


def step_of(table):
    return pick([(block - table.index(block)) % STEPS for block in range(STEPS)])


def assemble_kernel(own_ref, first_ref, second_ref, out_ref):
    out_ref[0] = own_ref[...]
    for ref, table in ((first_ref, BLOCK_ONE), (second_ref, BLOCK_TWO)):
        out_ref[step_of(table)(row_index())] = ref[...].astype(jnp.float32)


def finish_kernel(mine_ref, arrived_ref, scores_hbm, out_hbm, total, copied):
    del scores_hbm
    rows = total.shape[0]
    share = pl.ds(pl.multiple_of(lax.rem(layer_index(), 2) * rows, rows), rows)
    total[...] = mine_ref[share, :].astype(jnp.float32) + arrived_ref[share, :].astype(jnp.float32)
    copy = pltpu.make_async_copy(total, out_hbm.at[step_of(BLOCK_LAST)(row_index())], copied)
    copy.start()
    copy.wait()


def finish(mine, arrived, scores):
    hbm = pl.BlockSpec(memory_space=pltpu.HBM)
    vmem = pl.BlockSpec(memory_space=pltpu.VMEM)
    return pl.pallas_call(
        finish_kernel,
        out_shape=jax.ShapeDtypeStruct(scores.shape, scores.dtype),
        in_specs=[vmem, vmem, hbm],
        out_specs=hbm,
        scratch_shapes=[pltpu.VMEM(scores.shape[1:], jnp.float32), pltpu.SemaphoreType.DMA],
        input_output_aliases={2: 0},
        compiler_params=pltpu.CompilerParams(vmem_limit_bytes=4 * MIB),
    )(mine, arrived, scores)


def along_line(documents, conditioned, query_ids):
    docs = documents.shape[0]
    half = (conditioned.shape[0] // 2, docs)

    def halves(block, block_of, front=()):
        width = docs * (1 + bool(front))
        out_shape = [jax.ShapeDtypeStruct((half[0], width), jnp.float32)] * 2
        scratch = [pltpu.VMEM((2 * half[0], docs), jnp.float32)]
        kernel = functools.partial(halves_kernel, block_of)
        return scoring(kernel, out_shape, conditioned, query_ids, block, front, scratch)

    def one_half(block, block_of, kept):
        kernel = functools.partial(half_kernel, block_of, kept)
        out_shape = [jax.ShapeDtypeStruct(half, jnp.float32)]
        return scoring(kernel, out_shape, conditioned, query_ids, block)[0]

    def back(total, table):
        return lax.ppermute(total, "rows", tuple(enumerate(table)))

    one = lax.ppermute(documents, "rows", ROUND_ONE)
    later, conditioned = lax.optimization_barrier((documents, conditioned))
    two = lax.ppermute(later, "rows", ROUND_TWO)
    own = halves(later, lambda row: row)
    one, own = lax.optimization_barrier((one, own))
    three = lax.ppermute(one, "rows", ROUND_ONE)

    own, first = layer_sum(*halves(one, pick(BLOCK_ONE), own), (jnp.float32, jnp.bfloat16))
    two, first = lax.optimization_barrier((two, first))
    first = back(first, BLOCK_ONE)
    (second,) = layer_sum(*halves(two, pick(BLOCK_TWO)), (jnp.bfloat16,))
    second = back(second, BLOCK_TWO)
    three, first, second = lax.optimization_barrier((three, first, second))

    arrived = swap(one_half(three, pick(BLOCK_LAST), False), 1)
    kept = one_half(three, pick(BLOCK_LAST), True)
    (both,) = small_call(sum_kernel, [jax.ShapeDtypeStruct(half, jnp.bfloat16)], kept, arrived)
    shares = lax.axis_size("layer")
    pairs = [
        (row * shares + lay, BLOCK_LAST[row] * shares + 2 * ((lay // 2) ^ (lay % 2)) + lay % 2)
        for row in range(len(BLOCK_LAST))
        for lay in range(shares)
    ]
    mine = lax.ppermute(both, ("rows", "layer"), pairs)
    out_shape = [jax.ShapeDtypeStruct((STEPS,) + own.shape, jnp.float32)]
    (scores,) = small_call(assemble_kernel, out_shape, own, first, second)
    return finish(mine, swap(mine, 1), scores)


def around_ring(documents, conditioned, query_ids):
    n_rows, shares = lax.axis_size("rows"), lax.axis_size("layer")
    rows, docs = conditioned.shape[0], documents.shape[0]
    result = []
    for step in range(STEPS):
        behind = [(row, (row - step) % n_rows) for row in range(n_rows)]
        block = lax.ppermute(documents, "rows", behind) if step else documents

        def ahead(row, step=step):
            return lax.rem(row + step, n_rows)

        kernel = functools.partial(turned_kernel, shares, ahead)
        out_shape = [jax.ShapeDtypeStruct((rows // shares, docs), jnp.bfloat16)] * shares
        scratch = [pltpu.VMEM((rows, docs), jnp.float32)]
        total = direct_sum(scoring(kernel, out_shape, conditioned, query_ids, block, (), scratch))
        onward = [(row, (row + step) % n_rows) for row in range(n_rows)]
        result.append(lax.ppermute(total, "rows", onward) if step else total)
    return jnp.stack(result)


def local(train_grads, query_grads, eigenbases, eigenvalues, layer_offsets, query_doc_ids):
    conditioned = prepare(query_grads, eigenbases, eigenvalues, layer_offsets)
    on_line = lax.axis_size("rows") == 4 and lax.axis_size("layer") == 4
    plan = along_line if on_line else around_ring
    return plan(train_grads, conditioned, query_doc_ids[:, None])


def solution(mesh):
    in_specs = (
        P(("group", "rows"), "layer"),
        P(("group", "rows"), "layer"),
        P("layer", None, None),
        P("layer", None),
        P("layer"),
        P(("group", "rows")),
    )
    out_specs = P(None, "layer", ("group", "rows"))
    return jax.shard_map(local, mesh=mesh, in_specs=in_specs, out_specs=out_specs, check_vma=False)
```

```python
import functools

import jax
import jax.numpy as jnp
from jax import lax
from jax.experimental import pallas as pl
from jax.experimental.pallas import tpu as pltpu
from jax.sharding import PartitionSpec as P

LDIM = 512
LAY_DEV = 4
STEPS = 4
DAMPING = 0.05
NT = (((1,), (1,)), ((), ()))
MIB = 1024 * 1024


def layer_index():
    return lax.axis_index("layer").astype(jnp.int32)


def row_index():
    return lax.axis_index("rows").astype(jnp.int32)


def prepare_kernel(
    offsets, queries_hbm, bases_hbm, values_hbm, conditioned_ref, queries, bases, values, arrived
):
    copies = [pltpu.make_async_copy(values_hbm, values, arrived.at[0])]
    for layer in range(LAY_DEV):
        columns = queries_hbm.at[:, layer * LDIM : (layer + 1) * LDIM]
        copies.append(pltpu.make_async_copy(columns, queries.at[layer], arrived.at[1 + 2 * layer]))
        copies.append(pltpu.make_async_copy(bases_hbm.at[layer], bases.at[layer], arrived.at[2 + 2 * layer]))
    for copy in copies:
        copy.start()
    base_column = layer_index() * (LAY_DEV * LDIM)
    copies[0].wait()
    for layer in range(LAY_DEV):
        copies[1 + 2 * layer].wait()
        copies[2 + 2 * layer].wait()
        basis = bases[layer]
        projected = jnp.dot(queries[layer], basis, preferred_element_type=jnp.float32)
        scaled = (projected / (values[layer : layer + 1, :] + DAMPING)).astype(jnp.bfloat16)
        restored = lax.dot_general(scaled, basis, NT, preferred_element_type=jnp.float32)
        first = pl.multiple_of(offsets[layer] - base_column, LDIM)
        conditioned_ref[:, pl.ds(first, LDIM)] = restored.astype(jnp.bfloat16)


def prepare(queries, bases, values, offsets):
    rows, dims = queries.shape
    hbm = pl.BlockSpec(memory_space=pltpu.HBM)
    return pl.pallas_call(
        prepare_kernel,
        out_shape=jax.ShapeDtypeStruct((rows, dims), jnp.bfloat16),
        in_specs=[pl.BlockSpec(memory_space=pltpu.SMEM), hbm, hbm, hbm],
        out_specs=pl.BlockSpec(memory_space=pltpu.VMEM),
        scratch_shapes=[
            pltpu.VMEM((LAY_DEV, rows, LDIM), jnp.bfloat16),
            pltpu.VMEM(bases.shape, jnp.bfloat16),
            pltpu.VMEM(values.shape, jnp.float32),
            pltpu.SemaphoreType.DMA((1 + 2 * LAY_DEV,)),
        ],
        compiler_params=pltpu.CompilerParams(vmem_limit_bytes=62 * MIB),
        cost_estimate=pl.CostEstimate(
            flops=4 * rows * dims * LDIM, bytes_accessed=6 * MIB, transcendentals=0
        ),
    )(offsets, queries, bases, values)


def masked_tile(queries, documents, query_ids, block):
    tile = lax.dot_general(queries, documents, NT, preferred_element_type=jnp.float32)
    doc_ids = block * tile.shape[1] + lax.broadcasted_iota(jnp.int32, tile.shape, 1)
    return jnp.where(query_ids == doc_ids, 0.0, tile)


def scoring(kernel, out_shape, conditioned, query_ids, documents, extra=(), scratch=()):
    dims = conditioned.shape[1]
    docs = documents.shape[0]
    rows = sum(shape.shape[0] for shape in out_shape)
    vmem = pl.BlockSpec(memory_space=pltpu.VMEM)
    return pl.pallas_call(
        kernel,
        out_shape=out_shape,
        in_specs=[vmem] * (3 + len(extra)),
        out_specs=[vmem] * len(out_shape),
        scratch_shapes=scratch,
        compiler_params=pltpu.CompilerParams(vmem_limit_bytes=12 * MIB),
        cost_estimate=pl.CostEstimate(
            flops=2 * rows * docs * dims, bytes_accessed=2 * dims * (rows + docs), transcendentals=0
        ),
    )(conditioned, query_ids, documents, *extra)


def turned_kernel(shares, block_of, queries_ref, ids_ref, documents_ref, *refs):
    *out_refs, held = refs
    held[...] = masked_tile(queries_ref[...], documents_ref[...], ids_ref[...], block_of(row_index()))
    for turn, out_ref in enumerate(out_refs):
        share_rows = out_ref.shape[0]
        first = pl.multiple_of(lax.rem(layer_index() + turn, shares) * share_rows, share_rows)
        out_ref[...] = held[pl.ds(first, share_rows), :].astype(jnp.bfloat16)


def half_shares(share_rows, kept):
    core = lax.rem(layer_index(), 2)
    core = core if kept else 1 - core
    return [pl.multiple_of((2 * chip + core) * share_rows, share_rows) for chip in range(2)]


def halves_kernel(block_of, queries_ref, ids_ref, documents_ref, *refs):
    front_refs, out_refs, held = refs[:-3], refs[-3:-1], refs[-1]
    held[...] = masked_tile(queries_ref[...], documents_ref[...], ids_ref[...], block_of(row_index()))
    docs = documents_ref.shape[0]
    rows, width = out_refs[0].shape
    for side, kept in enumerate((True, False)):
        if front_refs:
            out_refs[side][:, : width - docs] = front_refs[side][...]
        for chip, first in enumerate(half_shares(rows // 2, kept)):
            spot = slice(chip * (rows // 2), (chip + 1) * (rows // 2))
            out_refs[side][spot, width - docs :] = held[pl.ds(first, rows // 2), :]


def target_chip():
    chip, core = lax.div(layer_index(), 2), lax.rem(layer_index(), 2)
    return jnp.where(chip == core, 0, 1)


def half_kernel(block_of, kept, queries_ref, ids_ref, documents_ref, out_ref):
    rows = out_ref.shape[0]
    chip = target_chip() if kept else 1 - target_chip()
    spot = pl.ds(pl.multiple_of(chip * rows, rows), rows)
    tile = masked_tile(queries_ref[spot, :], documents_ref[...], ids_ref[spot, :], block_of(row_index()))
    out_ref[...] = tile.astype(out_ref.dtype)


def total_of(refs):
    total = refs[0][...].astype(jnp.float32)
    for ref in refs[1:]:
        total += ref[...].astype(jnp.float32)
    return total


def sum_kernel(*refs):
    refs[-1][...] = total_of(refs[:-1]).astype(refs[-1].dtype)


def small_call(kernel, out_shape, *args):
    vmem = pl.BlockSpec(memory_space=pltpu.VMEM)
    return pl.pallas_call(
        kernel,
        out_shape=out_shape,
        in_specs=[vmem] * len(args),
        out_specs=[vmem] * len(out_shape),
        compiler_params=pltpu.CompilerParams(vmem_limit_bytes=4 * MIB),
    )(*args)


def direct_sum(tiles):
    shares = len(tiles)
    arrived = [tiles[0]]
    for turn in range(1, shares):
        pairs = [(lay, (lay + turn) % shares) for lay in range(shares)]
        arrived.append(lax.ppermute(tiles[turn], "layer", pairs))
    (total,) = small_call(sum_kernel, [jax.ShapeDtypeStruct(tiles[0].shape, jnp.float32)], *arrived)
    return total


def core_sum_kernel(kept_ref, arrived_ref, mine_ref, other_ref):
    rows = mine_ref.shape[0]
    chip = lax.div(layer_index(), 2)
    mine = pl.ds(pl.multiple_of(chip * rows, rows), rows)
    other = pl.ds(pl.multiple_of((1 - chip) * rows, rows), rows)
    mine_ref[...] = (kept_ref[mine, :] + arrived_ref[mine, :]).astype(mine_ref.dtype)
    other_ref[...] = (kept_ref[other, :] + arrived_ref[other, :]).astype(other_ref.dtype)


def chip_sum_kernel(mine_ref, arrived_ref, *out_refs):
    docs = out_refs[0].shape[1]
    for spot, out_ref in enumerate(out_refs):
        columns = slice(spot * docs, (spot + 1) * docs)
        total = mine_ref[:, columns] + arrived_ref[:, columns].astype(jnp.float32)
        out_ref[...] = total.astype(out_ref.dtype)


def swap(value, distance):
    count = lax.axis_size("layer")
    return lax.ppermute(value, "layer", [(lay, lay ^ distance) for lay in range(count)])


def core_sum(kept, arrived, mine_type):
    rows, width = kept.shape[0] // 2, kept.shape[1]
    out_shape = [jax.ShapeDtypeStruct((rows, width), out_type) for out_type in (mine_type, jnp.bfloat16)]
    return small_call(core_sum_kernel, out_shape, kept, arrived)


def layer_sum(kept, sent, out_types):
    mine, other = core_sum(kept, swap(sent, 1), jnp.float32)
    rows, docs = mine.shape[0], mine.shape[1] // len(out_types)
    out_shape = [jax.ShapeDtypeStruct((rows, docs), out_type) for out_type in out_types]
    return small_call(chip_sum_kernel, out_shape, mine, swap(other, 2))


ROUND_ONE = ((0, 2), (2, 3), (3, 1), (1, 0))
ROUND_TWO = ((0, 1), (1, 3), (3, 2), (2, 0))
BLOCK_ONE = (1, 3, 0, 2)
BLOCK_TWO = (2, 0, 3, 1)
BLOCK_LAST = (3, 2, 1, 0)


def pick(table):
    def entry(row):
        value = jnp.int32(table[0])
        for index in range(1, len(table)):
            value = jnp.where(row == index, jnp.int32(table[index]), value)
        return value

    return entry


def step_of(table):
    return pick([(block - table.index(block)) % STEPS for block in range(STEPS)])


def assemble_kernel(own_ref, first_ref, second_ref, out_ref):
    out_ref[0] = own_ref[...]
    for ref, table in ((first_ref, BLOCK_ONE), (second_ref, BLOCK_TWO)):
        out_ref[step_of(table)(row_index())] = ref[...].astype(jnp.float32)


def finish(mine, arrived, scores):
    rows = scores.shape[1]
    first = layer_index() % 2 * rows
    parts = [lax.dynamic_slice_in_dim(part, first, rows, 0).astype(jnp.float32) for part in (mine, arrived)]
    step = step_of(BLOCK_LAST)(row_index())
    return lax.dynamic_update_slice(scores, (parts[0] + parts[1])[None], (step, 0, 0))


def along_line(documents, conditioned, query_ids):
    docs = documents.shape[0]
    half = (conditioned.shape[0] // 2, docs)

    def halves(block, block_of, front=()):
        width = docs * (1 + bool(front))
        out_shape = [jax.ShapeDtypeStruct((half[0], width), jnp.float32)] * 2
        scratch = [pltpu.VMEM((2 * half[0], docs), jnp.float32)]
        kernel = functools.partial(halves_kernel, block_of)
        return scoring(kernel, out_shape, conditioned, query_ids, block, front, scratch)

    def one_half(block, block_of, kept):
        kernel = functools.partial(half_kernel, block_of, kept)
        out_shape = [jax.ShapeDtypeStruct(half, jnp.float32 if kept else jnp.bfloat16)]
        return scoring(kernel, out_shape, conditioned, query_ids, block)[0]

    def back(total, table):
        return lax.ppermute(total, "rows", tuple(enumerate(table)))

    one = lax.ppermute(documents, "rows", ROUND_ONE)
    later, conditioned = lax.optimization_barrier((documents, conditioned))
    two = lax.ppermute(later, "rows", ROUND_TWO)
    own = halves(later, lambda row: row)
    one, own = lax.optimization_barrier((one, own))
    three = lax.ppermute(one, "rows", ROUND_ONE)

    own, first = layer_sum(*halves(one, pick(BLOCK_ONE), own), (jnp.float32, jnp.bfloat16))
    two, first = lax.optimization_barrier((two, first))
    first = back(first, BLOCK_ONE)
    (second,) = layer_sum(*halves(two, pick(BLOCK_TWO)), (jnp.bfloat16,))
    second = back(second, BLOCK_TWO)
    three, first, second = lax.optimization_barrier((three, first, second))

    arrived = swap(one_half(three, pick(BLOCK_LAST), False), 1)
    kept = one_half(three, pick(BLOCK_LAST), True)
    (both,) = small_call(sum_kernel, [jax.ShapeDtypeStruct(half, jnp.bfloat16)], kept, arrived)
    shares = lax.axis_size("layer")
    pairs = [
        (row * shares + lay, BLOCK_LAST[row] * shares + 2 * ((lay // 2) ^ (lay % 2)) + lay % 2)
        for row in range(len(BLOCK_LAST))
        for lay in range(shares)
    ]
    mine = lax.ppermute(both, ("rows", "layer"), pairs)
    out_shape = [jax.ShapeDtypeStruct((STEPS,) + own.shape, jnp.float32)]
    (scores,) = small_call(assemble_kernel, out_shape, own, first, second)
    return finish(mine, swap(mine, 1), scores)


def around_ring(documents, conditioned, query_ids):
    n_rows, shares = lax.axis_size("rows"), lax.axis_size("layer")
    rows, docs = conditioned.shape[0], documents.shape[0]
    result = []
    for step in range(STEPS):
        behind = [(row, (row - step) % n_rows) for row in range(n_rows)]
        block = lax.ppermute(documents, "rows", behind) if step else documents

        def ahead(row, step=step):
            return lax.rem(row + step, n_rows)

        kernel = functools.partial(turned_kernel, shares, ahead)
        out_shape = [jax.ShapeDtypeStruct((rows // shares, docs), jnp.bfloat16)] * shares
        scratch = [pltpu.VMEM((rows, docs), jnp.float32)]
        total = direct_sum(scoring(kernel, out_shape, conditioned, query_ids, block, (), scratch))
        onward = [(row, (row + step) % n_rows) for row in range(n_rows)]
        result.append(lax.ppermute(total, "rows", onward) if step else total)
    return jnp.stack(result)


def local(train_grads, query_grads, eigenbases, eigenvalues, layer_offsets, query_doc_ids):
    conditioned = prepare(query_grads, eigenbases, eigenvalues, layer_offsets)
    on_line = lax.axis_size("rows") == 4 and lax.axis_size("layer") == 4
    plan = along_line if on_line else around_ring
    return plan(train_grads, conditioned, query_doc_ids[:, None])


def solution(mesh):
    in_specs = (
        P(("group", "rows"), "layer"),
        P(("group", "rows"), "layer"),
        P("layer", None, None),
        P("layer", None),
        P("layer"),
        P(("group", "rows")),
    )
    out_specs = P(None, "layer", ("group", "rows"))
    return jax.shard_map(local, mesh=mesh, in_specs=in_specs, out_specs=out_specs, check_vma=False)
```

```python
import functools

import jax
import jax.numpy as jnp
from jax import lax
from jax.experimental import pallas as pl
from jax.experimental.pallas import tpu as pltpu
from jax.sharding import PartitionSpec as P

LDIM = 512
LAY_DEV = 4
STEPS = 4
DAMPING = 0.05
NT = (((1,), (1,)), ((), ()))
MIB = 1024 * 1024


def layer_index():
    return lax.axis_index("layer").astype(jnp.int32)


def row_index():
    return lax.axis_index("rows").astype(jnp.int32)


def prepare_kernel(
    offsets, queries_hbm, bases_hbm, values_hbm, conditioned_ref, queries, bases, values, arrived
):
    copies = [pltpu.make_async_copy(values_hbm, values, arrived.at[0])]
    for layer in range(LAY_DEV):
        columns = queries_hbm.at[:, layer * LDIM : (layer + 1) * LDIM]
        copies.append(pltpu.make_async_copy(columns, queries.at[layer], arrived.at[1 + 2 * layer]))
        copies.append(pltpu.make_async_copy(bases_hbm.at[layer], bases.at[layer], arrived.at[2 + 2 * layer]))
    for copy in copies:
        copy.start()
    base_column = layer_index() * (LAY_DEV * LDIM)
    copies[0].wait()
    for layer in range(LAY_DEV):
        copies[1 + 2 * layer].wait()
        copies[2 + 2 * layer].wait()
        basis = bases[layer]
        projected = jnp.dot(queries[layer], basis, preferred_element_type=jnp.float32)
        scaled = (projected / (values[layer : layer + 1, :] + DAMPING)).astype(jnp.bfloat16)
        restored = lax.dot_general(scaled, basis, NT, preferred_element_type=jnp.float32)
        first = pl.multiple_of(offsets[layer] - base_column, LDIM)
        conditioned_ref[:, pl.ds(first, LDIM)] = restored.astype(jnp.bfloat16)


def prepare(queries, bases, values, offsets):
    rows, dims = queries.shape
    hbm = pl.BlockSpec(memory_space=pltpu.HBM)
    return pl.pallas_call(
        prepare_kernel,
        out_shape=jax.ShapeDtypeStruct((rows, dims), jnp.bfloat16),
        in_specs=[pl.BlockSpec(memory_space=pltpu.SMEM), hbm, hbm, hbm],
        out_specs=pl.BlockSpec(memory_space=pltpu.VMEM),
        scratch_shapes=[
            pltpu.VMEM((LAY_DEV, rows, LDIM), jnp.bfloat16),
            pltpu.VMEM(bases.shape, jnp.bfloat16),
            pltpu.VMEM(values.shape, jnp.float32),
            pltpu.SemaphoreType.DMA((1 + 2 * LAY_DEV,)),
        ],
        compiler_params=pltpu.CompilerParams(vmem_limit_bytes=62 * MIB),
        cost_estimate=pl.CostEstimate(
            flops=4 * rows * dims * LDIM, bytes_accessed=6 * MIB, transcendentals=0
        ),
    )(offsets, queries, bases, values)


def masked_tile(queries, documents, query_ids, block):
    tile = lax.dot_general(queries, documents, NT, preferred_element_type=jnp.float32)
    doc_ids = block * tile.shape[1] + lax.broadcasted_iota(jnp.int32, tile.shape, 1)
    return jnp.where(query_ids == doc_ids, 0.0, tile)


def scoring(kernel, out_shape, conditioned, query_ids, *documents, extra=(), scratch=()):
    dims = conditioned.shape[1]
    docs = sum(part.shape[0] for part in documents)
    rows = sum(shape.shape[0] for shape in out_shape)
    vmem = pl.BlockSpec(memory_space=pltpu.VMEM)
    return pl.pallas_call(
        kernel,
        out_shape=out_shape,
        in_specs=[vmem] * (2 + len(documents) + len(extra)),
        out_specs=[vmem] * len(out_shape),
        scratch_shapes=scratch,
        compiler_params=pltpu.CompilerParams(vmem_limit_bytes=12 * MIB),
        cost_estimate=pl.CostEstimate(
            flops=2 * rows * docs * dims, bytes_accessed=2 * dims * (rows + docs), transcendentals=0
        ),
    )(conditioned, query_ids, *documents, *extra)


def turned_kernel(shares, block_of, queries_ref, ids_ref, documents_ref, *refs):
    *out_refs, held = refs
    held[...] = masked_tile(queries_ref[...], documents_ref[...], ids_ref[...], block_of(row_index()))
    for turn, out_ref in enumerate(out_refs):
        share_rows = out_ref.shape[0]
        first = pl.multiple_of(lax.rem(layer_index() + turn, shares) * share_rows, share_rows)
        out_ref[...] = held[pl.ds(first, share_rows), :].astype(jnp.bfloat16)


def half_shares(share_rows, kept):
    core = lax.rem(layer_index(), 2)
    core = core if kept else 1 - core
    return [pl.multiple_of((2 * chip + core) * share_rows, share_rows) for chip in range(2)]


def halves_kernel(block_of, queries_ref, ids_ref, documents_ref, *refs):
    front_refs, out_refs, held = refs[:-3], refs[-3:-1], refs[-1]
    held[...] = masked_tile(queries_ref[...], documents_ref[...], ids_ref[...], block_of(row_index()))
    docs = documents_ref.shape[0]
    rows, width = out_refs[0].shape
    for side, kept in enumerate((True, False)):
        if front_refs:
            out_refs[side][:, : width - docs] = front_refs[side][...]
        for chip, first in enumerate(half_shares(rows // 2, kept)):
            spot = slice(chip * (rows // 2), (chip + 1) * (rows // 2))
            out_refs[side][spot, width - docs :] = held[pl.ds(first, rows // 2), :]


def target_chip():
    chip, core = lax.div(layer_index(), 2), lax.rem(layer_index(), 2)
    return jnp.where(chip == core, 0, 1)


def half_kernel(block_of, kept, queries_ref, ids_ref, lower_ref, upper_ref, out_ref):
    documents = jnp.concatenate([lower_ref[...], upper_ref[...]], axis=0)
    rows = out_ref.shape[0]
    chip = target_chip() if kept else 1 - target_chip()
    spot = pl.ds(pl.multiple_of(chip * rows, rows), rows)
    out_ref[...] = masked_tile(queries_ref[spot, :], documents, ids_ref[spot, :], block_of(row_index()))


def total_of(refs):
    total = refs[0][...].astype(jnp.float32)
    for ref in refs[1:]:
        total += ref[...].astype(jnp.float32)
    return total


def sum_kernel(*refs):
    refs[-1][...] = total_of(refs[:-1]).astype(refs[-1].dtype)


def small_call(kernel, out_shape, *args):
    vmem = pl.BlockSpec(memory_space=pltpu.VMEM)
    return pl.pallas_call(
        kernel,
        out_shape=out_shape,
        in_specs=[vmem] * len(args),
        out_specs=[vmem] * len(out_shape),
        compiler_params=pltpu.CompilerParams(vmem_limit_bytes=4 * MIB),
    )(*args)


def direct_sum(tiles):
    shares = len(tiles)
    arrived = [tiles[0]]
    for turn in range(1, shares):
        pairs = [(lay, (lay + turn) % shares) for lay in range(shares)]
        arrived.append(lax.ppermute(tiles[turn], "layer", pairs))
    (total,) = small_call(sum_kernel, [jax.ShapeDtypeStruct(tiles[0].shape, jnp.float32)], *arrived)
    return total


def core_sum_kernel(kept_ref, arrived_ref, mine_ref, other_ref):
    rows = mine_ref.shape[0]
    chip = lax.div(layer_index(), 2)
    mine = pl.ds(pl.multiple_of(chip * rows, rows), rows)
    other = pl.ds(pl.multiple_of((1 - chip) * rows, rows), rows)
    mine_ref[...] = (kept_ref[mine, :] + arrived_ref[mine, :]).astype(mine_ref.dtype)
    other_ref[...] = (kept_ref[other, :] + arrived_ref[other, :]).astype(other_ref.dtype)


def chip_sum_kernel(mine_ref, arrived_ref, *out_refs):
    docs = out_refs[0].shape[1]
    for spot, out_ref in enumerate(out_refs):
        columns = slice(spot * docs, (spot + 1) * docs)
        total = mine_ref[:, columns] + arrived_ref[:, columns].astype(jnp.float32)
        out_ref[...] = total.astype(out_ref.dtype)


def swap(value, distance):
    count = lax.axis_size("layer")
    return lax.ppermute(value, "layer", [(lay, lay ^ distance) for lay in range(count)])


def core_sum(kept, arrived, mine_type):
    rows, width = kept.shape[0] // 2, kept.shape[1]
    out_shape = [jax.ShapeDtypeStruct((rows, width), out_type) for out_type in (mine_type, jnp.bfloat16)]
    return small_call(core_sum_kernel, out_shape, kept, arrived)


def layer_sum(kept, sent, out_types):
    mine, other = core_sum(kept, swap(sent, 1), jnp.float32)
    rows, docs = mine.shape[0], mine.shape[1] // len(out_types)
    out_shape = [jax.ShapeDtypeStruct((rows, docs), out_type) for out_type in out_types]
    return small_call(chip_sum_kernel, out_shape, mine, swap(other, 2))


ROUND_ONE = ((0, 2), (2, 3), (3, 1), (1, 0))
ROUND_TWO = ((0, 1), (1, 3), (3, 2), (2, 0))
BLOCK_ONE = (1, 3, 0, 2)
BLOCK_TWO = (2, 0, 3, 1)
BLOCK_LAST = (3, 2, 1, 0)


def pick(table):
    def entry(row):
        value = jnp.int32(table[0])
        for index in range(1, len(table)):
            value = jnp.where(row == index, jnp.int32(table[index]), value)
        return value

    return entry


def step_of(table):
    return pick([(block - table.index(block)) % STEPS for block in range(STEPS)])


def assemble_kernel(own_ref, first_ref, second_ref, out_ref):
    out_ref[0] = own_ref[...]
    for ref, table in ((first_ref, BLOCK_ONE), (second_ref, BLOCK_TWO)):
        out_ref[step_of(table)(row_index())] = ref[...].astype(jnp.float32)


def finish_kernel(mine_ref, arrived_ref, scores_hbm, out_hbm, total, copied):
    del scores_hbm
    rows = total.shape[0]
    share = pl.ds(pl.multiple_of(lax.rem(layer_index(), 2) * rows, rows), rows)
    total[...] = mine_ref[share, :].astype(jnp.float32) + arrived_ref[share, :].astype(jnp.float32)
    copy = pltpu.make_async_copy(total, out_hbm.at[step_of(BLOCK_LAST)(row_index())], copied)
    copy.start()
    copy.wait()


def finish(mine, arrived, scores):
    hbm = pl.BlockSpec(memory_space=pltpu.HBM)
    vmem = pl.BlockSpec(memory_space=pltpu.VMEM)
    return pl.pallas_call(
        finish_kernel,
        out_shape=jax.ShapeDtypeStruct(scores.shape, scores.dtype),
        in_specs=[vmem, vmem, hbm],
        out_specs=hbm,
        scratch_shapes=[pltpu.VMEM(scores.shape[1:], jnp.float32), pltpu.SemaphoreType.DMA],
        input_output_aliases={2: 0},
        compiler_params=pltpu.CompilerParams(vmem_limit_bytes=4 * MIB),
    )(mine, arrived, scores)


def along_line(documents, conditioned, query_ids):
    docs = documents.shape[0]
    half = (conditioned.shape[0] // 2, docs)

    def halves(block, block_of, front=()):
        width = docs * (1 + bool(front))
        out_shape = [jax.ShapeDtypeStruct((half[0], width), jnp.float32)] * 2
        scratch = [pltpu.VMEM((2 * half[0], docs), jnp.float32)]
        kernel = functools.partial(halves_kernel, block_of)
        return scoring(kernel, out_shape, conditioned, query_ids, block, extra=front, scratch=scratch)

    def one_half(parts, block_of, kept):
        kernel = functools.partial(half_kernel, block_of, kept)
        out_shape = [jax.ShapeDtypeStruct(half, jnp.float32)]
        return scoring(kernel, out_shape, conditioned, query_ids, *parts)[0]

    def back(total, table):
        return lax.ppermute(total, "rows", tuple(enumerate(table)))

    one = lax.ppermute(documents, "rows", ROUND_ONE)
    later, conditioned = lax.optimization_barrier((documents, conditioned))
    two = lax.ppermute(later, "rows", ROUND_TWO)
    own = halves(later, lambda row: row)
    one, own = lax.optimization_barrier((one, own))
    three = [
        lax.ppermute(part, "rows", ROUND_ONE) for part in (one[: docs * 3 // 4], one[docs * 3 // 4 :])
    ]

    own, first = layer_sum(*halves(one, pick(BLOCK_ONE), own), (jnp.float32, jnp.bfloat16))
    two, first = lax.optimization_barrier((two, first))
    first = back(first, BLOCK_ONE)
    (second,) = layer_sum(*halves(two, pick(BLOCK_TWO)), (jnp.bfloat16,))
    second = back(second, BLOCK_TWO)
    three, first, second = lax.optimization_barrier((three, first, second))

    arrived = swap(one_half(three, pick(BLOCK_LAST), False), 1)
    kept = one_half(three, pick(BLOCK_LAST), True)
    (both,) = small_call(sum_kernel, [jax.ShapeDtypeStruct(half, jnp.bfloat16)], kept, arrived)
    shares = lax.axis_size("layer")
    pairs = [
        (row * shares + lay, BLOCK_LAST[row] * shares + 2 * ((lay // 2) ^ (lay % 2)) + lay % 2)
        for row in range(len(BLOCK_LAST))
        for lay in range(shares)
    ]
    mine = lax.ppermute(both, ("rows", "layer"), pairs)
    out_shape = [jax.ShapeDtypeStruct((STEPS,) + own.shape, jnp.float32)]
    (scores,) = small_call(assemble_kernel, out_shape, own, first, second)
    return finish(mine, swap(mine, 1), scores)


def around_ring(documents, conditioned, query_ids):
    n_rows, shares = lax.axis_size("rows"), lax.axis_size("layer")
    rows, docs = conditioned.shape[0], documents.shape[0]
    result = []
    for step in range(STEPS):
        behind = [(row, (row - step) % n_rows) for row in range(n_rows)]
        block = lax.ppermute(documents, "rows", behind) if step else documents

        def ahead(row, step=step):
            return lax.rem(row + step, n_rows)

        kernel = functools.partial(turned_kernel, shares, ahead)
        out_shape = [jax.ShapeDtypeStruct((rows // shares, docs), jnp.bfloat16)] * shares
        scratch = [pltpu.VMEM((rows, docs), jnp.float32)]
        total = direct_sum(scoring(kernel, out_shape, conditioned, query_ids, block, scratch=scratch))
        onward = [(row, (row + step) % n_rows) for row in range(n_rows)]
        result.append(lax.ppermute(total, "rows", onward) if step else total)
    return jnp.stack(result)


def local(train_grads, query_grads, eigenbases, eigenvalues, layer_offsets, query_doc_ids):
    conditioned = prepare(query_grads, eigenbases, eigenvalues, layer_offsets)
    on_line = lax.axis_size("rows") == 4 and lax.axis_size("layer") == 4
    plan = along_line if on_line else around_ring
    return plan(train_grads, conditioned, query_doc_ids[:, None])


def solution(mesh):
    in_specs = (
        P(("group", "rows"), "layer"),
        P(("group", "rows"), "layer"),
        P("layer", None, None),
        P("layer", None),
        P("layer"),
        P(("group", "rows")),
    )
    out_specs = P(None, "layer", ("group", "rows"))
    return jax.shard_map(local, mesh=mesh, in_specs=in_specs, out_specs=out_specs, check_vma=False)
```

```python
import functools

import jax
import jax.numpy as jnp
from jax import lax
from jax.experimental import pallas as pl
from jax.experimental.pallas import tpu as pltpu
from jax.sharding import PartitionSpec as P

LDIM = 512
LAY_DEV = 4
STEPS = 4
DAMPING = 0.05
NT = (((1,), (1,)), ((), ()))
MIB = 1024 * 1024


def layer_index():
    return lax.axis_index("layer").astype(jnp.int32)


def row_index():
    return lax.axis_index("rows").astype(jnp.int32)


def prepare_kernel(
    offsets, queries_hbm, bases_hbm, values_hbm, conditioned_ref, queries, bases, values, arrived
):
    copies = [pltpu.make_async_copy(values_hbm, values, arrived.at[0])]
    for layer in range(LAY_DEV):
        columns = queries_hbm.at[:, layer * LDIM : (layer + 1) * LDIM]
        copies.append(pltpu.make_async_copy(columns, queries.at[layer], arrived.at[1 + 2 * layer]))
        copies.append(pltpu.make_async_copy(bases_hbm.at[layer], bases.at[layer], arrived.at[2 + 2 * layer]))
    for copy in copies:
        copy.start()
    base_column = layer_index() * (LAY_DEV * LDIM)
    copies[0].wait()
    for layer in range(LAY_DEV):
        copies[1 + 2 * layer].wait()
        copies[2 + 2 * layer].wait()
        basis = bases[layer]
        projected = jnp.dot(queries[layer], basis, preferred_element_type=jnp.float32)
        scaled = (projected / (values[layer : layer + 1, :] + DAMPING)).astype(jnp.bfloat16)
        restored = lax.dot_general(scaled, basis, NT, preferred_element_type=jnp.float32)
        first = pl.multiple_of(offsets[layer] - base_column, LDIM)
        conditioned_ref[:, pl.ds(first, LDIM)] = restored.astype(jnp.bfloat16)


def prepare(queries, bases, values, offsets):
    rows, dims = queries.shape
    hbm = pl.BlockSpec(memory_space=pltpu.HBM)
    return pl.pallas_call(
        prepare_kernel,
        out_shape=jax.ShapeDtypeStruct((rows, dims), jnp.bfloat16),
        in_specs=[pl.BlockSpec(memory_space=pltpu.SMEM), hbm, hbm, hbm],
        out_specs=pl.BlockSpec(memory_space=pltpu.VMEM),
        scratch_shapes=[
            pltpu.VMEM((LAY_DEV, rows, LDIM), jnp.bfloat16),
            pltpu.VMEM(bases.shape, jnp.bfloat16),
            pltpu.VMEM(values.shape, jnp.float32),
            pltpu.SemaphoreType.DMA((1 + 2 * LAY_DEV,)),
        ],
        compiler_params=pltpu.CompilerParams(vmem_limit_bytes=62 * MIB),
        cost_estimate=pl.CostEstimate(
            flops=4 * rows * dims * LDIM, bytes_accessed=6 * MIB, transcendentals=0
        ),
    )(offsets, queries, bases, values)


def masked_tile(queries, documents, query_ids, block):
    tile = lax.dot_general(queries, documents, NT, preferred_element_type=jnp.float32)
    doc_ids = block * tile.shape[1] + lax.broadcasted_iota(jnp.int32, tile.shape, 1)
    return jnp.where(query_ids == doc_ids, 0.0, tile)


def scoring(kernel, out_shape, conditioned, query_ids, documents, extra=(), scratch=()):
    dims = conditioned.shape[1]
    docs = documents.shape[0]
    rows = sum(shape.shape[0] for shape in out_shape)
    vmem = pl.BlockSpec(memory_space=pltpu.VMEM)
    return pl.pallas_call(
        kernel,
        out_shape=out_shape,
        in_specs=[vmem] * (3 + len(extra)),
        out_specs=[vmem] * len(out_shape),
        scratch_shapes=scratch,
        compiler_params=pltpu.CompilerParams(vmem_limit_bytes=12 * MIB),
        cost_estimate=pl.CostEstimate(
            flops=2 * rows * docs * dims, bytes_accessed=2 * dims * (rows + docs), transcendentals=0
        ),
    )(conditioned, query_ids, documents, *extra)


def turned_kernel(shares, block_of, queries_ref, ids_ref, documents_ref, *refs):
    *out_refs, held = refs
    held[...] = masked_tile(queries_ref[...], documents_ref[...], ids_ref[...], block_of(row_index()))
    for turn, out_ref in enumerate(out_refs):
        share_rows = out_ref.shape[0]
        first = pl.multiple_of(lax.rem(layer_index() + turn, shares) * share_rows, share_rows)
        out_ref[...] = held[pl.ds(first, share_rows), :].astype(jnp.bfloat16)


def half_shares(share_rows, kept):
    core = lax.rem(layer_index(), 2)
    core = core if kept else 1 - core
    return [pl.multiple_of((2 * chip + core) * share_rows, share_rows) for chip in range(2)]


def halves_kernel(block_of, queries_ref, ids_ref, documents_ref, *refs):
    front_refs, out_refs, held = refs[:-3], refs[-3:-1], refs[-1]
    held[...] = masked_tile(queries_ref[...], documents_ref[...], ids_ref[...], block_of(row_index()))
    docs = documents_ref.shape[0]
    rows, width = out_refs[0].shape
    for side, kept in enumerate((True, False)):
        if front_refs:
            out_refs[side][:, : width - docs] = front_refs[side][...]
        for chip, first in enumerate(half_shares(rows // 2, kept)):
            spot = slice(chip * (rows // 2), (chip + 1) * (rows // 2))
            out_refs[side][spot, width - docs :] = held[pl.ds(first, rows // 2), :]


def target_chip():
    chip, core = lax.div(layer_index(), 2), lax.rem(layer_index(), 2)
    return jnp.where(chip == core, 0, 1)


def half_kernel(block_of, kept, queries_ref, ids_ref, documents_ref, out_ref):
    rows = out_ref.shape[0]
    chip = target_chip() if kept else 1 - target_chip()
    spot = pl.ds(pl.multiple_of(chip * rows, rows), rows)
    out_ref[...] = masked_tile(queries_ref[spot, :], documents_ref[...], ids_ref[spot, :], block_of(row_index()))


def total_of(refs):
    total = refs[0][...].astype(jnp.float32)
    for ref in refs[1:]:
        total += ref[...].astype(jnp.float32)
    return total


def sum_kernel(*refs):
    refs[-1][...] = total_of(refs[:-1]).astype(refs[-1].dtype)


def small_call(kernel, out_shape, *args):
    vmem = pl.BlockSpec(memory_space=pltpu.VMEM)
    return pl.pallas_call(
        kernel,
        out_shape=out_shape,
        in_specs=[vmem] * len(args),
        out_specs=[vmem] * len(out_shape),
        compiler_params=pltpu.CompilerParams(vmem_limit_bytes=4 * MIB),
    )(*args)


def direct_sum(tiles):
    shares = len(tiles)
    arrived = [tiles[0]]
    for turn in range(1, shares):
        pairs = [(lay, (lay + turn) % shares) for lay in range(shares)]
        arrived.append(lax.ppermute(tiles[turn], "layer", pairs))
    (total,) = small_call(sum_kernel, [jax.ShapeDtypeStruct(tiles[0].shape, jnp.float32)], *arrived)
    return total


def core_sum_kernel(kept_ref, arrived_ref, mine_ref, other_ref):
    rows = mine_ref.shape[0]
    chip = lax.div(layer_index(), 2)
    mine = pl.ds(pl.multiple_of(chip * rows, rows), rows)
    other = pl.ds(pl.multiple_of((1 - chip) * rows, rows), rows)
    mine_ref[...] = (kept_ref[mine, :] + arrived_ref[mine, :]).astype(mine_ref.dtype)
    other_ref[...] = (kept_ref[other, :] + arrived_ref[other, :]).astype(other_ref.dtype)


def chip_sum_kernel(mine_ref, arrived_ref, *out_refs):
    docs = out_refs[0].shape[1]
    for spot, out_ref in enumerate(out_refs):
        columns = slice(spot * docs, (spot + 1) * docs)
        total = mine_ref[:, columns] + arrived_ref[:, columns].astype(jnp.float32)
        out_ref[...] = total.astype(out_ref.dtype)


def swap(value, distance):
    count = lax.axis_size("layer")
    return lax.ppermute(value, "layer", [(lay, lay ^ distance) for lay in range(count)])


def core_sum(kept, arrived, mine_type):
    rows, width = kept.shape[0] // 2, kept.shape[1]
    out_shape = [jax.ShapeDtypeStruct((rows, width), out_type) for out_type in (mine_type, jnp.bfloat16)]
    return small_call(core_sum_kernel, out_shape, kept, arrived)


def layer_sum(kept, sent, out_types):
    mine, other = core_sum(kept, swap(sent, 1), jnp.float32)
    rows, docs = mine.shape[0], mine.shape[1] // len(out_types)
    out_shape = [jax.ShapeDtypeStruct((rows, docs), out_type) for out_type in out_types]
    return small_call(chip_sum_kernel, out_shape, mine, swap(other, 2))


ROUND_ONE = ((0, 1), (1, 3), (3, 2), (2, 0))
ROUND_TWO = ((0, 2), (2, 3), (3, 1), (1, 0))
BLOCK_ONE = (2, 0, 3, 1)
BLOCK_TWO = (1, 3, 0, 2)
BLOCK_LAST = (3, 2, 1, 0)


def pick(table):
    def entry(row):
        value = jnp.int32(table[0])
        for index in range(1, len(table)):
            value = jnp.where(row == index, jnp.int32(table[index]), value)
        return value

    return entry


def step_of(table):
    return pick([(block - table.index(block)) % STEPS for block in range(STEPS)])


def assemble_kernel(own_ref, first_ref, second_ref, out_ref):
    out_ref[0] = own_ref[...]
    for ref, table in ((first_ref, BLOCK_ONE), (second_ref, BLOCK_TWO)):
        out_ref[step_of(table)(row_index())] = ref[...].astype(jnp.float32)


def finish_kernel(mine_ref, arrived_ref, scores_hbm, out_hbm, total, copied):
    del scores_hbm
    rows = total.shape[0]
    share = pl.ds(pl.multiple_of(lax.rem(layer_index(), 2) * rows, rows), rows)
    total[...] = mine_ref[share, :].astype(jnp.float32) + arrived_ref[share, :].astype(jnp.float32)
    copy = pltpu.make_async_copy(total, out_hbm.at[step_of(BLOCK_LAST)(row_index())], copied)
    copy.start()
    copy.wait()


def finish(mine, arrived, scores):
    hbm = pl.BlockSpec(memory_space=pltpu.HBM)
    vmem = pl.BlockSpec(memory_space=pltpu.VMEM)
    return pl.pallas_call(
        finish_kernel,
        out_shape=jax.ShapeDtypeStruct(scores.shape, scores.dtype),
        in_specs=[vmem, vmem, hbm],
        out_specs=hbm,
        scratch_shapes=[pltpu.VMEM(scores.shape[1:], jnp.float32), pltpu.SemaphoreType.DMA],
        input_output_aliases={2: 0},
        compiler_params=pltpu.CompilerParams(vmem_limit_bytes=4 * MIB),
    )(mine, arrived, scores)


def along_line(documents, conditioned, query_ids):
    docs = documents.shape[0]
    half = (conditioned.shape[0] // 2, docs)

    def halves(block, block_of, front=()):
        width = docs * (1 + bool(front))
        out_shape = [jax.ShapeDtypeStruct((half[0], width), jnp.float32)] * 2
        scratch = [pltpu.VMEM((2 * half[0], docs), jnp.float32)]
        kernel = functools.partial(halves_kernel, block_of)
        return scoring(kernel, out_shape, conditioned, query_ids, block, front, scratch)

    def one_half(block, block_of, kept):
        kernel = functools.partial(half_kernel, block_of, kept)
        out_shape = [jax.ShapeDtypeStruct(half, jnp.float32)]
        return scoring(kernel, out_shape, conditioned, query_ids, block)[0]

    def back(total, table):
        return lax.ppermute(total, "rows", tuple(enumerate(table)))

    one = lax.ppermute(documents, "rows", ROUND_ONE)
    later, conditioned = lax.optimization_barrier((documents, conditioned))
    two = lax.ppermute(later, "rows", ROUND_TWO)
    own = halves(later, lambda row: row)
    one, own = lax.optimization_barrier((one, own))
    three = lax.ppermute(one, "rows", ROUND_ONE)

    own, first = layer_sum(*halves(one, pick(BLOCK_ONE), own), (jnp.float32, jnp.bfloat16))
    two, first = lax.optimization_barrier((two, first))
    first = back(first, BLOCK_ONE)
    (second,) = layer_sum(*halves(two, pick(BLOCK_TWO)), (jnp.bfloat16,))
    second = back(second, BLOCK_TWO)
    three, first, second = lax.optimization_barrier((three, first, second))

    arrived = swap(one_half(three, pick(BLOCK_LAST), False), 1)
    kept = one_half(three, pick(BLOCK_LAST), True)
    (both,) = small_call(sum_kernel, [jax.ShapeDtypeStruct(half, jnp.bfloat16)], kept, arrived)
    shares = lax.axis_size("layer")
    pairs = [
        (row * shares + lay, BLOCK_LAST[row] * shares + 2 * ((lay // 2) ^ (lay % 2)) + lay % 2)
        for row in range(len(BLOCK_LAST))
        for lay in range(shares)
    ]
    mine = lax.ppermute(both, ("rows", "layer"), pairs)
    out_shape = [jax.ShapeDtypeStruct((STEPS,) + own.shape, jnp.float32)]
    (scores,) = small_call(assemble_kernel, out_shape, own, first, second)
    return finish(mine, swap(mine, 1), scores)


def around_ring(documents, conditioned, query_ids):
    n_rows, shares = lax.axis_size("rows"), lax.axis_size("layer")
    rows, docs = conditioned.shape[0], documents.shape[0]
    result = []
    for step in range(STEPS):
        behind = [(row, (row - step) % n_rows) for row in range(n_rows)]
        block = lax.ppermute(documents, "rows", behind) if step else documents

        def ahead(row, step=step):
            return lax.rem(row + step, n_rows)

        kernel = functools.partial(turned_kernel, shares, ahead)
        out_shape = [jax.ShapeDtypeStruct((rows // shares, docs), jnp.bfloat16)] * shares
        scratch = [pltpu.VMEM((rows, docs), jnp.float32)]
        total = direct_sum(scoring(kernel, out_shape, conditioned, query_ids, block, (), scratch))
        onward = [(row, (row + step) % n_rows) for row in range(n_rows)]
        result.append(lax.ppermute(total, "rows", onward) if step else total)
    return jnp.stack(result)


def local(train_grads, query_grads, eigenbases, eigenvalues, layer_offsets, query_doc_ids):
    conditioned = prepare(query_grads, eigenbases, eigenvalues, layer_offsets)
    on_line = lax.axis_size("rows") == 4 and lax.axis_size("layer") == 4
    plan = along_line if on_line else around_ring
    return plan(train_grads, conditioned, query_doc_ids[:, None])


def solution(mesh):
    in_specs = (
        P(("group", "rows"), "layer"),
        P(("group", "rows"), "layer"),
        P("layer", None, None),
        P("layer", None),
        P("layer"),
        P(("group", "rows")),
    )
    out_specs = P(None, "layer", ("group", "rows"))
    return jax.shard_map(local, mesh=mesh, in_specs=in_specs, out_specs=out_specs, check_vma=False)
```

```python
import functools

import jax
import jax.numpy as jnp
from jax import lax
from jax.experimental import pallas as pl
from jax.experimental.pallas import tpu as pltpu
from jax.sharding import PartitionSpec as P

LDIM = 512
LAY_DEV = 4
STEPS = 4
DAMPING = 0.05
NT = (((1,), (1,)), ((), ()))
MIB = 1024 * 1024


def layer_index():
    return lax.axis_index("layer").astype(jnp.int32)


def row_index():
    return lax.axis_index("rows").astype(jnp.int32)


def prepare_kernel(
    offsets, queries_hbm, bases_hbm, values_hbm, conditioned_ref, queries, bases, values, arrived
):
    copies = [pltpu.make_async_copy(values_hbm, values, arrived.at[0])]
    for layer in range(LAY_DEV):
        columns = queries_hbm.at[:, layer * LDIM : (layer + 1) * LDIM]
        copies.append(pltpu.make_async_copy(columns, queries.at[layer], arrived.at[1 + 2 * layer]))
        copies.append(pltpu.make_async_copy(bases_hbm.at[layer], bases.at[layer], arrived.at[2 + 2 * layer]))
    for copy in copies:
        copy.start()
    base_column = layer_index() * (LAY_DEV * LDIM)
    copies[0].wait()
    for layer in range(LAY_DEV):
        copies[1 + 2 * layer].wait()
        copies[2 + 2 * layer].wait()
        basis = bases[layer]
        projected = jnp.dot(queries[layer], basis, preferred_element_type=jnp.float32)
        scaled = (projected / (values[layer : layer + 1, :] + DAMPING)).astype(jnp.bfloat16)
        restored = lax.dot_general(scaled, basis, NT, preferred_element_type=jnp.float32)
        first = pl.multiple_of(offsets[layer] - base_column, LDIM)
        conditioned_ref[:, pl.ds(first, LDIM)] = restored.astype(jnp.bfloat16)


def prepare(queries, bases, values, offsets):
    rows, dims = queries.shape
    hbm = pl.BlockSpec(memory_space=pltpu.HBM)
    return pl.pallas_call(
        prepare_kernel,
        out_shape=jax.ShapeDtypeStruct((rows, dims), jnp.bfloat16),
        in_specs=[pl.BlockSpec(memory_space=pltpu.SMEM), hbm, hbm, hbm],
        out_specs=pl.BlockSpec(memory_space=pltpu.VMEM),
        scratch_shapes=[
            pltpu.VMEM((LAY_DEV, rows, LDIM), jnp.bfloat16),
            pltpu.VMEM(bases.shape, jnp.bfloat16),
            pltpu.VMEM(values.shape, jnp.float32),
            pltpu.SemaphoreType.DMA((1 + 2 * LAY_DEV,)),
        ],
        compiler_params=pltpu.CompilerParams(vmem_limit_bytes=62 * MIB),
        cost_estimate=pl.CostEstimate(
            flops=4 * rows * dims * LDIM, bytes_accessed=6 * MIB, transcendentals=0
        ),
    )(offsets, queries, bases, values)


def masked_tile(queries, documents, query_ids, block):
    tile = lax.dot_general(queries, documents, NT, preferred_element_type=jnp.float32)
    doc_ids = block * tile.shape[1] + lax.broadcasted_iota(jnp.int32, tile.shape, 1)
    return jnp.where(query_ids == doc_ids, 0.0, tile)


def scoring(kernel, out_shape, conditioned, query_ids, documents, extra=(), scratch=()):
    dims = conditioned.shape[1]
    docs = documents.shape[0]
    rows = sum(shape.shape[0] for shape in out_shape)
    vmem = pl.BlockSpec(memory_space=pltpu.VMEM)
    return pl.pallas_call(
        kernel,
        out_shape=out_shape,
        in_specs=[vmem] * (3 + len(extra)),
        out_specs=[vmem] * len(out_shape),
        scratch_shapes=scratch,
        compiler_params=pltpu.CompilerParams(vmem_limit_bytes=12 * MIB),
        cost_estimate=pl.CostEstimate(
            flops=2 * rows * docs * dims, bytes_accessed=2 * dims * (rows + docs), transcendentals=0
        ),
    )(conditioned, query_ids, documents, *extra)


def turned_kernel(shares, block_of, queries_ref, ids_ref, documents_ref, *refs):
    *out_refs, held = refs
    held[...] = masked_tile(queries_ref[...], documents_ref[...], ids_ref[...], block_of(row_index()))
    for turn, out_ref in enumerate(out_refs):
        share_rows = out_ref.shape[0]
        first = pl.multiple_of(lax.rem(layer_index() + turn, shares) * share_rows, share_rows)
        out_ref[...] = held[pl.ds(first, share_rows), :].astype(jnp.bfloat16)


def half_shares(share_rows, kept):
    core = lax.rem(layer_index(), 2)
    core = core if kept else 1 - core
    return [pl.multiple_of((2 * chip + core) * share_rows, share_rows) for chip in range(2)]


def halves_kernel(block_of, queries_ref, ids_ref, documents_ref, *refs):
    front_refs, out_refs, held = refs[:-3], refs[-3:-1], refs[-1]
    held[...] = masked_tile(queries_ref[...], documents_ref[...], ids_ref[...], block_of(row_index()))
    docs = documents_ref.shape[0]
    rows, width = out_refs[0].shape
    for side, kept in enumerate((True, False)):
        if front_refs:
            out_refs[side][:, : width - docs] = front_refs[side][...]
        for chip, first in enumerate(half_shares(rows // 2, kept)):
            spot = slice(chip * (rows // 2), (chip + 1) * (rows // 2))
            out_refs[side][spot, width - docs :] = held[pl.ds(first, rows // 2), :]


def target_chip():
    chip, core = lax.div(layer_index(), 2), lax.rem(layer_index(), 2)
    return jnp.where(chip == core, 1, 0)


def half_kernel(block_of, kept, queries_ref, ids_ref, documents_ref, out_ref):
    rows = out_ref.shape[0]
    chip = target_chip() if kept else 1 - target_chip()
    spot = pl.ds(pl.multiple_of(chip * rows, rows), rows)
    out_ref[...] = masked_tile(queries_ref[spot, :], documents_ref[...], ids_ref[spot, :], block_of(row_index()))


def total_of(refs):
    total = refs[0][...].astype(jnp.float32)
    for ref in refs[1:]:
        total += ref[...].astype(jnp.float32)
    return total


def sum_kernel(*refs):
    refs[-1][...] = total_of(refs[:-1]).astype(refs[-1].dtype)


def small_call(kernel, out_shape, *args):
    vmem = pl.BlockSpec(memory_space=pltpu.VMEM)
    return pl.pallas_call(
        kernel,
        out_shape=out_shape,
        in_specs=[vmem] * len(args),
        out_specs=[vmem] * len(out_shape),
        compiler_params=pltpu.CompilerParams(vmem_limit_bytes=4 * MIB),
    )(*args)


def direct_sum(tiles):
    shares = len(tiles)
    arrived = [tiles[0]]
    for turn in range(1, shares):
        pairs = [(lay, (lay + turn) % shares) for lay in range(shares)]
        arrived.append(lax.ppermute(tiles[turn], "layer", pairs))
    (total,) = small_call(sum_kernel, [jax.ShapeDtypeStruct(tiles[0].shape, jnp.float32)], *arrived)
    return total


def core_sum_kernel(kept_ref, arrived_ref, mine_ref, other_ref):
    rows = mine_ref.shape[0]
    chip = lax.div(layer_index(), 2)
    mine = pl.ds(pl.multiple_of(chip * rows, rows), rows)
    other = pl.ds(pl.multiple_of((1 - chip) * rows, rows), rows)
    mine_ref[...] = (kept_ref[mine, :] + arrived_ref[mine, :]).astype(mine_ref.dtype)
    other_ref[...] = (kept_ref[other, :] + arrived_ref[other, :]).astype(other_ref.dtype)


def chip_sum_kernel(mine_ref, arrived_ref, *out_refs):
    docs = out_refs[0].shape[1]
    for spot, out_ref in enumerate(out_refs):
        columns = slice(spot * docs, (spot + 1) * docs)
        total = mine_ref[:, columns] + arrived_ref[:, columns].astype(jnp.float32)
        out_ref[...] = total.astype(out_ref.dtype)


def swap(value, distance):
    count = lax.axis_size("layer")
    return lax.ppermute(value, "layer", [(lay, lay ^ distance) for lay in range(count)])


def core_sum(kept, arrived, mine_type):
    rows, width = kept.shape[0] // 2, kept.shape[1]
    out_shape = [jax.ShapeDtypeStruct((rows, width), out_type) for out_type in (mine_type, jnp.bfloat16)]
    return small_call(core_sum_kernel, out_shape, kept, arrived)


def layer_sum(kept, sent, out_types):
    mine, other = core_sum(kept, swap(sent, 1), jnp.float32)
    rows, docs = mine.shape[0], mine.shape[1] // len(out_types)
    out_shape = [jax.ShapeDtypeStruct((rows, docs), out_type) for out_type in out_types]
    return small_call(chip_sum_kernel, out_shape, mine, swap(other, 2))


ROUND_ONE = ((0, 2), (2, 3), (3, 1), (1, 0))
ROUND_TWO = ((0, 1), (1, 3), (3, 2), (2, 0))
BLOCK_ONE = (1, 3, 0, 2)
BLOCK_TWO = (2, 0, 3, 1)
BLOCK_LAST = (3, 2, 1, 0)


def pick(table):
    def entry(row):
        value = jnp.int32(table[0])
        for index in range(1, len(table)):
            value = jnp.where(row == index, jnp.int32(table[index]), value)
        return value

    return entry


def step_of(table):
    return pick([(block - table.index(block)) % STEPS for block in range(STEPS)])


def assemble_kernel(own_ref, first_ref, second_ref, out_ref):
    out_ref[0] = own_ref[...]
    for ref, table in ((first_ref, BLOCK_ONE), (second_ref, BLOCK_TWO)):
        out_ref[step_of(table)(row_index())] = ref[...].astype(jnp.float32)


def finish_kernel(mine_ref, arrived_ref, scores_hbm, out_hbm, total, copied):
    del scores_hbm
    rows = total.shape[0]
    share = pl.ds(pl.multiple_of(lax.rem(layer_index(), 2) * rows, rows), rows)
    total[...] = mine_ref[share, :].astype(jnp.float32) + arrived_ref[share, :].astype(jnp.float32)
    copy = pltpu.make_async_copy(total, out_hbm.at[step_of(BLOCK_LAST)(row_index())], copied)
    copy.start()
    copy.wait()


def finish(mine, arrived, scores):
    hbm = pl.BlockSpec(memory_space=pltpu.HBM)
    vmem = pl.BlockSpec(memory_space=pltpu.VMEM)
    return pl.pallas_call(
        finish_kernel,
        out_shape=jax.ShapeDtypeStruct(scores.shape, scores.dtype),
        in_specs=[vmem, vmem, hbm],
        out_specs=hbm,
        scratch_shapes=[pltpu.VMEM(scores.shape[1:], jnp.float32), pltpu.SemaphoreType.DMA],
        input_output_aliases={2: 0},
        compiler_params=pltpu.CompilerParams(vmem_limit_bytes=4 * MIB),
    )(mine, arrived, scores)


def along_line(documents, conditioned, query_ids):
    docs = documents.shape[0]
    half = (conditioned.shape[0] // 2, docs)

    def halves(block, block_of, front=()):
        width = docs * (1 + bool(front))
        out_shape = [jax.ShapeDtypeStruct((half[0], width), jnp.float32)] * 2
        scratch = [pltpu.VMEM((2 * half[0], docs), jnp.float32)]
        kernel = functools.partial(halves_kernel, block_of)
        return scoring(kernel, out_shape, conditioned, query_ids, block, front, scratch)

    def one_half(block, block_of, kept):
        kernel = functools.partial(half_kernel, block_of, kept)
        out_shape = [jax.ShapeDtypeStruct(half, jnp.float32)]
        return scoring(kernel, out_shape, conditioned, query_ids, block)[0]

    def back(total, table):
        return lax.ppermute(total, "rows", tuple(enumerate(table)))

    one = lax.ppermute(documents, "rows", ROUND_ONE)
    later, conditioned = lax.optimization_barrier((documents, conditioned))
    two = lax.ppermute(later, "rows", ROUND_TWO)
    own = halves(later, lambda row: row)
    one, own = lax.optimization_barrier((one, own))
    three = lax.ppermute(one, "rows", ROUND_ONE)

    own, first = layer_sum(*halves(one, pick(BLOCK_ONE), own), (jnp.float32, jnp.bfloat16))
    two, first = lax.optimization_barrier((two, first))
    first = back(first, BLOCK_ONE)
    (second,) = layer_sum(*halves(two, pick(BLOCK_TWO)), (jnp.bfloat16,))
    second = back(second, BLOCK_TWO)
    three, first, second = lax.optimization_barrier((three, first, second))

    arrived = swap(one_half(three, pick(BLOCK_LAST), False), 1)
    kept = one_half(three, pick(BLOCK_LAST), True)
    (both,) = small_call(sum_kernel, [jax.ShapeDtypeStruct(half, jnp.bfloat16)], kept, arrived)
    shares = lax.axis_size("layer")
    pairs = [
        (row * shares + lay, BLOCK_LAST[row] * shares + 2 * (1 - ((lay // 2) ^ (lay % 2))) + lay % 2)
        for row in range(len(BLOCK_LAST))
        for lay in range(shares)
    ]
    mine = lax.ppermute(both, ("rows", "layer"), pairs)
    out_shape = [jax.ShapeDtypeStruct((STEPS,) + own.shape, jnp.float32)]
    (scores,) = small_call(assemble_kernel, out_shape, own, first, second)
    return finish(mine, swap(mine, 1), scores)


def around_ring(documents, conditioned, query_ids):
    n_rows, shares = lax.axis_size("rows"), lax.axis_size("layer")
    rows, docs = conditioned.shape[0], documents.shape[0]
    result = []
    for step in range(STEPS):
        behind = [(row, (row - step) % n_rows) for row in range(n_rows)]
        block = lax.ppermute(documents, "rows", behind) if step else documents

        def ahead(row, step=step):
            return lax.rem(row + step, n_rows)

        kernel = functools.partial(turned_kernel, shares, ahead)
        out_shape = [jax.ShapeDtypeStruct((rows // shares, docs), jnp.bfloat16)] * shares
        scratch = [pltpu.VMEM((rows, docs), jnp.float32)]
        total = direct_sum(scoring(kernel, out_shape, conditioned, query_ids, block, (), scratch))
        onward = [(row, (row + step) % n_rows) for row in range(n_rows)]
        result.append(lax.ppermute(total, "rows", onward) if step else total)
    return jnp.stack(result)


def local(train_grads, query_grads, eigenbases, eigenvalues, layer_offsets, query_doc_ids):
    conditioned = prepare(query_grads, eigenbases, eigenvalues, layer_offsets)
    on_line = lax.axis_size("rows") == 4 and lax.axis_size("layer") == 4
    plan = along_line if on_line else around_ring
    return plan(train_grads, conditioned, query_doc_ids[:, None])


def solution(mesh):
    in_specs = (
        P(("group", "rows"), "layer"),
        P(("group", "rows"), "layer"),
        P("layer", None, None),
        P("layer", None),
        P("layer"),
        P(("group", "rows")),
    )
    out_specs = P(None, "layer", ("group", "rows"))
    return jax.shard_map(local, mesh=mesh, in_specs=in_specs, out_specs=out_specs, check_vma=False)
```

```python
import functools

import jax
import jax.numpy as jnp
from jax import lax
from jax.experimental import pallas as pl
from jax.experimental.pallas import tpu as pltpu
from jax.sharding import PartitionSpec as P

LDIM = 512
LAY_DEV = 4
STEPS = 4
DAMPING = 0.05
NT = (((1,), (1,)), ((), ()))
MIB = 1024 * 1024


def layer_index():
    return lax.axis_index("layer").astype(jnp.int32)


def row_index():
    return lax.axis_index("rows").astype(jnp.int32)


def prepare_kernel(
    offsets, queries_hbm, bases_hbm, values_hbm, conditioned_ref, queries, bases, values, arrived
):
    copies = [pltpu.make_async_copy(values_hbm, values, arrived.at[0])]
    for layer in range(LAY_DEV):
        columns = queries_hbm.at[:, layer * LDIM : (layer + 1) * LDIM]
        copies.append(pltpu.make_async_copy(columns, queries.at[layer], arrived.at[1 + 2 * layer]))
        copies.append(pltpu.make_async_copy(bases_hbm.at[layer], bases.at[layer], arrived.at[2 + 2 * layer]))
    for copy in copies:
        copy.start()
    base_column = layer_index() * (LAY_DEV * LDIM)
    copies[0].wait()
    for layer in range(LAY_DEV):
        copies[1 + 2 * layer].wait()
        copies[2 + 2 * layer].wait()
        basis = bases[layer]
        projected = jnp.dot(queries[layer], basis, preferred_element_type=jnp.float32)
        scaled = (projected / (values[layer : layer + 1, :] + DAMPING)).astype(jnp.bfloat16)
        restored = lax.dot_general(scaled, basis, NT, preferred_element_type=jnp.float32)
        first = pl.multiple_of(offsets[layer] - base_column, LDIM)
        conditioned_ref[:, pl.ds(first, LDIM)] = restored.astype(jnp.bfloat16)


def prepare(queries, bases, values, offsets):
    rows, dims = queries.shape
    hbm = pl.BlockSpec(memory_space=pltpu.HBM)
    return pl.pallas_call(
        prepare_kernel,
        out_shape=jax.ShapeDtypeStruct((rows, dims), jnp.bfloat16),
        in_specs=[pl.BlockSpec(memory_space=pltpu.SMEM), hbm, hbm, hbm],
        out_specs=pl.BlockSpec(memory_space=pltpu.VMEM),
        scratch_shapes=[
            pltpu.VMEM((LAY_DEV, rows, LDIM), jnp.bfloat16),
            pltpu.VMEM(bases.shape, jnp.bfloat16),
            pltpu.VMEM(values.shape, jnp.float32),
            pltpu.SemaphoreType.DMA((1 + 2 * LAY_DEV,)),
        ],
        compiler_params=pltpu.CompilerParams(vmem_limit_bytes=62 * MIB),
        cost_estimate=pl.CostEstimate(
            flops=4 * rows * dims * LDIM, bytes_accessed=6 * MIB, transcendentals=0
        ),
    )(offsets, queries, bases, values)


def masked_tile(queries, documents, query_ids, block):
    tile = lax.dot_general(queries, documents, NT, preferred_element_type=jnp.float32)
    doc_ids = block * tile.shape[1] + lax.broadcasted_iota(jnp.int32, tile.shape, 1)
    return jnp.where(query_ids == doc_ids, 0.0, tile)


def scoring(kernel, out_shape, conditioned, query_ids, documents, extra=(), scratch=()):
    dims = conditioned.shape[1]
    docs = documents.shape[0]
    rows = sum(shape.shape[0] for shape in out_shape)
    vmem = pl.BlockSpec(memory_space=pltpu.VMEM)
    return pl.pallas_call(
        kernel,
        out_shape=out_shape,
        in_specs=[vmem] * (3 + len(extra)),
        out_specs=[vmem] * len(out_shape),
        scratch_shapes=scratch,
        compiler_params=pltpu.CompilerParams(vmem_limit_bytes=12 * MIB),
        cost_estimate=pl.CostEstimate(
            flops=2 * rows * docs * dims, bytes_accessed=2 * dims * (rows + docs), transcendentals=0
        ),
    )(conditioned, query_ids, documents, *extra)


def turned_kernel(shares, block_of, queries_ref, ids_ref, documents_ref, *refs):
    *out_refs, held = refs
    held[...] = masked_tile(queries_ref[...], documents_ref[...], ids_ref[...], block_of(row_index()))
    for turn, out_ref in enumerate(out_refs):
        share_rows = out_ref.shape[0]
        first = pl.multiple_of(lax.rem(layer_index() + turn, shares) * share_rows, share_rows)
        out_ref[...] = held[pl.ds(first, share_rows), :].astype(jnp.bfloat16)


def half_shares(share_rows, kept):
    core = lax.rem(layer_index(), 2)
    core = core if kept else 1 - core
    return [pl.multiple_of((2 * chip + core) * share_rows, share_rows) for chip in range(2)]


def halves_kernel(block_of, queries_ref, ids_ref, documents_ref, *refs):
    front_refs, out_refs, held = refs[:-3], refs[-3:-1], refs[-1]
    held[...] = masked_tile(queries_ref[...], documents_ref[...], ids_ref[...], block_of(row_index()))
    docs = documents_ref.shape[0]
    rows, width = out_refs[0].shape
    for side, kept in enumerate((True, False)):
        if front_refs:
            out_refs[side][:, : width - docs] = front_refs[side][...]
        for chip, first in enumerate(half_shares(rows // 2, kept)):
            spot = slice(chip * (rows // 2), (chip + 1) * (rows // 2))
            out_refs[side][spot, width - docs :] = held[pl.ds(first, rows // 2), :]


def target_chip():
    chip, core = lax.div(layer_index(), 2), lax.rem(layer_index(), 2)
    return jnp.where(chip == core, 0, 1)


def half_kernel(block_of, kept, queries_ref, ids_ref, documents_ref, out_ref):
    rows = out_ref.shape[0]
    chip = target_chip() if kept else 1 - target_chip()
    spot = pl.ds(pl.multiple_of(chip * rows, rows), rows)
    tile = masked_tile(queries_ref[spot, :], documents_ref[...], ids_ref[spot, :], block_of(row_index()))
    out_ref[...] = tile.astype(out_ref.dtype)


def total_of(refs):
    total = refs[0][...].astype(jnp.float32)
    for ref in refs[1:]:
        total += ref[...].astype(jnp.float32)
    return total


def sum_kernel(*refs):
    refs[-1][...] = total_of(refs[:-1]).astype(refs[-1].dtype)


def small_call(kernel, out_shape, *args):
    vmem = pl.BlockSpec(memory_space=pltpu.VMEM)
    return pl.pallas_call(
        kernel,
        out_shape=out_shape,
        in_specs=[vmem] * len(args),
        out_specs=[vmem] * len(out_shape),
        compiler_params=pltpu.CompilerParams(vmem_limit_bytes=4 * MIB),
    )(*args)


def direct_sum(tiles):
    shares = len(tiles)
    arrived = [tiles[0]]
    for turn in range(1, shares):
        pairs = [(lay, (lay + turn) % shares) for lay in range(shares)]
        arrived.append(lax.ppermute(tiles[turn], "layer", pairs))
    (total,) = small_call(sum_kernel, [jax.ShapeDtypeStruct(tiles[0].shape, jnp.float32)], *arrived)
    return total


def core_sum_kernel(kept_ref, arrived_ref, mine_ref, other_ref):
    rows = mine_ref.shape[0]
    chip = lax.div(layer_index(), 2)
    mine = pl.ds(pl.multiple_of(chip * rows, rows), rows)
    other = pl.ds(pl.multiple_of((1 - chip) * rows, rows), rows)
    mine_ref[...] = (kept_ref[mine, :] + arrived_ref[mine, :]).astype(mine_ref.dtype)
    other_ref[...] = (kept_ref[other, :] + arrived_ref[other, :]).astype(other_ref.dtype)


def chip_sum_kernel(mine_ref, arrived_ref, *out_refs):
    docs = out_refs[0].shape[1]
    for spot, out_ref in enumerate(out_refs):
        columns = slice(spot * docs, (spot + 1) * docs)
        total = mine_ref[:, columns] + arrived_ref[:, columns].astype(jnp.float32)
        out_ref[...] = total.astype(out_ref.dtype)


def swap(value, distance):
    count = lax.axis_size("layer")
    return lax.ppermute(value, "layer", [(lay, lay ^ distance) for lay in range(count)])


def core_sum(kept, arrived, mine_type):
    rows, width = kept.shape[0] // 2, kept.shape[1]
    out_shape = [jax.ShapeDtypeStruct((rows, width), out_type) for out_type in (mine_type, jnp.bfloat16)]
    return small_call(core_sum_kernel, out_shape, kept, arrived)


def layer_sum(kept, sent, out_types):
    mine, other = core_sum(kept, swap(sent, 1), jnp.float32)
    rows, docs = mine.shape[0], mine.shape[1] // len(out_types)
    out_shape = [jax.ShapeDtypeStruct((rows, docs), out_type) for out_type in out_types]
    return small_call(chip_sum_kernel, out_shape, mine, swap(other, 2))


ROUND_ONE = ((0, 2), (2, 3), (3, 1), (1, 0))
ROUND_TWO = ((0, 1), (1, 3), (3, 2), (2, 0))
BLOCK_ONE = (1, 3, 0, 2)
BLOCK_TWO = (2, 0, 3, 1)
BLOCK_LAST = (3, 2, 1, 0)


def pick(table):
    def entry(row):
        value = jnp.int32(table[0])
        for index in range(1, len(table)):
            value = jnp.where(row == index, jnp.int32(table[index]), value)
        return value

    return entry


def step_of(table):
    return pick([(block - table.index(block)) % STEPS for block in range(STEPS)])


def assemble_kernel(own_ref, first_ref, second_ref, out_ref):
    out_ref[0] = own_ref[...]
    for ref, table in ((first_ref, BLOCK_ONE), (second_ref, BLOCK_TWO)):
        out_ref[step_of(table)(row_index())] = ref[...].astype(jnp.float32)


def core_share(rows, own):
    core = lax.rem(layer_index(), 2)
    return pl.ds(pl.multiple_of((core if own else 1 - core) * rows, rows), rows)


def other_share_kernel(mine_ref, out_ref):
    out_ref[...] = mine_ref[core_share(out_ref.shape[0], False), :]


def finish_kernel(mine_ref, arrived_ref, scores_hbm, out_hbm, total, copied):
    del scores_hbm
    mine = mine_ref[core_share(total.shape[0], True), :].astype(jnp.float32)
    total[...] = mine + arrived_ref[...].astype(jnp.float32)
    copy = pltpu.make_async_copy(total, out_hbm.at[step_of(BLOCK_LAST)(row_index())], copied)
    copy.start()
    copy.wait()


def finish(mine, arrived, scores):
    hbm = pl.BlockSpec(memory_space=pltpu.HBM)
    vmem = pl.BlockSpec(memory_space=pltpu.VMEM)
    return pl.pallas_call(
        finish_kernel,
        out_shape=jax.ShapeDtypeStruct(scores.shape, scores.dtype),
        in_specs=[vmem, vmem, hbm],
        out_specs=hbm,
        scratch_shapes=[pltpu.VMEM(scores.shape[1:], jnp.float32), pltpu.SemaphoreType.DMA],
        input_output_aliases={2: 0},
        compiler_params=pltpu.CompilerParams(vmem_limit_bytes=4 * MIB),
    )(mine, arrived, scores)


def along_line(documents, conditioned, query_ids):
    docs = documents.shape[0]
    half = (conditioned.shape[0] // 2, docs)

    def halves(block, block_of, front=()):
        width = docs * (1 + bool(front))
        out_shape = [jax.ShapeDtypeStruct((half[0], width), jnp.float32)] * 2
        scratch = [pltpu.VMEM((2 * half[0], docs), jnp.float32)]
        kernel = functools.partial(halves_kernel, block_of)
        return scoring(kernel, out_shape, conditioned, query_ids, block, front, scratch)

    def one_half(block, block_of, kept):
        kernel = functools.partial(half_kernel, block_of, kept)
        out_shape = [jax.ShapeDtypeStruct(half, jnp.float32 if kept else jnp.bfloat16)]
        return scoring(kernel, out_shape, conditioned, query_ids, block)[0]

    def back(total, table):
        return lax.ppermute(total, "rows", tuple(enumerate(table)))

    one = lax.ppermute(documents, "rows", ROUND_ONE)
    later, conditioned = lax.optimization_barrier((documents, conditioned))
    two = lax.ppermute(later, "rows", ROUND_TWO)
    own = halves(later, lambda row: row)
    one, own = lax.optimization_barrier((one, own))
    three = lax.ppermute(one, "rows", ROUND_ONE)

    own, first = layer_sum(*halves(one, pick(BLOCK_ONE), own), (jnp.float32, jnp.bfloat16))
    two, first = lax.optimization_barrier((two, first))
    first = back(first, BLOCK_ONE)
    (second,) = layer_sum(*halves(two, pick(BLOCK_TWO)), (jnp.bfloat16,))
    second = back(second, BLOCK_TWO)
    three, first, second = lax.optimization_barrier((three, first, second))

    arrived = swap(one_half(three, pick(BLOCK_LAST), False), 1)
    kept = one_half(three, pick(BLOCK_LAST), True)
    (both,) = small_call(sum_kernel, [jax.ShapeDtypeStruct(half, jnp.bfloat16)], kept, arrived)
    shares = lax.axis_size("layer")
    pairs = [
        (row * shares + lay, BLOCK_LAST[row] * shares + 2 * ((lay // 2) ^ (lay % 2)) + lay % 2)
        for row in range(len(BLOCK_LAST))
        for lay in range(shares)
    ]
    mine = lax.ppermute(both, ("rows", "layer"), pairs)
    out_shape = [jax.ShapeDtypeStruct((STEPS,) + own.shape, jnp.float32)]
    (scores,) = small_call(assemble_kernel, out_shape, own, first, second)
    (other,) = small_call(other_share_kernel, [jax.ShapeDtypeStruct(own.shape, jnp.bfloat16)], mine)
    return finish(mine, swap(other, 1), scores)


def around_ring(documents, conditioned, query_ids):
    n_rows, shares = lax.axis_size("rows"), lax.axis_size("layer")
    rows, docs = conditioned.shape[0], documents.shape[0]
    result = []
    for step in range(STEPS):
        behind = [(row, (row - step) % n_rows) for row in range(n_rows)]
        block = lax.ppermute(documents, "rows", behind) if step else documents

        def ahead(row, step=step):
            return lax.rem(row + step, n_rows)

        kernel = functools.partial(turned_kernel, shares, ahead)
        out_shape = [jax.ShapeDtypeStruct((rows // shares, docs), jnp.bfloat16)] * shares
        scratch = [pltpu.VMEM((rows, docs), jnp.float32)]
        total = direct_sum(scoring(kernel, out_shape, conditioned, query_ids, block, (), scratch))
        onward = [(row, (row + step) % n_rows) for row in range(n_rows)]
        result.append(lax.ppermute(total, "rows", onward) if step else total)
    return jnp.stack(result)


def local(train_grads, query_grads, eigenbases, eigenvalues, layer_offsets, query_doc_ids):
    conditioned = prepare(query_grads, eigenbases, eigenvalues, layer_offsets)
    on_line = lax.axis_size("rows") == 4 and lax.axis_size("layer") == 4
    plan = along_line if on_line else around_ring
    return plan(train_grads, conditioned, query_doc_ids[:, None])


def solution(mesh):
    in_specs = (
        P(("group", "rows"), "layer"),
        P(("group", "rows"), "layer"),
        P("layer", None, None),
        P("layer", None),
        P("layer"),
        P(("group", "rows")),
    )
    out_specs = P(None, "layer", ("group", "rows"))
    return jax.shard_map(local, mesh=mesh, in_specs=in_specs, out_specs=out_specs, check_vma=False)
```

```python
import functools

import jax
import jax.numpy as jnp
from jax import lax
from jax.experimental import pallas as pl
from jax.experimental.pallas import tpu as pltpu
from jax.sharding import PartitionSpec as P

LDIM = 512
LAY_DEV = 4
STEPS = 4
DAMPING = 0.05
NT = (((1,), (1,)), ((), ()))
MIB = 1024 * 1024


def layer_index():
    return lax.axis_index("layer").astype(jnp.int32)


def row_index():
    return lax.axis_index("rows").astype(jnp.int32)


def prepare_kernel(
    offsets, queries_hbm, bases_hbm, values_hbm, conditioned_ref, queries, bases, values, arrived
):
    copies = [pltpu.make_async_copy(values_hbm, values, arrived.at[0])]
    for layer in range(LAY_DEV):
        columns = queries_hbm.at[:, layer * LDIM : (layer + 1) * LDIM]
        copies.append(pltpu.make_async_copy(columns, queries.at[layer], arrived.at[1 + 2 * layer]))
        copies.append(pltpu.make_async_copy(bases_hbm.at[layer], bases.at[layer], arrived.at[2 + 2 * layer]))
    for copy in copies:
        copy.start()
    base_column = layer_index() * (LAY_DEV * LDIM)
    copies[0].wait()
    for layer in range(LAY_DEV):
        copies[1 + 2 * layer].wait()
        copies[2 + 2 * layer].wait()
        basis = bases[layer]
        projected = jnp.dot(queries[layer], basis, preferred_element_type=jnp.float32)
        scaled = (projected / (values[layer : layer + 1, :] + DAMPING)).astype(jnp.bfloat16)
        restored = lax.dot_general(scaled, basis, NT, preferred_element_type=jnp.float32)
        first = pl.multiple_of(offsets[layer] - base_column, LDIM)
        conditioned_ref[:, pl.ds(first, LDIM)] = restored.astype(jnp.bfloat16)


def prepare(queries, bases, values, offsets):
    rows, dims = queries.shape
    hbm = pl.BlockSpec(memory_space=pltpu.HBM)
    return pl.pallas_call(
        prepare_kernel,
        out_shape=jax.ShapeDtypeStruct((rows, dims), jnp.bfloat16),
        in_specs=[pl.BlockSpec(memory_space=pltpu.SMEM), hbm, hbm, hbm],
        out_specs=pl.BlockSpec(memory_space=pltpu.VMEM),
        scratch_shapes=[
            pltpu.VMEM((LAY_DEV, rows, LDIM), jnp.bfloat16),
            pltpu.VMEM(bases.shape, jnp.bfloat16),
            pltpu.VMEM(values.shape, jnp.float32),
            pltpu.SemaphoreType.DMA((1 + 2 * LAY_DEV,)),
        ],
        compiler_params=pltpu.CompilerParams(vmem_limit_bytes=62 * MIB),
        cost_estimate=pl.CostEstimate(
            flops=4 * rows * dims * LDIM, bytes_accessed=6 * MIB, transcendentals=0
        ),
    )(offsets, queries, bases, values)


def masked_tile(queries, documents, query_ids, block):
    tile = lax.dot_general(queries, documents, NT, preferred_element_type=jnp.float32)
    doc_ids = block * tile.shape[1] + lax.broadcasted_iota(jnp.int32, tile.shape, 1)
    return jnp.where(query_ids == doc_ids, 0.0, tile)


def scoring(kernel, out_shape, conditioned, query_ids, documents, extra=(), scratch=(), weight=1):
    dims = conditioned.shape[1]
    docs = documents.shape[0]
    rows = sum(shape.shape[0] for shape in out_shape)
    vmem = pl.BlockSpec(memory_space=pltpu.VMEM)
    return pl.pallas_call(
        kernel,
        out_shape=out_shape,
        in_specs=[vmem] * (3 + len(extra)),
        out_specs=[vmem] * len(out_shape),
        scratch_shapes=scratch,
        compiler_params=pltpu.CompilerParams(vmem_limit_bytes=12 * MIB),
        cost_estimate=pl.CostEstimate(
            flops=2 * rows * docs * dims * weight, bytes_accessed=2 * dims * (rows + docs) * weight, transcendentals=0
        ),
    )(conditioned, query_ids, documents, *extra)


def turned_kernel(shares, block_of, queries_ref, ids_ref, documents_ref, *refs):
    *out_refs, held = refs
    held[...] = masked_tile(queries_ref[...], documents_ref[...], ids_ref[...], block_of(row_index()))
    for turn, out_ref in enumerate(out_refs):
        share_rows = out_ref.shape[0]
        first = pl.multiple_of(lax.rem(layer_index() + turn, shares) * share_rows, share_rows)
        out_ref[...] = held[pl.ds(first, share_rows), :].astype(jnp.bfloat16)


def half_shares(share_rows, kept):
    core = lax.rem(layer_index(), 2)
    core = core if kept else 1 - core
    return [pl.multiple_of((2 * chip + core) * share_rows, share_rows) for chip in range(2)]


def halves_kernel(block_of, queries_ref, ids_ref, documents_ref, *refs):
    front_refs, out_refs, held = refs[:-3], refs[-3:-1], refs[-1]
    held[...] = masked_tile(queries_ref[...], documents_ref[...], ids_ref[...], block_of(row_index()))
    docs = documents_ref.shape[0]
    rows, width = out_refs[0].shape
    for side, kept in enumerate((True, False)):
        if front_refs:
            out_refs[side][:, : width - docs] = front_refs[side][...]
        for chip, first in enumerate(half_shares(rows // 2, kept)):
            spot = slice(chip * (rows // 2), (chip + 1) * (rows // 2))
            out_refs[side][spot, width - docs :] = held[pl.ds(first, rows // 2), :]


def target_chip():
    chip, core = lax.div(layer_index(), 2), lax.rem(layer_index(), 2)
    return jnp.where(chip == core, 0, 1)


def half_kernel(block_of, kept, queries_ref, ids_ref, documents_ref, out_ref):
    rows = out_ref.shape[0]
    chip = target_chip() if kept else 1 - target_chip()
    spot = pl.ds(pl.multiple_of(chip * rows, rows), rows)
    out_ref[...] = masked_tile(queries_ref[spot, :], documents_ref[...], ids_ref[spot, :], block_of(row_index()))


def total_of(refs):
    total = refs[0][...].astype(jnp.float32)
    for ref in refs[1:]:
        total += ref[...].astype(jnp.float32)
    return total


def sum_kernel(*refs):
    refs[-1][...] = total_of(refs[:-1]).astype(refs[-1].dtype)


def small_call(kernel, out_shape, *args):
    vmem = pl.BlockSpec(memory_space=pltpu.VMEM)
    return pl.pallas_call(
        kernel,
        out_shape=out_shape,
        in_specs=[vmem] * len(args),
        out_specs=[vmem] * len(out_shape),
        compiler_params=pltpu.CompilerParams(vmem_limit_bytes=4 * MIB),
    )(*args)


def direct_sum(tiles):
    shares = len(tiles)
    arrived = [tiles[0]]
    for turn in range(1, shares):
        pairs = [(lay, (lay + turn) % shares) for lay in range(shares)]
        arrived.append(lax.ppermute(tiles[turn], "layer", pairs))
    (total,) = small_call(sum_kernel, [jax.ShapeDtypeStruct(tiles[0].shape, jnp.float32)], *arrived)
    return total


def core_sum_kernel(kept_ref, arrived_ref, mine_ref, other_ref):
    rows = mine_ref.shape[0]
    chip = lax.div(layer_index(), 2)
    mine = pl.ds(pl.multiple_of(chip * rows, rows), rows)
    other = pl.ds(pl.multiple_of((1 - chip) * rows, rows), rows)
    mine_ref[...] = (kept_ref[mine, :] + arrived_ref[mine, :]).astype(mine_ref.dtype)
    other_ref[...] = (kept_ref[other, :] + arrived_ref[other, :]).astype(other_ref.dtype)


def chip_sum_kernel(mine_ref, arrived_ref, *out_refs):
    docs = out_refs[0].shape[1]
    for spot, out_ref in enumerate(out_refs):
        columns = slice(spot * docs, (spot + 1) * docs)
        total = mine_ref[:, columns] + arrived_ref[:, columns].astype(jnp.float32)
        out_ref[...] = total.astype(out_ref.dtype)


def swap(value, distance):
    count = lax.axis_size("layer")
    return lax.ppermute(value, "layer", [(lay, lay ^ distance) for lay in range(count)])


def core_sum(kept, arrived, mine_type):
    rows, width = kept.shape[0] // 2, kept.shape[1]
    out_shape = [jax.ShapeDtypeStruct((rows, width), out_type) for out_type in (mine_type, jnp.bfloat16)]
    return small_call(core_sum_kernel, out_shape, kept, arrived)


def layer_sum(kept, sent, out_types):
    mine, other = core_sum(kept, swap(sent, 1), jnp.float32)
    rows, docs = mine.shape[0], mine.shape[1] // len(out_types)
    out_shape = [jax.ShapeDtypeStruct((rows, docs), out_type) for out_type in out_types]
    return small_call(chip_sum_kernel, out_shape, mine, swap(other, 2))


ROUND_ONE = ((0, 2), (2, 3), (3, 1), (1, 0))
ROUND_TWO = ((0, 1), (1, 3), (3, 2), (2, 0))
BLOCK_ONE = (1, 3, 0, 2)
BLOCK_TWO = (2, 0, 3, 1)
BLOCK_LAST = (3, 2, 1, 0)


def pick(table):
    def entry(row):
        value = jnp.int32(table[0])
        for index in range(1, len(table)):
            value = jnp.where(row == index, jnp.int32(table[index]), value)
        return value

    return entry


def step_of(table):
    return pick([(block - table.index(block)) % STEPS for block in range(STEPS)])


def assemble_kernel(own_ref, first_ref, second_ref, out_ref):
    out_ref[0] = own_ref[...]
    for ref, table in ((first_ref, BLOCK_ONE), (second_ref, BLOCK_TWO)):
        out_ref[step_of(table)(row_index())] = ref[...].astype(jnp.float32)


def finish_kernel(mine_ref, arrived_ref, scores_hbm, out_hbm, total, copied):
    del scores_hbm
    rows = total.shape[0]
    share = pl.ds(pl.multiple_of(lax.rem(layer_index(), 2) * rows, rows), rows)
    total[...] = mine_ref[share, :].astype(jnp.float32) + arrived_ref[share, :].astype(jnp.float32)
    copy = pltpu.make_async_copy(total, out_hbm.at[step_of(BLOCK_LAST)(row_index())], copied)
    copy.start()
    copy.wait()


def finish(mine, arrived, scores):
    hbm = pl.BlockSpec(memory_space=pltpu.HBM)
    vmem = pl.BlockSpec(memory_space=pltpu.VMEM)
    return pl.pallas_call(
        finish_kernel,
        out_shape=jax.ShapeDtypeStruct(scores.shape, scores.dtype),
        in_specs=[vmem, vmem, hbm],
        out_specs=hbm,
        scratch_shapes=[pltpu.VMEM(scores.shape[1:], jnp.float32), pltpu.SemaphoreType.DMA],
        input_output_aliases={2: 0},
        compiler_params=pltpu.CompilerParams(vmem_limit_bytes=4 * MIB),
    )(mine, arrived, scores)


def along_line(documents, conditioned, query_ids):
    docs = documents.shape[0]
    half = (conditioned.shape[0] // 2, docs)

    def halves(block, block_of, front=()):
        width = docs * (1 + bool(front))
        out_shape = [jax.ShapeDtypeStruct((half[0], width), jnp.float32)] * 2
        scratch = [pltpu.VMEM((2 * half[0], docs), jnp.float32)]
        kernel = functools.partial(halves_kernel, block_of)
        return scoring(kernel, out_shape, conditioned, query_ids, block, front, scratch)

    def one_half(block, block_of, kept):
        kernel = functools.partial(half_kernel, block_of, kept)
        out_shape = [jax.ShapeDtypeStruct(half, jnp.float32)]
        weight = 8 if kept else 1
        return scoring(kernel, out_shape, conditioned, query_ids, block, weight=weight)[0]

    def back(total, table):
        return lax.ppermute(total, "rows", tuple(enumerate(table)))

    one = lax.ppermute(documents, "rows", ROUND_ONE)
    later, conditioned = lax.optimization_barrier((documents, conditioned))
    two = lax.ppermute(later, "rows", ROUND_TWO)
    own = halves(later, lambda row: row)
    one, own = lax.optimization_barrier((one, own))
    three = lax.ppermute(one, "rows", ROUND_ONE)

    own, first = layer_sum(*halves(one, pick(BLOCK_ONE), own), (jnp.float32, jnp.bfloat16))
    two, first = lax.optimization_barrier((two, first))
    (second,) = layer_sum(*halves(two, pick(BLOCK_TWO)), (jnp.bfloat16,))
    three, *_ = lax.optimization_barrier((three, first, second))
    first, second = back(first, BLOCK_ONE), back(second, BLOCK_TWO)

    arrived = swap(one_half(three, pick(BLOCK_LAST), False), 1)
    three, first, second = lax.optimization_barrier((three, first, second))
    kept = one_half(three, pick(BLOCK_LAST), True)
    (both,) = small_call(sum_kernel, [jax.ShapeDtypeStruct(half, jnp.bfloat16)], kept, arrived)
    shares = lax.axis_size("layer")
    pairs = [
        (row * shares + lay, BLOCK_LAST[row] * shares + 2 * ((lay // 2) ^ (lay % 2)) + lay % 2)
        for row in range(len(BLOCK_LAST))
        for lay in range(shares)
    ]
    mine = lax.ppermute(both, ("rows", "layer"), pairs)
    out_shape = [jax.ShapeDtypeStruct((STEPS,) + own.shape, jnp.float32)]
    (scores,) = small_call(assemble_kernel, out_shape, own, first, second)
    return finish(mine, swap(mine, 1), scores)


def around_ring(documents, conditioned, query_ids):
    n_rows, shares = lax.axis_size("rows"), lax.axis_size("layer")
    rows, docs = conditioned.shape[0], documents.shape[0]
    result = []
    for step in range(STEPS):
        behind = [(row, (row - step) % n_rows) for row in range(n_rows)]
        block = lax.ppermute(documents, "rows", behind) if step else documents

        def ahead(row, step=step):
            return lax.rem(row + step, n_rows)

        kernel = functools.partial(turned_kernel, shares, ahead)
        out_shape = [jax.ShapeDtypeStruct((rows // shares, docs), jnp.bfloat16)] * shares
        scratch = [pltpu.VMEM((rows, docs), jnp.float32)]
        total = direct_sum(scoring(kernel, out_shape, conditioned, query_ids, block, (), scratch))
        onward = [(row, (row + step) % n_rows) for row in range(n_rows)]
        result.append(lax.ppermute(total, "rows", onward) if step else total)
    return jnp.stack(result)


def local(train_grads, query_grads, eigenbases, eigenvalues, layer_offsets, query_doc_ids):
    conditioned = prepare(query_grads, eigenbases, eigenvalues, layer_offsets)
    on_line = lax.axis_size("rows") == 4 and lax.axis_size("layer") == 4
    plan = along_line if on_line else around_ring
    return plan(train_grads, conditioned, query_doc_ids[:, None])


def solution(mesh):
    in_specs = (
        P(("group", "rows"), "layer"),
        P(("group", "rows"), "layer"),
        P("layer", None, None),
        P("layer", None),
        P("layer"),
        P(("group", "rows")),
    )
    out_specs = P(None, "layer", ("group", "rows"))
    return jax.shard_map(local, mesh=mesh, in_specs=in_specs, out_specs=out_specs, check_vma=False)
```

```python
import functools

import jax
import jax.numpy as jnp
from jax import lax
from jax.experimental import pallas as pl
from jax.experimental.pallas import tpu as pltpu
from jax.sharding import PartitionSpec as P

LDIM = 512
LAY_DEV = 4
STEPS = 4
DAMPING = 0.05
NT = (((1,), (1,)), ((), ()))
MIB = 1024 * 1024


def layer_index():
    return lax.axis_index("layer").astype(jnp.int32)


def row_index():
    return lax.axis_index("rows").astype(jnp.int32)


def prepare_kernel(
    offsets, queries_hbm, bases_hbm, values_hbm, conditioned_ref, queries, bases, values, arrived
):
    copies = [pltpu.make_async_copy(values_hbm, values, arrived.at[0])]
    for layer in range(LAY_DEV):
        columns = queries_hbm.at[:, layer * LDIM : (layer + 1) * LDIM]
        copies.append(pltpu.make_async_copy(columns, queries.at[layer], arrived.at[1 + 2 * layer]))
        copies.append(pltpu.make_async_copy(bases_hbm.at[layer], bases.at[layer], arrived.at[2 + 2 * layer]))
    for copy in copies:
        copy.start()
    base_column = layer_index() * (LAY_DEV * LDIM)
    copies[0].wait()
    for layer in range(LAY_DEV):
        copies[1 + 2 * layer].wait()
        copies[2 + 2 * layer].wait()
        basis = bases[layer]
        projected = jnp.dot(queries[layer], basis, preferred_element_type=jnp.float32)
        scaled = (projected / (values[layer : layer + 1, :] + DAMPING)).astype(jnp.bfloat16)
        restored = lax.dot_general(scaled, basis, NT, preferred_element_type=jnp.float32)
        first = pl.multiple_of(offsets[layer] - base_column, LDIM)
        conditioned_ref[:, pl.ds(first, LDIM)] = restored.astype(jnp.bfloat16)


def prepare(queries, bases, values, offsets):
    rows, dims = queries.shape
    hbm = pl.BlockSpec(memory_space=pltpu.HBM)
    return pl.pallas_call(
        prepare_kernel,
        out_shape=jax.ShapeDtypeStruct((rows, dims), jnp.bfloat16),
        in_specs=[pl.BlockSpec(memory_space=pltpu.SMEM), hbm, hbm, hbm],
        out_specs=pl.BlockSpec(memory_space=pltpu.VMEM),
        scratch_shapes=[
            pltpu.VMEM((LAY_DEV, rows, LDIM), jnp.bfloat16),
            pltpu.VMEM(bases.shape, jnp.bfloat16),
            pltpu.VMEM(values.shape, jnp.float32),
            pltpu.SemaphoreType.DMA((1 + 2 * LAY_DEV,)),
        ],
        compiler_params=pltpu.CompilerParams(vmem_limit_bytes=62 * MIB),
        cost_estimate=pl.CostEstimate(
            flops=4 * rows * dims * LDIM, bytes_accessed=6 * MIB, transcendentals=0
        ),
    )(offsets, queries, bases, values)


def masked_tile(queries, documents, query_ids, block):
    tile = lax.dot_general(queries, documents, NT, preferred_element_type=jnp.float32)
    doc_ids = block * tile.shape[1] + lax.broadcasted_iota(jnp.int32, tile.shape, 1)
    return jnp.where(query_ids == doc_ids, 0.0, tile)


def scoring(kernel, out_shape, conditioned, query_ids, documents, extra=(), scratch=(), weight=1):
    dims = conditioned.shape[1]
    docs = documents.shape[0]
    rows = sum(shape.shape[0] for shape in out_shape)
    vmem = pl.BlockSpec(memory_space=pltpu.VMEM)
    return pl.pallas_call(
        kernel,
        out_shape=out_shape,
        in_specs=[vmem] * (3 + len(extra)),
        out_specs=[vmem] * len(out_shape),
        scratch_shapes=scratch,
        compiler_params=pltpu.CompilerParams(vmem_limit_bytes=12 * MIB),
        cost_estimate=pl.CostEstimate(
            flops=2 * rows * docs * dims * weight, bytes_accessed=2 * dims * (rows + docs) * weight, transcendentals=0
        ),
    )(conditioned, query_ids, documents, *extra)


def turned_kernel(shares, block_of, queries_ref, ids_ref, documents_ref, *refs):
    *out_refs, held = refs
    held[...] = masked_tile(queries_ref[...], documents_ref[...], ids_ref[...], block_of(row_index()))
    for turn, out_ref in enumerate(out_refs):
        share_rows = out_ref.shape[0]
        first = pl.multiple_of(lax.rem(layer_index() + turn, shares) * share_rows, share_rows)
        out_ref[...] = held[pl.ds(first, share_rows), :].astype(jnp.bfloat16)


def half_shares(share_rows, kept):
    core = lax.rem(layer_index(), 2)
    core = core if kept else 1 - core
    return [pl.multiple_of((2 * chip + core) * share_rows, share_rows) for chip in range(2)]


def halves_kernel(block_of, queries_ref, ids_ref, documents_ref, *refs):
    front_refs, out_refs, held = refs[:-3], refs[-3:-1], refs[-1]
    held[...] = masked_tile(queries_ref[...], documents_ref[...], ids_ref[...], block_of(row_index()))
    docs = documents_ref.shape[0]
    rows, width = out_refs[0].shape
    for side, kept in enumerate((True, False)):
        if front_refs:
            out_refs[side][:, : width - docs] = front_refs[side][...]
        for chip, first in enumerate(half_shares(rows // 2, kept)):
            spot = slice(chip * (rows // 2), (chip + 1) * (rows // 2))
            out_refs[side][spot, width - docs :] = held[pl.ds(first, rows // 2), :]


def target_chip():
    chip, core = lax.div(layer_index(), 2), lax.rem(layer_index(), 2)
    return jnp.where(chip == core, 0, 1)


def half_kernel(block_of, kept, queries_ref, ids_ref, documents_ref, out_ref):
    rows = out_ref.shape[0]
    chip = target_chip() if kept else 1 - target_chip()
    spot = pl.ds(pl.multiple_of(chip * rows, rows), rows)
    tile = masked_tile(queries_ref[spot, :], documents_ref[...], ids_ref[spot, :], block_of(row_index()))
    out_ref[...] = tile.astype(out_ref.dtype)


def total_of(refs):
    total = refs[0][...].astype(jnp.float32)
    for ref in refs[1:]:
        total += ref[...].astype(jnp.float32)
    return total


def sum_kernel(*refs):
    refs[-1][...] = total_of(refs[:-1]).astype(refs[-1].dtype)


def small_call(kernel, out_shape, *args):
    vmem = pl.BlockSpec(memory_space=pltpu.VMEM)
    return pl.pallas_call(
        kernel,
        out_shape=out_shape,
        in_specs=[vmem] * len(args),
        out_specs=[vmem] * len(out_shape),
        compiler_params=pltpu.CompilerParams(vmem_limit_bytes=4 * MIB),
    )(*args)


def direct_sum(tiles):
    shares = len(tiles)
    arrived = [tiles[0]]
    for turn in range(1, shares):
        pairs = [(lay, (lay + turn) % shares) for lay in range(shares)]
        arrived.append(lax.ppermute(tiles[turn], "layer", pairs))
    (total,) = small_call(sum_kernel, [jax.ShapeDtypeStruct(tiles[0].shape, jnp.float32)], *arrived)
    return total


def core_sum_kernel(kept_ref, arrived_ref, mine_ref, other_ref):
    rows = mine_ref.shape[0]
    chip = lax.div(layer_index(), 2)
    mine = pl.ds(pl.multiple_of(chip * rows, rows), rows)
    other = pl.ds(pl.multiple_of((1 - chip) * rows, rows), rows)
    mine_ref[...] = (kept_ref[mine, :] + arrived_ref[mine, :]).astype(mine_ref.dtype)
    other_ref[...] = (kept_ref[other, :] + arrived_ref[other, :]).astype(other_ref.dtype)


def chip_sum_kernel(mine_ref, arrived_ref, *out_refs):
    docs = out_refs[0].shape[1]
    for spot, out_ref in enumerate(out_refs):
        columns = slice(spot * docs, (spot + 1) * docs)
        total = mine_ref[:, columns] + arrived_ref[:, columns].astype(jnp.float32)
        out_ref[...] = total.astype(out_ref.dtype)


def swap(value, distance):
    count = lax.axis_size("layer")
    return lax.ppermute(value, "layer", [(lay, lay ^ distance) for lay in range(count)])


def core_sum(kept, arrived, mine_type):
    rows, width = kept.shape[0] // 2, kept.shape[1]
    out_shape = [jax.ShapeDtypeStruct((rows, width), out_type) for out_type in (mine_type, jnp.bfloat16)]
    return small_call(core_sum_kernel, out_shape, kept, arrived)


def layer_sum(kept, sent, out_types):
    mine, other = core_sum(kept, swap(sent, 1), jnp.float32)
    rows, docs = mine.shape[0], mine.shape[1] // len(out_types)
    out_shape = [jax.ShapeDtypeStruct((rows, docs), out_type) for out_type in out_types]
    return small_call(chip_sum_kernel, out_shape, mine, swap(other, 2))


ROUND_ONE = ((0, 2), (2, 3), (3, 1), (1, 0))
ROUND_TWO = ((0, 1), (1, 3), (3, 2), (2, 0))
BLOCK_ONE = (1, 3, 0, 2)
BLOCK_TWO = (2, 0, 3, 1)
BLOCK_LAST = (3, 2, 1, 0)


def pick(table):
    def entry(row):
        value = jnp.int32(table[0])
        for index in range(1, len(table)):
            value = jnp.where(row == index, jnp.int32(table[index]), value)
        return value

    return entry


def step_of(table):
    return pick([(block - table.index(block)) % STEPS for block in range(STEPS)])


def assemble_kernel(own_ref, first_ref, second_ref, out_ref):
    out_ref[0] = own_ref[...]
    for ref, table in ((first_ref, BLOCK_ONE), (second_ref, BLOCK_TWO)):
        out_ref[step_of(table)(row_index())] = ref[...].astype(jnp.float32)


def core_share(rows, own):
    core = lax.rem(layer_index(), 2)
    return pl.ds(pl.multiple_of((core if own else 1 - core) * rows, rows), rows)


def other_share_kernel(mine_ref, out_ref):
    out_ref[...] = mine_ref[core_share(out_ref.shape[0], False), :]


def finish_kernel(mine_ref, arrived_ref, scores_hbm, out_hbm, total, copied):
    del scores_hbm
    mine = mine_ref[core_share(total.shape[0], True), :].astype(jnp.float32)
    total[...] = mine + arrived_ref[...].astype(jnp.float32)
    copy = pltpu.make_async_copy(total, out_hbm.at[step_of(BLOCK_LAST)(row_index())], copied)
    copy.start()
    copy.wait()


def finish(mine, arrived, scores):
    hbm = pl.BlockSpec(memory_space=pltpu.HBM)
    vmem = pl.BlockSpec(memory_space=pltpu.VMEM)
    return pl.pallas_call(
        finish_kernel,
        out_shape=jax.ShapeDtypeStruct(scores.shape, scores.dtype),
        in_specs=[vmem, vmem, hbm],
        out_specs=hbm,
        scratch_shapes=[pltpu.VMEM(scores.shape[1:], jnp.float32), pltpu.SemaphoreType.DMA],
        input_output_aliases={2: 0},
        compiler_params=pltpu.CompilerParams(vmem_limit_bytes=4 * MIB),
    )(mine, arrived, scores)


def along_line(documents, conditioned, query_ids):
    docs = documents.shape[0]
    half = (conditioned.shape[0] // 2, docs)

    def halves(block, block_of, front=()):
        width = docs * (1 + bool(front))
        out_shape = [jax.ShapeDtypeStruct((half[0], width), jnp.float32)] * 2
        scratch = [pltpu.VMEM((2 * half[0], docs), jnp.float32)]
        kernel = functools.partial(halves_kernel, block_of)
        return scoring(kernel, out_shape, conditioned, query_ids, block, front, scratch)

    def one_half(block, block_of, kept):
        kernel = functools.partial(half_kernel, block_of, kept)
        out_shape = [jax.ShapeDtypeStruct(half, jnp.float32 if kept else jnp.bfloat16)]
        weight = 5 if kept else 1
        return scoring(kernel, out_shape, conditioned, query_ids, block, weight=weight)[0]

    def back(total, table):
        return lax.ppermute(total, "rows", tuple(enumerate(table)))

    one = lax.ppermute(documents, "rows", ROUND_ONE)
    later, conditioned = lax.optimization_barrier((documents, conditioned))
    two = lax.ppermute(later, "rows", ROUND_TWO)
    own = halves(later, lambda row: row)
    one, own = lax.optimization_barrier((one, own))
    three = lax.ppermute(one, "rows", ROUND_ONE)

    own, first = layer_sum(*halves(one, pick(BLOCK_ONE), own), (jnp.float32, jnp.bfloat16))
    two, first = lax.optimization_barrier((two, first))
    (second,) = layer_sum(*halves(two, pick(BLOCK_TWO)), (jnp.bfloat16,))
    three, *_ = lax.optimization_barrier((three, first, second))
    first, second = back(first, BLOCK_ONE), back(second, BLOCK_TWO)

    arrived = swap(one_half(three, pick(BLOCK_LAST), False), 1)
    three, first, second = lax.optimization_barrier((three, first, second))
    kept = one_half(three, pick(BLOCK_LAST), True)
    (both,) = small_call(sum_kernel, [jax.ShapeDtypeStruct(half, jnp.bfloat16)], kept, arrived)
    shares = lax.axis_size("layer")
    pairs = [
        (row * shares + lay, BLOCK_LAST[row] * shares + 2 * ((lay // 2) ^ (lay % 2)) + lay % 2)
        for row in range(len(BLOCK_LAST))
        for lay in range(shares)
    ]
    mine = lax.ppermute(both, ("rows", "layer"), pairs)
    out_shape = [jax.ShapeDtypeStruct((STEPS,) + own.shape, jnp.float32)]
    (scores,) = small_call(assemble_kernel, out_shape, own, first, second)
    (other,) = small_call(other_share_kernel, [jax.ShapeDtypeStruct(own.shape, jnp.bfloat16)], mine)
    return finish(mine, swap(other, 1), scores)


def around_ring(documents, conditioned, query_ids):
    n_rows, shares = lax.axis_size("rows"), lax.axis_size("layer")
    rows, docs = conditioned.shape[0], documents.shape[0]
    result = []
    for step in range(STEPS):
        behind = [(row, (row - step) % n_rows) for row in range(n_rows)]
        block = lax.ppermute(documents, "rows", behind) if step else documents

        def ahead(row, step=step):
            return lax.rem(row + step, n_rows)

        kernel = functools.partial(turned_kernel, shares, ahead)
        out_shape = [jax.ShapeDtypeStruct((rows // shares, docs), jnp.bfloat16)] * shares
        scratch = [pltpu.VMEM((rows, docs), jnp.float32)]
        total = direct_sum(scoring(kernel, out_shape, conditioned, query_ids, block, (), scratch))
        onward = [(row, (row + step) % n_rows) for row in range(n_rows)]
        result.append(lax.ppermute(total, "rows", onward) if step else total)
    return jnp.stack(result)


def local(train_grads, query_grads, eigenbases, eigenvalues, layer_offsets, query_doc_ids):
    conditioned = prepare(query_grads, eigenbases, eigenvalues, layer_offsets)
    on_line = lax.axis_size("rows") == 4 and lax.axis_size("layer") == 4
    plan = along_line if on_line else around_ring
    return plan(train_grads, conditioned, query_doc_ids[:, None])


def solution(mesh):
    in_specs = (
        P(("group", "rows"), "layer"),
        P(("group", "rows"), "layer"),
        P("layer", None, None),
        P("layer", None),
        P("layer"),
        P(("group", "rows")),
    )
    out_specs = P(None, "layer", ("group", "rows"))
    return jax.shard_map(local, mesh=mesh, in_specs=in_specs, out_specs=out_specs, check_vma=False)
```

```python
import functools

import jax
import jax.numpy as jnp
from jax import lax
from jax.experimental import pallas as pl
from jax.experimental.pallas import tpu as pltpu
from jax.sharding import PartitionSpec as P

LDIM = 512
LAY_DEV = 4
STEPS = 4
DAMPING = 0.05
NT = (((1,), (1,)), ((), ()))
MIB = 1024 * 1024


def layer_index():
    return lax.axis_index("layer").astype(jnp.int32)


def row_index():
    return lax.axis_index("rows").astype(jnp.int32)


def prepare_kernel(
    offsets, queries_hbm, bases_hbm, values_hbm, conditioned_ref, queries, bases, values, arrived
):
    copies = [pltpu.make_async_copy(values_hbm, values, arrived.at[0])]
    for layer in range(LAY_DEV):
        columns = queries_hbm.at[:, layer * LDIM : (layer + 1) * LDIM]
        copies.append(pltpu.make_async_copy(columns, queries.at[layer], arrived.at[1 + 2 * layer]))
        copies.append(pltpu.make_async_copy(bases_hbm.at[layer], bases.at[layer], arrived.at[2 + 2 * layer]))
    for copy in copies:
        copy.start()
    base_column = layer_index() * (LAY_DEV * LDIM)
    copies[0].wait()
    for layer in range(LAY_DEV):
        copies[1 + 2 * layer].wait()
        copies[2 + 2 * layer].wait()
        basis = bases[layer]
        projected = jnp.dot(queries[layer], basis, preferred_element_type=jnp.float32)
        scaled = (projected / (values[layer : layer + 1, :] + DAMPING)).astype(jnp.bfloat16)
        restored = lax.dot_general(scaled, basis, NT, preferred_element_type=jnp.float32)
        first = pl.multiple_of(offsets[layer] - base_column, LDIM)
        conditioned_ref[:, pl.ds(first, LDIM)] = restored.astype(jnp.bfloat16)


def prepare(queries, bases, values, offsets):
    rows, dims = queries.shape
    hbm = pl.BlockSpec(memory_space=pltpu.HBM)
    return pl.pallas_call(
        prepare_kernel,
        out_shape=jax.ShapeDtypeStruct((rows, dims), jnp.bfloat16),
        in_specs=[pl.BlockSpec(memory_space=pltpu.SMEM), hbm, hbm, hbm],
        out_specs=pl.BlockSpec(memory_space=pltpu.VMEM),
        scratch_shapes=[
            pltpu.VMEM((LAY_DEV, rows, LDIM), jnp.bfloat16),
            pltpu.VMEM(bases.shape, jnp.bfloat16),
            pltpu.VMEM(values.shape, jnp.float32),
            pltpu.SemaphoreType.DMA((1 + 2 * LAY_DEV,)),
        ],
        compiler_params=pltpu.CompilerParams(vmem_limit_bytes=62 * MIB),
        cost_estimate=pl.CostEstimate(
            flops=4 * rows * dims * LDIM, bytes_accessed=6 * MIB, transcendentals=0
        ),
    )(offsets, queries, bases, values)


def masked_tile(queries, documents, query_ids, block):
    tile = lax.dot_general(queries, documents, NT, preferred_element_type=jnp.float32)
    doc_ids = block * tile.shape[1] + lax.broadcasted_iota(jnp.int32, tile.shape, 1)
    return jnp.where(query_ids == doc_ids, 0.0, tile)


def scoring(kernel, out_shape, conditioned, query_ids, documents, extra=(), scratch=(), weight=1):
    dims = conditioned.shape[1]
    docs = documents.shape[0]
    rows = sum(shape.shape[0] for shape in out_shape)
    vmem = pl.BlockSpec(memory_space=pltpu.VMEM)
    return pl.pallas_call(
        kernel,
        out_shape=out_shape,
        in_specs=[vmem] * (3 + len(extra)),
        out_specs=[vmem] * len(out_shape),
        scratch_shapes=scratch,
        compiler_params=pltpu.CompilerParams(vmem_limit_bytes=12 * MIB),
        cost_estimate=pl.CostEstimate(
            flops=2 * rows * docs * dims * weight, bytes_accessed=2 * dims * (rows + docs) * weight, transcendentals=0
        ),
    )(conditioned, query_ids, documents, *extra)


def turned_kernel(shares, block_of, queries_ref, ids_ref, documents_ref, *refs):
    *out_refs, held = refs
    held[...] = masked_tile(queries_ref[...], documents_ref[...], ids_ref[...], block_of(row_index()))
    for turn, out_ref in enumerate(out_refs):
        share_rows = out_ref.shape[0]
        first = pl.multiple_of(lax.rem(layer_index() + turn, shares) * share_rows, share_rows)
        out_ref[...] = held[pl.ds(first, share_rows), :].astype(jnp.bfloat16)


def half_shares(share_rows, kept):
    core = lax.rem(layer_index(), 2)
    core = core if kept else 1 - core
    return [pl.multiple_of((2 * chip + core) * share_rows, share_rows) for chip in range(2)]


def halves_kernel(block_of, queries_ref, ids_ref, documents_ref, *refs):
    front_refs, out_refs, held = refs[:-3], refs[-3:-1], refs[-1]
    held[...] = masked_tile(queries_ref[...], documents_ref[...], ids_ref[...], block_of(row_index()))
    docs = documents_ref.shape[0]
    rows, width = out_refs[0].shape
    for side, kept in enumerate((True, False)):
        if front_refs:
            out_refs[side][:, : width - docs] = front_refs[side][...]
        for chip, first in enumerate(half_shares(rows // 2, kept)):
            spot = slice(chip * (rows // 2), (chip + 1) * (rows // 2))
            out_refs[side][spot, width - docs :] = held[pl.ds(first, rows // 2), :]


def target_chip():
    chip, core = lax.div(layer_index(), 2), lax.rem(layer_index(), 2)
    return jnp.where(chip == core, 0, 1)


def half_kernel(block_of, kept, queries_ref, ids_ref, documents_ref, out_ref):
    rows = out_ref.shape[0]
    chip = target_chip() if kept else 1 - target_chip()
    spot = pl.ds(pl.multiple_of(chip * rows, rows), rows)
    tile = lax.dot_general(documents_ref[...], queries_ref[spot, :], NT, preferred_element_type=jnp.float32).T
    doc_ids = block_of(row_index()) * tile.shape[1] + lax.broadcasted_iota(jnp.int32, tile.shape, 1)
    tile = jnp.where(ids_ref[spot, :] == doc_ids, 0.0, tile)
    out_ref[...] = tile.astype(out_ref.dtype)


def total_of(refs):
    total = refs[0][...].astype(jnp.float32)
    for ref in refs[1:]:
        total += ref[...].astype(jnp.float32)
    return total


def sum_kernel(*refs):
    refs[-1][...] = total_of(refs[:-1]).astype(refs[-1].dtype)


def small_call(kernel, out_shape, *args):
    vmem = pl.BlockSpec(memory_space=pltpu.VMEM)
    return pl.pallas_call(
        kernel,
        out_shape=out_shape,
        in_specs=[vmem] * len(args),
        out_specs=[vmem] * len(out_shape),
        compiler_params=pltpu.CompilerParams(vmem_limit_bytes=4 * MIB),
    )(*args)


def direct_sum(tiles):
    shares = len(tiles)
    arrived = [tiles[0]]
    for turn in range(1, shares):
        pairs = [(lay, (lay + turn) % shares) for lay in range(shares)]
        arrived.append(lax.ppermute(tiles[turn], "layer", pairs))
    (total,) = small_call(sum_kernel, [jax.ShapeDtypeStruct(tiles[0].shape, jnp.float32)], *arrived)
    return total


def core_sum_kernel(kept_ref, arrived_ref, mine_ref, other_ref):
    rows = mine_ref.shape[0]
    chip = lax.div(layer_index(), 2)
    mine = pl.ds(pl.multiple_of(chip * rows, rows), rows)
    other = pl.ds(pl.multiple_of((1 - chip) * rows, rows), rows)
    mine_ref[...] = (kept_ref[mine, :] + arrived_ref[mine, :]).astype(mine_ref.dtype)
    other_ref[...] = (kept_ref[other, :] + arrived_ref[other, :]).astype(other_ref.dtype)


def chip_sum_kernel(mine_ref, arrived_ref, *out_refs):
    docs = out_refs[0].shape[1]
    for spot, out_ref in enumerate(out_refs):
        columns = slice(spot * docs, (spot + 1) * docs)
        total = mine_ref[:, columns] + arrived_ref[:, columns].astype(jnp.float32)
        out_ref[...] = total.astype(out_ref.dtype)


def swap(value, distance):
    count = lax.axis_size("layer")
    return lax.ppermute(value, "layer", [(lay, lay ^ distance) for lay in range(count)])


def core_sum(kept, arrived, mine_type):
    rows, width = kept.shape[0] // 2, kept.shape[1]
    out_shape = [jax.ShapeDtypeStruct((rows, width), out_type) for out_type in (mine_type, jnp.bfloat16)]
    return small_call(core_sum_kernel, out_shape, kept, arrived)


def layer_sum(kept, sent, out_types):
    mine, other = core_sum(kept, swap(sent, 1), jnp.float32)
    rows, docs = mine.shape[0], mine.shape[1] // len(out_types)
    out_shape = [jax.ShapeDtypeStruct((rows, docs), out_type) for out_type in out_types]
    return small_call(chip_sum_kernel, out_shape, mine, swap(other, 2))


ROUND_ONE = ((0, 2), (2, 3), (3, 1), (1, 0))
ROUND_TWO = ((0, 1), (1, 3), (3, 2), (2, 0))
BLOCK_ONE = (1, 3, 0, 2)
BLOCK_TWO = (2, 0, 3, 1)
BLOCK_LAST = (3, 2, 1, 0)


def pick(table):
    def entry(row):
        value = jnp.int32(table[0])
        for index in range(1, len(table)):
            value = jnp.where(row == index, jnp.int32(table[index]), value)
        return value

    return entry


def step_of(table):
    return pick([(block - table.index(block)) % STEPS for block in range(STEPS)])


def assemble_kernel(own_ref, first_ref, second_ref, out_ref):
    out_ref[0] = own_ref[...]
    for ref, table in ((first_ref, BLOCK_ONE), (second_ref, BLOCK_TWO)):
        out_ref[step_of(table)(row_index())] = ref[...].astype(jnp.float32)


def core_share(rows, own):
    core = lax.rem(layer_index(), 2)
    return pl.ds(pl.multiple_of((core if own else 1 - core) * rows, rows), rows)


def other_share_kernel(mine_ref, out_ref):
    out_ref[...] = mine_ref[core_share(out_ref.shape[0], False), :]


def finish_kernel(mine_ref, arrived_ref, scores_hbm, out_hbm, total, copied):
    del scores_hbm
    mine = mine_ref[core_share(total.shape[0], True), :].astype(jnp.float32)
    total[...] = mine + arrived_ref[...].astype(jnp.float32)
    copy = pltpu.make_async_copy(total, out_hbm.at[step_of(BLOCK_LAST)(row_index())], copied)
    copy.start()
    copy.wait()


def finish(mine, arrived, scores):
    hbm = pl.BlockSpec(memory_space=pltpu.HBM)
    vmem = pl.BlockSpec(memory_space=pltpu.VMEM)
    return pl.pallas_call(
        finish_kernel,
        out_shape=jax.ShapeDtypeStruct(scores.shape, scores.dtype),
        in_specs=[vmem, vmem, hbm],
        out_specs=hbm,
        scratch_shapes=[pltpu.VMEM(scores.shape[1:], jnp.float32), pltpu.SemaphoreType.DMA],
        input_output_aliases={2: 0},
        compiler_params=pltpu.CompilerParams(vmem_limit_bytes=4 * MIB),
    )(mine, arrived, scores)


def along_line(documents, conditioned, query_ids):
    docs = documents.shape[0]
    half = (conditioned.shape[0] // 2, docs)

    def halves(block, block_of, front=()):
        width = docs * (1 + bool(front))
        out_shape = [jax.ShapeDtypeStruct((half[0], width), jnp.float32)] * 2
        scratch = [pltpu.VMEM((2 * half[0], docs), jnp.float32)]
        kernel = functools.partial(halves_kernel, block_of)
        return scoring(kernel, out_shape, conditioned, query_ids, block, front, scratch)

    def one_half(block, block_of, kept):
        kernel = functools.partial(half_kernel, block_of, kept)
        out_shape = [jax.ShapeDtypeStruct(half, jnp.float32 if kept else jnp.bfloat16)]
        weight = 5 if kept else 1
        return scoring(kernel, out_shape, conditioned, query_ids, block, weight=weight)[0]

    def back(total, table):
        return lax.ppermute(total, "rows", tuple(enumerate(table)))

    one = lax.ppermute(documents, "rows", ROUND_ONE)
    later, conditioned = lax.optimization_barrier((documents, conditioned))
    two = lax.ppermute(later, "rows", ROUND_TWO)
    own = halves(later, lambda row: row)
    one, own = lax.optimization_barrier((one, own))
    three = lax.ppermute(one, "rows", ROUND_ONE)

    own, first = layer_sum(*halves(one, pick(BLOCK_ONE), own), (jnp.float32, jnp.bfloat16))
    two, first = lax.optimization_barrier((two, first))
    (second,) = layer_sum(*halves(two, pick(BLOCK_TWO)), (jnp.bfloat16,))
    three, *_ = lax.optimization_barrier((three, first, second))
    first, second = back(first, BLOCK_ONE), back(second, BLOCK_TWO)

    arrived = swap(one_half(three, pick(BLOCK_LAST), False), 1)
    three, first, second = lax.optimization_barrier((three, first, second))
    kept = one_half(three, pick(BLOCK_LAST), True)
    (both,) = small_call(sum_kernel, [jax.ShapeDtypeStruct(half, jnp.bfloat16)], kept, arrived)
    shares = lax.axis_size("layer")
    pairs = [
        (row * shares + lay, BLOCK_LAST[row] * shares + 2 * ((lay // 2) ^ (lay % 2)) + lay % 2)
        for row in range(len(BLOCK_LAST))
        for lay in range(shares)
    ]
    mine = lax.ppermute(both, ("rows", "layer"), pairs)
    out_shape = [jax.ShapeDtypeStruct((STEPS,) + own.shape, jnp.float32)]
    (scores,) = small_call(assemble_kernel, out_shape, own, first, second)
    (other,) = small_call(other_share_kernel, [jax.ShapeDtypeStruct(own.shape, jnp.bfloat16)], mine)
    return finish(mine, swap(other, 1), scores)


def around_ring(documents, conditioned, query_ids):
    n_rows, shares = lax.axis_size("rows"), lax.axis_size("layer")
    rows, docs = conditioned.shape[0], documents.shape[0]
    result = []
    for step in range(STEPS):
        behind = [(row, (row - step) % n_rows) for row in range(n_rows)]
        block = lax.ppermute(documents, "rows", behind) if step else documents

        def ahead(row, step=step):
            return lax.rem(row + step, n_rows)

        kernel = functools.partial(turned_kernel, shares, ahead)
        out_shape = [jax.ShapeDtypeStruct((rows // shares, docs), jnp.bfloat16)] * shares
        scratch = [pltpu.VMEM((rows, docs), jnp.float32)]
        total = direct_sum(scoring(kernel, out_shape, conditioned, query_ids, block, (), scratch))
        onward = [(row, (row + step) % n_rows) for row in range(n_rows)]
        result.append(lax.ppermute(total, "rows", onward) if step else total)
    return jnp.stack(result)


def local(train_grads, query_grads, eigenbases, eigenvalues, layer_offsets, query_doc_ids):
    conditioned = prepare(query_grads, eigenbases, eigenvalues, layer_offsets)
    on_line = lax.axis_size("rows") == 4 and lax.axis_size("layer") == 4
    plan = along_line if on_line else around_ring
    return plan(train_grads, conditioned, query_doc_ids[:, None])


def solution(mesh):
    in_specs = (
        P(("group", "rows"), "layer"),
        P(("group", "rows"), "layer"),
        P("layer", None, None),
        P("layer", None),
        P("layer"),
        P(("group", "rows")),
    )
    out_specs = P(None, "layer", ("group", "rows"))
    return jax.shard_map(local, mesh=mesh, in_specs=in_specs, out_specs=out_specs, check_vma=False)
```

```python
import functools

import jax
import jax.numpy as jnp
from jax import lax
from jax.experimental import pallas as pl
from jax.experimental.pallas import tpu as pltpu
from jax.sharding import PartitionSpec as P

LDIM = 512
LAY_DEV = 4
STEPS = 4
DAMPING = 0.05
NT = (((1,), (1,)), ((), ()))
MIB = 1024 * 1024


def layer_index():
    return lax.axis_index("layer").astype(jnp.int32)


def row_index():
    return lax.axis_index("rows").astype(jnp.int32)


def prepare_kernel(
    offsets, queries_hbm, bases_hbm, values_hbm, conditioned_ref, queries, bases, values, arrived
):
    copies = [pltpu.make_async_copy(values_hbm, values, arrived.at[0])]
    for layer in range(LAY_DEV):
        columns = queries_hbm.at[:, layer * LDIM : (layer + 1) * LDIM]
        copies.append(pltpu.make_async_copy(columns, queries.at[layer], arrived.at[1 + 2 * layer]))
        copies.append(pltpu.make_async_copy(bases_hbm.at[layer], bases.at[layer], arrived.at[2 + 2 * layer]))
    for copy in copies:
        copy.start()
    base_column = layer_index() * (LAY_DEV * LDIM)
    copies[0].wait()
    for layer in range(LAY_DEV):
        copies[1 + 2 * layer].wait()
        copies[2 + 2 * layer].wait()
        basis = bases[layer]
        projected = jnp.dot(queries[layer], basis, preferred_element_type=jnp.float32)
        scaled = (projected / (values[layer : layer + 1, :] + DAMPING)).astype(jnp.bfloat16)
        restored = lax.dot_general(scaled, basis, NT, preferred_element_type=jnp.float32)
        first = pl.multiple_of(offsets[layer] - base_column, LDIM)
        conditioned_ref[:, pl.ds(first, LDIM)] = restored.astype(jnp.bfloat16)


def prepare(queries, bases, values, offsets):
    rows, dims = queries.shape
    hbm = pl.BlockSpec(memory_space=pltpu.HBM)
    return pl.pallas_call(
        prepare_kernel,
        out_shape=jax.ShapeDtypeStruct((rows, dims), jnp.bfloat16),
        in_specs=[pl.BlockSpec(memory_space=pltpu.SMEM), hbm, hbm, hbm],
        out_specs=pl.BlockSpec(memory_space=pltpu.VMEM),
        scratch_shapes=[
            pltpu.VMEM((LAY_DEV, rows, LDIM), jnp.bfloat16),
            pltpu.VMEM(bases.shape, jnp.bfloat16),
            pltpu.VMEM(values.shape, jnp.float32),
            pltpu.SemaphoreType.DMA((1 + 2 * LAY_DEV,)),
        ],
        compiler_params=pltpu.CompilerParams(vmem_limit_bytes=62 * MIB),
        cost_estimate=pl.CostEstimate(
            flops=4 * rows * dims * LDIM, bytes_accessed=6 * MIB, transcendentals=0
        ),
    )(offsets, queries, bases, values)


def masked_tile(queries, documents, query_ids, block):
    tile = lax.dot_general(queries, documents, NT, preferred_element_type=jnp.float32)
    doc_ids = block * tile.shape[1] + lax.broadcasted_iota(jnp.int32, tile.shape, 1)
    return jnp.where(query_ids == doc_ids, 0.0, tile)


def scoring(kernel, out_shape, conditioned, query_ids, documents, extra=(), scratch=(), weight=1):
    dims = conditioned.shape[1]
    docs = documents.shape[0]
    rows = sum(shape.shape[0] for shape in out_shape)
    vmem = pl.BlockSpec(memory_space=pltpu.VMEM)
    return pl.pallas_call(
        kernel,
        out_shape=out_shape,
        in_specs=[vmem] * (3 + len(extra)),
        out_specs=[vmem] * len(out_shape),
        scratch_shapes=scratch,
        compiler_params=pltpu.CompilerParams(vmem_limit_bytes=12 * MIB),
        cost_estimate=pl.CostEstimate(
            flops=2 * rows * docs * dims * weight, bytes_accessed=2 * dims * (rows + docs) * weight, transcendentals=0
        ),
    )(conditioned, query_ids, documents, *extra)


def turned_kernel(shares, block_of, queries_ref, ids_ref, documents_ref, *refs):
    *out_refs, held = refs
    held[...] = masked_tile(queries_ref[...], documents_ref[...], ids_ref[...], block_of(row_index()))
    for turn, out_ref in enumerate(out_refs):
        share_rows = out_ref.shape[0]
        first = pl.multiple_of(lax.rem(layer_index() + turn, shares) * share_rows, share_rows)
        out_ref[...] = held[pl.ds(first, share_rows), :].astype(jnp.bfloat16)


def half_shares(share_rows, kept):
    core = lax.rem(layer_index(), 2)
    core = core if kept else 1 - core
    return [pl.multiple_of((2 * chip + core) * share_rows, share_rows) for chip in range(2)]


def halves_kernel(block_of, queries_ref, ids_ref, documents_ref, *refs):
    front_refs, out_refs, held = refs[:-3], refs[-3:-1], refs[-1]
    held[...] = masked_tile(queries_ref[...], documents_ref[...], ids_ref[...], block_of(row_index()))
    docs = documents_ref.shape[0]
    rows, width = out_refs[0].shape
    for side, kept in enumerate((True, False)):
        if front_refs:
            out_refs[side][:, : width - docs] = front_refs[side][...]
        for chip, first in enumerate(half_shares(rows // 2, kept)):
            spot = slice(chip * (rows // 2), (chip + 1) * (rows // 2))
            out_refs[side][spot, width - docs :] = held[pl.ds(first, rows // 2), :]


def target_chip():
    chip, core = lax.div(layer_index(), 2), lax.rem(layer_index(), 2)
    return jnp.where(chip == core, 0, 1)


def half_kernel(block_of, kept, queries_ref, ids_ref, documents_ref, out_ref):
    rows = out_ref.shape[0]
    chip = target_chip() if kept else 1 - target_chip()
    spot = pl.ds(pl.multiple_of(chip * rows, rows), rows)
    tile = masked_tile(queries_ref[spot, :], documents_ref[...], ids_ref[spot, :], block_of(row_index()))
    out_ref[...] = tile.astype(out_ref.dtype)


def total_of(refs):
    total = refs[0][...].astype(jnp.float32)
    for ref in refs[1:]:
        total += ref[...].astype(jnp.float32)
    return total


def sum_kernel(*refs):
    refs[-1][...] = total_of(refs[:-1]).astype(refs[-1].dtype)


def small_call(kernel, out_shape, *args):
    vmem = pl.BlockSpec(memory_space=pltpu.VMEM)
    return pl.pallas_call(
        kernel,
        out_shape=out_shape,
        in_specs=[vmem] * len(args),
        out_specs=[vmem] * len(out_shape),
        compiler_params=pltpu.CompilerParams(vmem_limit_bytes=4 * MIB),
    )(*args)


def direct_sum(tiles):
    shares = len(tiles)
    arrived = [tiles[0]]
    for turn in range(1, shares):
        pairs = [(lay, (lay + turn) % shares) for lay in range(shares)]
        arrived.append(lax.ppermute(tiles[turn], "layer", pairs))
    (total,) = small_call(sum_kernel, [jax.ShapeDtypeStruct(tiles[0].shape, jnp.float32)], *arrived)
    return total


def core_sum_kernel(kept_ref, arrived_ref, mine_ref, other_ref):
    rows = mine_ref.shape[0]
    chip = lax.div(layer_index(), 2)
    mine = pl.ds(pl.multiple_of(chip * rows, rows), rows)
    other = pl.ds(pl.multiple_of((1 - chip) * rows, rows), rows)
    mine_ref[...] = (kept_ref[mine, :] + arrived_ref[mine, :]).astype(mine_ref.dtype)
    other_ref[...] = (kept_ref[other, :] + arrived_ref[other, :]).astype(other_ref.dtype)


def chip_sum_kernel(mine_ref, arrived_ref, *out_refs):
    docs = out_refs[0].shape[1]
    for spot, out_ref in enumerate(out_refs):
        columns = slice(spot * docs, (spot + 1) * docs)
        total = mine_ref[:, columns] + arrived_ref[:, columns].astype(jnp.float32)
        out_ref[...] = total.astype(out_ref.dtype)


def swap(value, distance):
    count = lax.axis_size("layer")
    return lax.ppermute(value, "layer", [(lay, lay ^ distance) for lay in range(count)])


def core_sum(kept, arrived, mine_type):
    rows, width = kept.shape[0] // 2, kept.shape[1]
    out_shape = [jax.ShapeDtypeStruct((rows, width), out_type) for out_type in (mine_type, jnp.bfloat16)]
    return small_call(core_sum_kernel, out_shape, kept, arrived)


def layer_sum(kept, sent, out_types):
    mine, other = core_sum(kept, swap(sent, 1), jnp.float32)
    rows, docs = mine.shape[0], mine.shape[1] // len(out_types)
    out_shape = [jax.ShapeDtypeStruct((rows, docs), out_type) for out_type in out_types]
    return small_call(chip_sum_kernel, out_shape, mine, swap(other, 2))


ROUND_ONE = ((0, 2), (2, 3), (3, 1), (1, 0))
ROUND_TWO = ((0, 1), (1, 3), (3, 2), (2, 0))
BLOCK_ONE = (1, 3, 0, 2)
BLOCK_TWO = (2, 0, 3, 1)
BLOCK_LAST = (3, 2, 1, 0)


def pick(table):
    def entry(row):
        value = jnp.int32(table[0])
        for index in range(1, len(table)):
            value = jnp.where(row == index, jnp.int32(table[index]), value)
        return value

    return entry


def step_of(table):
    return pick([(block - table.index(block)) % STEPS for block in range(STEPS)])


def assemble_kernel(own_ref, first_ref, second_ref, out_ref):
    out_ref[0] = own_ref[...]
    for ref, table in ((first_ref, BLOCK_ONE), (second_ref, BLOCK_TWO)):
        out_ref[step_of(table)(row_index())] = ref[...].astype(jnp.float32)


def core_share(rows, own):
    core = lax.rem(layer_index(), 2)
    return pl.ds(pl.multiple_of((core if own else 1 - core) * rows, rows), rows)


def other_share_kernel(mine_ref, out_ref):
    out_ref[...] = mine_ref[core_share(out_ref.shape[0], False), :]


def finish_kernel(mine_ref, arrived_ref, scores_hbm, out_hbm, total, copied):
    del scores_hbm
    mine = mine_ref[core_share(total.shape[0], True), :].astype(jnp.float32)
    total[...] = mine + arrived_ref[...].astype(jnp.float32)
    copy = pltpu.make_async_copy(total, out_hbm.at[step_of(BLOCK_LAST)(row_index())], copied)
    copy.start()
    copy.wait()


def finish(mine, arrived, scores):
    hbm = pl.BlockSpec(memory_space=pltpu.HBM)
    vmem = pl.BlockSpec(memory_space=pltpu.VMEM)
    return pl.pallas_call(
        finish_kernel,
        out_shape=jax.ShapeDtypeStruct(scores.shape, scores.dtype),
        in_specs=[vmem, vmem, hbm],
        out_specs=hbm,
        scratch_shapes=[pltpu.VMEM(scores.shape[1:], jnp.float32), pltpu.SemaphoreType.DMA],
        input_output_aliases={2: 0},
        compiler_params=pltpu.CompilerParams(vmem_limit_bytes=4 * MIB),
    )(mine, arrived, scores)


def along_line(documents, conditioned, query_ids):
    docs = documents.shape[0]
    half = (conditioned.shape[0] // 2, docs)

    def halves(block, block_of, front=()):
        width = docs * (1 + bool(front))
        out_shape = [jax.ShapeDtypeStruct((half[0], width), jnp.float32)] * 2
        scratch = [pltpu.VMEM((2 * half[0], docs), jnp.float32)]
        kernel = functools.partial(halves_kernel, block_of)
        return scoring(kernel, out_shape, conditioned, query_ids, block, front, scratch)

    def one_half(block, block_of, kept):
        kernel = functools.partial(half_kernel, block_of, kept)
        out_shape = [jax.ShapeDtypeStruct(half, jnp.float32 if kept else jnp.bfloat16)]
        weight = 5 if kept else 1
        return scoring(kernel, out_shape, conditioned, query_ids, block, weight=weight)[0]

    def back(total, table):
        return lax.ppermute(total, "rows", tuple(enumerate(table)))

    one = lax.ppermute(documents, "rows", ROUND_ONE)
    two = lax.ppermute(documents, "rows", ROUND_TWO)
    own = halves(documents, lambda row: row)
    one, own = lax.optimization_barrier((one, own))
    three = lax.ppermute(one, "rows", ROUND_ONE)

    own, first = layer_sum(*halves(one, pick(BLOCK_ONE), own), (jnp.float32, jnp.bfloat16))
    two, first = lax.optimization_barrier((two, first))
    (second,) = layer_sum(*halves(two, pick(BLOCK_TWO)), (jnp.bfloat16,))
    three, *_ = lax.optimization_barrier((three, first, second))
    first, second = back(first, BLOCK_ONE), back(second, BLOCK_TWO)

    arrived = swap(one_half(three, pick(BLOCK_LAST), False), 1)
    three, first, second = lax.optimization_barrier((three, first, second))
    kept = one_half(three, pick(BLOCK_LAST), True)
    (both,) = small_call(sum_kernel, [jax.ShapeDtypeStruct(half, jnp.bfloat16)], kept, arrived)
    shares = lax.axis_size("layer")
    pairs = [
        (row * shares + lay, BLOCK_LAST[row] * shares + 2 * ((lay // 2) ^ (lay % 2)) + lay % 2)
        for row in range(len(BLOCK_LAST))
        for lay in range(shares)
    ]
    mine = lax.ppermute(both, ("rows", "layer"), pairs)
    out_shape = [jax.ShapeDtypeStruct((STEPS,) + own.shape, jnp.float32)]
    (scores,) = small_call(assemble_kernel, out_shape, own, first, second)
    (other,) = small_call(other_share_kernel, [jax.ShapeDtypeStruct(own.shape, jnp.bfloat16)], mine)
    return finish(mine, swap(other, 1), scores)


def around_ring(documents, conditioned, query_ids):
    n_rows, shares = lax.axis_size("rows"), lax.axis_size("layer")
    rows, docs = conditioned.shape[0], documents.shape[0]
    result = []
    for step in range(STEPS):
        behind = [(row, (row - step) % n_rows) for row in range(n_rows)]
        block = lax.ppermute(documents, "rows", behind) if step else documents

        def ahead(row, step=step):
            return lax.rem(row + step, n_rows)

        kernel = functools.partial(turned_kernel, shares, ahead)
        out_shape = [jax.ShapeDtypeStruct((rows // shares, docs), jnp.bfloat16)] * shares
        scratch = [pltpu.VMEM((rows, docs), jnp.float32)]
        total = direct_sum(scoring(kernel, out_shape, conditioned, query_ids, block, (), scratch))
        onward = [(row, (row + step) % n_rows) for row in range(n_rows)]
        result.append(lax.ppermute(total, "rows", onward) if step else total)
    return jnp.stack(result)


def local(train_grads, query_grads, eigenbases, eigenvalues, layer_offsets, query_doc_ids):
    conditioned = prepare(query_grads, eigenbases, eigenvalues, layer_offsets)
    on_line = lax.axis_size("rows") == 4 and lax.axis_size("layer") == 4
    plan = along_line if on_line else around_ring
    return plan(train_grads, conditioned, query_doc_ids[:, None])


def solution(mesh):
    in_specs = (
        P(("group", "rows"), "layer"),
        P(("group", "rows"), "layer"),
        P("layer", None, None),
        P("layer", None),
        P("layer"),
        P(("group", "rows")),
    )
    out_specs = P(None, "layer", ("group", "rows"))
    return jax.shard_map(local, mesh=mesh, in_specs=in_specs, out_specs=out_specs, check_vma=False)
```

```python
import functools

import jax
import jax.numpy as jnp
from jax import lax
from jax.experimental import pallas as pl
from jax.experimental.pallas import tpu as pltpu
from jax.sharding import PartitionSpec as P

LDIM = 512
LAY_DEV = 4
STEPS = 4
DAMPING = 0.05
NT = (((1,), (1,)), ((), ()))
MIB = 1024 * 1024


def layer_index():
    return lax.axis_index("layer").astype(jnp.int32)


def row_index():
    return lax.axis_index("rows").astype(jnp.int32)


def prepare_kernel(
    offsets, queries_hbm, bases_hbm, values_hbm, conditioned_ref, queries, bases, values, arrived
):
    copies = [pltpu.make_async_copy(values_hbm, values, arrived.at[0])]
    for layer in range(LAY_DEV):
        columns = queries_hbm.at[:, layer * LDIM : (layer + 1) * LDIM]
        copies.append(pltpu.make_async_copy(columns, queries.at[layer], arrived.at[1 + 2 * layer]))
        copies.append(pltpu.make_async_copy(bases_hbm.at[layer], bases.at[layer], arrived.at[2 + 2 * layer]))
    for copy in copies:
        copy.start()
    base_column = layer_index() * (LAY_DEV * LDIM)
    copies[0].wait()
    for layer in range(LAY_DEV):
        copies[1 + 2 * layer].wait()
        copies[2 + 2 * layer].wait()
        basis = bases[layer]
        projected = jnp.dot(queries[layer], basis, preferred_element_type=jnp.float32)
        scaled = (projected / (values[layer : layer + 1, :] + DAMPING)).astype(jnp.bfloat16)
        restored = lax.dot_general(scaled, basis, NT, preferred_element_type=jnp.float32)
        first = pl.multiple_of(offsets[layer] - base_column, LDIM)
        conditioned_ref[:, pl.ds(first, LDIM)] = restored.astype(jnp.bfloat16)


def prepare(queries, bases, values, offsets):
    rows, dims = queries.shape
    hbm = pl.BlockSpec(memory_space=pltpu.HBM)
    return pl.pallas_call(
        prepare_kernel,
        out_shape=jax.ShapeDtypeStruct((rows, dims), jnp.bfloat16),
        in_specs=[pl.BlockSpec(memory_space=pltpu.SMEM), hbm, hbm, hbm],
        out_specs=pl.BlockSpec(memory_space=pltpu.VMEM),
        scratch_shapes=[
            pltpu.VMEM((LAY_DEV, rows, LDIM), jnp.bfloat16),
            pltpu.VMEM(bases.shape, jnp.bfloat16),
            pltpu.VMEM(values.shape, jnp.float32),
            pltpu.SemaphoreType.DMA((1 + 2 * LAY_DEV,)),
        ],
        compiler_params=pltpu.CompilerParams(vmem_limit_bytes=48 * MIB),
        cost_estimate=pl.CostEstimate(
            flops=4 * rows * dims * LDIM, bytes_accessed=6 * MIB, transcendentals=0
        ),
    )(offsets, queries, bases, values)


def masked_tile(queries, documents, query_ids, block):
    tile = lax.dot_general(queries, documents, NT, preferred_element_type=jnp.float32)
    doc_ids = block * tile.shape[1] + lax.broadcasted_iota(jnp.int32, tile.shape, 1)
    return jnp.where(query_ids == doc_ids, 0.0, tile)


def scoring(kernel, out_shape, conditioned, query_ids, documents, extra=(), scratch=(), weight=1):
    dims = conditioned.shape[1]
    docs = documents.shape[0]
    rows = sum(shape.shape[0] for shape in out_shape)
    vmem = pl.BlockSpec(memory_space=pltpu.VMEM)
    return pl.pallas_call(
        kernel,
        out_shape=out_shape,
        in_specs=[vmem] * (3 + len(extra)),
        out_specs=[vmem] * len(out_shape),
        scratch_shapes=scratch,
        compiler_params=pltpu.CompilerParams(vmem_limit_bytes=12 * MIB),
        cost_estimate=pl.CostEstimate(
            flops=2 * rows * docs * dims * weight, bytes_accessed=2 * dims * (rows + docs) * weight, transcendentals=0
        ),
    )(conditioned, query_ids, documents, *extra)


def turned_kernel(shares, block_of, queries_ref, ids_ref, documents_ref, *refs):
    *out_refs, held = refs
    held[...] = masked_tile(queries_ref[...], documents_ref[...], ids_ref[...], block_of(row_index()))
    for turn, out_ref in enumerate(out_refs):
        share_rows = out_ref.shape[0]
        first = pl.multiple_of(lax.rem(layer_index() + turn, shares) * share_rows, share_rows)
        out_ref[...] = held[pl.ds(first, share_rows), :].astype(jnp.bfloat16)


def half_shares(share_rows, kept):
    core = lax.rem(layer_index(), 2)
    core = core if kept else 1 - core
    return [pl.multiple_of((2 * chip + core) * share_rows, share_rows) for chip in range(2)]


def halves_kernel(block_of, queries_ref, ids_ref, documents_ref, *refs):
    front_refs, out_refs, held = refs[:-3], refs[-3:-1], refs[-1]
    held[...] = masked_tile(queries_ref[...], documents_ref[...], ids_ref[...], block_of(row_index()))
    docs = documents_ref.shape[0]
    rows, width = out_refs[0].shape
    for side, kept in enumerate((True, False)):
        if front_refs:
            out_refs[side][:, : width - docs] = front_refs[side][...]
        for chip, first in enumerate(half_shares(rows // 2, kept)):
            spot = slice(chip * (rows // 2), (chip + 1) * (rows // 2))
            out_refs[side][spot, width - docs :] = held[pl.ds(first, rows // 2), :]


def target_chip():
    chip, core = lax.div(layer_index(), 2), lax.rem(layer_index(), 2)
    return jnp.where(chip == core, 0, 1)


def half_kernel(block_of, kept, queries_ref, ids_ref, documents_ref, out_ref):
    rows = out_ref.shape[0]
    chip = target_chip() if kept else 1 - target_chip()
    spot = pl.ds(pl.multiple_of(chip * rows, rows), rows)
    tile = masked_tile(queries_ref[spot, :], documents_ref[...], ids_ref[spot, :], block_of(row_index()))
    out_ref[...] = tile.astype(out_ref.dtype)


def total_of(refs):
    total = refs[0][...].astype(jnp.float32)
    for ref in refs[1:]:
        total += ref[...].astype(jnp.float32)
    return total


def sum_kernel(*refs):
    refs[-1][...] = total_of(refs[:-1]).astype(refs[-1].dtype)


def small_call(kernel, out_shape, *args):
    vmem = pl.BlockSpec(memory_space=pltpu.VMEM)
    return pl.pallas_call(
        kernel,
        out_shape=out_shape,
        in_specs=[vmem] * len(args),
        out_specs=[vmem] * len(out_shape),
        compiler_params=pltpu.CompilerParams(vmem_limit_bytes=4 * MIB),
    )(*args)


def direct_sum(tiles):
    shares = len(tiles)
    arrived = [tiles[0]]
    for turn in range(1, shares):
        pairs = [(lay, (lay + turn) % shares) for lay in range(shares)]
        arrived.append(lax.ppermute(tiles[turn], "layer", pairs))
    (total,) = small_call(sum_kernel, [jax.ShapeDtypeStruct(tiles[0].shape, jnp.float32)], *arrived)
    return total


def core_sum_kernel(kept_ref, arrived_ref, mine_ref, other_ref):
    rows = mine_ref.shape[0]
    chip = lax.div(layer_index(), 2)
    mine = pl.ds(pl.multiple_of(chip * rows, rows), rows)
    other = pl.ds(pl.multiple_of((1 - chip) * rows, rows), rows)
    mine_ref[...] = (kept_ref[mine, :] + arrived_ref[mine, :]).astype(mine_ref.dtype)
    other_ref[...] = (kept_ref[other, :] + arrived_ref[other, :]).astype(other_ref.dtype)


def chip_sum_kernel(mine_ref, arrived_ref, *out_refs):
    docs = out_refs[0].shape[1]
    for spot, out_ref in enumerate(out_refs):
        columns = slice(spot * docs, (spot + 1) * docs)
        total = mine_ref[:, columns] + arrived_ref[:, columns].astype(jnp.float32)
        out_ref[...] = total.astype(out_ref.dtype)


def swap(value, distance):
    count = lax.axis_size("layer")
    return lax.ppermute(value, "layer", [(lay, lay ^ distance) for lay in range(count)])


def core_sum(kept, arrived, mine_type):
    rows, width = kept.shape[0] // 2, kept.shape[1]
    out_shape = [jax.ShapeDtypeStruct((rows, width), out_type) for out_type in (mine_type, jnp.bfloat16)]
    return small_call(core_sum_kernel, out_shape, kept, arrived)


def layer_sum(kept, sent, out_types):
    mine, other = core_sum(kept, swap(sent, 1), jnp.float32)
    rows, docs = mine.shape[0], mine.shape[1] // len(out_types)
    out_shape = [jax.ShapeDtypeStruct((rows, docs), out_type) for out_type in out_types]
    return small_call(chip_sum_kernel, out_shape, mine, swap(other, 2))


ROUND_ONE = ((0, 2), (2, 3), (3, 1), (1, 0))
ROUND_TWO = ((0, 1), (1, 3), (3, 2), (2, 0))
BLOCK_ONE = (1, 3, 0, 2)
BLOCK_TWO = (2, 0, 3, 1)
BLOCK_LAST = (3, 2, 1, 0)


def pick(table):
    def entry(row):
        value = jnp.int32(table[0])
        for index in range(1, len(table)):
            value = jnp.where(row == index, jnp.int32(table[index]), value)
        return value

    return entry


def step_of(table):
    return pick([(block - table.index(block)) % STEPS for block in range(STEPS)])


def assemble_kernel(own_ref, first_ref, second_ref, out_ref):
    out_ref[0] = own_ref[...]
    for ref, table in ((first_ref, BLOCK_ONE), (second_ref, BLOCK_TWO)):
        out_ref[step_of(table)(row_index())] = ref[...].astype(jnp.float32)


def core_share(rows, own):
    core = lax.rem(layer_index(), 2)
    return pl.ds(pl.multiple_of((core if own else 1 - core) * rows, rows), rows)


def other_share_kernel(mine_ref, out_ref):
    out_ref[...] = mine_ref[core_share(out_ref.shape[0], False), :]


def finish_kernel(mine_ref, arrived_ref, scores_hbm, out_hbm, total, copied):
    del scores_hbm
    mine = mine_ref[core_share(total.shape[0], True), :].astype(jnp.float32)
    total[...] = mine + arrived_ref[...].astype(jnp.float32)
    copy = pltpu.make_async_copy(total, out_hbm.at[step_of(BLOCK_LAST)(row_index())], copied)
    copy.start()
    copy.wait()


def finish(mine, arrived, scores):
    hbm = pl.BlockSpec(memory_space=pltpu.HBM)
    vmem = pl.BlockSpec(memory_space=pltpu.VMEM)
    return pl.pallas_call(
        finish_kernel,
        out_shape=jax.ShapeDtypeStruct(scores.shape, scores.dtype),
        in_specs=[vmem, vmem, hbm],
        out_specs=hbm,
        scratch_shapes=[pltpu.VMEM(scores.shape[1:], jnp.float32), pltpu.SemaphoreType.DMA],
        input_output_aliases={2: 0},
        compiler_params=pltpu.CompilerParams(vmem_limit_bytes=4 * MIB),
    )(mine, arrived, scores)


def along_line(documents, conditioned, query_ids):
    docs = documents.shape[0]
    half = (conditioned.shape[0] // 2, docs)

    def halves(block, block_of, front=()):
        width = docs * (1 + bool(front))
        out_shape = [jax.ShapeDtypeStruct((half[0], width), jnp.float32)] * 2
        scratch = [pltpu.VMEM((2 * half[0], docs), jnp.float32)]
        kernel = functools.partial(halves_kernel, block_of)
        return scoring(kernel, out_shape, conditioned, query_ids, block, front, scratch)

    def one_half(block, block_of, kept):
        kernel = functools.partial(half_kernel, block_of, kept)
        out_shape = [jax.ShapeDtypeStruct(half, jnp.float32 if kept else jnp.bfloat16)]
        weight = 5 if kept else 1
        return scoring(kernel, out_shape, conditioned, query_ids, block, weight=weight)[0]

    def back(total, table):
        return lax.ppermute(total, "rows", tuple(enumerate(table)))

    one = lax.ppermute(documents, "rows", ROUND_ONE)
    two = lax.ppermute(documents, "rows", ROUND_TWO)
    own = halves(documents, lambda row: row)
    one, own = lax.optimization_barrier((one, own))
    three = lax.ppermute(one, "rows", ROUND_ONE)

    own, first = layer_sum(*halves(one, pick(BLOCK_ONE), own), (jnp.float32, jnp.bfloat16))
    two, first = lax.optimization_barrier((two, first))
    (second,) = layer_sum(*halves(two, pick(BLOCK_TWO)), (jnp.bfloat16,))
    three, *_ = lax.optimization_barrier((three, first, second))
    first, second = back(first, BLOCK_ONE), back(second, BLOCK_TWO)

    arrived = swap(one_half(three, pick(BLOCK_LAST), False), 1)
    three, first, second = lax.optimization_barrier((three, first, second))
    kept = one_half(three, pick(BLOCK_LAST), True)
    (both,) = small_call(sum_kernel, [jax.ShapeDtypeStruct(half, jnp.bfloat16)], kept, arrived)
    shares = lax.axis_size("layer")
    pairs = [
        (row * shares + lay, BLOCK_LAST[row] * shares + 2 * ((lay // 2) ^ (lay % 2)) + lay % 2)
        for row in range(len(BLOCK_LAST))
        for lay in range(shares)
    ]
    mine = lax.ppermute(both, ("rows", "layer"), pairs)
    out_shape = [jax.ShapeDtypeStruct((STEPS,) + own.shape, jnp.float32)]
    (scores,) = small_call(assemble_kernel, out_shape, own, first, second)
    (other,) = small_call(other_share_kernel, [jax.ShapeDtypeStruct(own.shape, jnp.bfloat16)], mine)
    return finish(mine, swap(other, 1), scores)


def around_ring(documents, conditioned, query_ids):
    n_rows, shares = lax.axis_size("rows"), lax.axis_size("layer")
    rows, docs = conditioned.shape[0], documents.shape[0]
    result = []
    for step in range(STEPS):
        behind = [(row, (row - step) % n_rows) for row in range(n_rows)]
        block = lax.ppermute(documents, "rows", behind) if step else documents

        def ahead(row, step=step):
            return lax.rem(row + step, n_rows)

        kernel = functools.partial(turned_kernel, shares, ahead)
        out_shape = [jax.ShapeDtypeStruct((rows // shares, docs), jnp.bfloat16)] * shares
        scratch = [pltpu.VMEM((rows, docs), jnp.float32)]
        total = direct_sum(scoring(kernel, out_shape, conditioned, query_ids, block, (), scratch))
        onward = [(row, (row + step) % n_rows) for row in range(n_rows)]
        result.append(lax.ppermute(total, "rows", onward) if step else total)
    return jnp.stack(result)


def local(train_grads, query_grads, eigenbases, eigenvalues, layer_offsets, query_doc_ids):
    conditioned = prepare(query_grads, eigenbases, eigenvalues, layer_offsets)
    on_line = lax.axis_size("rows") == 4 and lax.axis_size("layer") == 4
    plan = along_line if on_line else around_ring
    return plan(train_grads, conditioned, query_doc_ids[:, None])


def solution(mesh):
    in_specs = (
        P(("group", "rows"), "layer"),
        P(("group", "rows"), "layer"),
        P("layer", None, None),
        P("layer", None),
        P("layer"),
        P(("group", "rows")),
    )
    out_specs = P(None, "layer", ("group", "rows"))
    return jax.shard_map(local, mesh=mesh, in_specs=in_specs, out_specs=out_specs, check_vma=False)
```

```python
import functools

import jax
import jax.numpy as jnp
from jax import lax
from jax.experimental import pallas as pl
from jax.experimental.pallas import tpu as pltpu
from jax.sharding import PartitionSpec as P

LDIM = 512
LAY_DEV = 4
STEPS = 4
DAMPING = 0.05
NT = (((1,), (1,)), ((), ()))
MIB = 1024 * 1024


def layer_index():
    return lax.axis_index("layer").astype(jnp.int32)


def row_index():
    return lax.axis_index("rows").astype(jnp.int32)


def prepare_kernel(
    offsets, queries_hbm, bases_hbm, values_hbm, conditioned_ref, queries, bases, values, arrived
):
    copies = [pltpu.make_async_copy(values_hbm, values, arrived.at[0])]
    for layer in range(LAY_DEV):
        columns = queries_hbm.at[:, layer * LDIM : (layer + 1) * LDIM]
        copies.append(pltpu.make_async_copy(columns, queries.at[layer], arrived.at[1 + 2 * layer]))
        copies.append(pltpu.make_async_copy(bases_hbm.at[layer], bases.at[layer], arrived.at[2 + 2 * layer]))
    for copy in copies:
        copy.start()
    base_column = layer_index() * (LAY_DEV * LDIM)
    copies[0].wait()
    for layer in range(LAY_DEV):
        copies[1 + 2 * layer].wait()
        copies[2 + 2 * layer].wait()
        basis = bases[layer]
        projected = jnp.dot(queries[layer], basis, preferred_element_type=jnp.float32)
        scaled = (projected / (values[layer : layer + 1, :] + DAMPING)).astype(jnp.bfloat16)
        restored = lax.dot_general(scaled, basis, NT, preferred_element_type=jnp.float32)
        first = pl.multiple_of(offsets[layer] - base_column, LDIM)
        conditioned_ref[:, pl.ds(first, LDIM)] = restored.astype(jnp.bfloat16)


def prepare(queries, bases, values, offsets):
    rows, dims = queries.shape
    hbm = pl.BlockSpec(memory_space=pltpu.HBM)
    return pl.pallas_call(
        prepare_kernel,
        out_shape=jax.ShapeDtypeStruct((rows, dims), jnp.bfloat16),
        in_specs=[pl.BlockSpec(memory_space=pltpu.SMEM), hbm, hbm, hbm],
        out_specs=pl.BlockSpec(memory_space=pltpu.VMEM),
        scratch_shapes=[
            pltpu.VMEM((LAY_DEV, rows, LDIM), jnp.bfloat16),
            pltpu.VMEM(bases.shape, jnp.bfloat16),
            pltpu.VMEM(values.shape, jnp.float32),
            pltpu.SemaphoreType.DMA((1 + 2 * LAY_DEV,)),
        ],
        compiler_params=pltpu.CompilerParams(vmem_limit_bytes=62 * MIB),
        cost_estimate=pl.CostEstimate(
            flops=4 * rows * dims * LDIM, bytes_accessed=6 * MIB, transcendentals=0
        ),
    )(offsets, queries, bases, values)


def masked_tile(queries, documents, query_ids, block):
    tile = lax.dot_general(queries, documents, NT, preferred_element_type=jnp.float32)
    doc_ids = block * tile.shape[1] + lax.broadcasted_iota(jnp.int32, tile.shape, 1)
    return jnp.where(query_ids == doc_ids, 0.0, tile)


def scoring(kernel, out_shape, conditioned, query_ids, documents, extra=(), scratch=(), weight=1):
    dims = conditioned.shape[1]
    docs = documents.shape[0]
    rows = sum(shape.shape[0] for shape in out_shape)
    vmem = pl.BlockSpec(memory_space=pltpu.VMEM)
    return pl.pallas_call(
        kernel,
        out_shape=out_shape,
        in_specs=[vmem] * (3 + len(extra)),
        out_specs=[vmem] * len(out_shape),
        scratch_shapes=scratch,
        compiler_params=pltpu.CompilerParams(vmem_limit_bytes=12 * MIB),
        cost_estimate=pl.CostEstimate(
            flops=2 * rows * docs * dims * weight, bytes_accessed=2 * dims * (rows + docs) * weight, transcendentals=0
        ),
    )(conditioned, query_ids, documents, *extra)


def turned_kernel(shares, block_of, queries_ref, ids_ref, documents_ref, *refs):
    *out_refs, held = refs
    held[...] = masked_tile(queries_ref[...], documents_ref[...], ids_ref[...], block_of(row_index()))
    for turn, out_ref in enumerate(out_refs):
        share_rows = out_ref.shape[0]
        first = pl.multiple_of(lax.rem(layer_index() + turn, shares) * share_rows, share_rows)
        out_ref[...] = held[pl.ds(first, share_rows), :].astype(jnp.bfloat16)


def half_shares(share_rows, kept):
    core = lax.rem(layer_index(), 2)
    core = core if kept else 1 - core
    return [pl.multiple_of((2 * chip + core) * share_rows, share_rows) for chip in range(2)]


def halves_kernel(block_of, queries_ref, ids_ref, documents_ref, *refs):
    front_refs, out_refs, held = refs[:-3], refs[-3:-1], refs[-1]
    held[...] = masked_tile(queries_ref[...], documents_ref[...], ids_ref[...], block_of(row_index()))
    docs = documents_ref.shape[0]
    rows, width = out_refs[0].shape
    for side, kept in enumerate((True, False)):
        if front_refs:
            out_refs[side][:, : width - docs] = front_refs[side][...]
        for chip, first in enumerate(half_shares(rows // 2, kept)):
            spot = slice(chip * (rows // 2), (chip + 1) * (rows // 2))
            out_refs[side][spot, width - docs :] = held[pl.ds(first, rows // 2), :]


def target_chip():
    chip, core = lax.div(layer_index(), 2), lax.rem(layer_index(), 2)
    return jnp.where(chip == core, 0, 1)


def half_kernel(block_of, kept, queries_ref, ids_ref, documents_ref, out_ref):
    rows = out_ref.shape[0]
    chip = target_chip() if kept else 1 - target_chip()
    spot = pl.ds(pl.multiple_of(chip * rows, rows), rows)
    tile = masked_tile(queries_ref[spot, :], documents_ref[...], ids_ref[spot, :], block_of(row_index()))
    out_ref[...] = tile.astype(out_ref.dtype)


def total_of(refs):
    total = refs[0][...].astype(jnp.float32)
    for ref in refs[1:]:
        total += ref[...].astype(jnp.float32)
    return total


def sum_kernel(*refs):
    refs[-1][...] = total_of(refs[:-1]).astype(refs[-1].dtype)


def small_call(kernel, out_shape, *args):
    vmem = pl.BlockSpec(memory_space=pltpu.VMEM)
    return pl.pallas_call(
        kernel,
        out_shape=out_shape,
        in_specs=[vmem] * len(args),
        out_specs=[vmem] * len(out_shape),
        compiler_params=pltpu.CompilerParams(vmem_limit_bytes=4 * MIB),
    )(*args)


def direct_sum(tiles):
    shares = len(tiles)
    arrived = [tiles[0]]
    for turn in range(1, shares):
        pairs = [(lay, (lay + turn) % shares) for lay in range(shares)]
        arrived.append(lax.ppermute(tiles[turn], "layer", pairs))
    (total,) = small_call(sum_kernel, [jax.ShapeDtypeStruct(tiles[0].shape, jnp.float32)], *arrived)
    return total


def core_sum_kernel(kept_ref, arrived_ref, mine_ref, other_ref):
    rows = mine_ref.shape[0]
    chip = lax.div(layer_index(), 2)
    mine = pl.ds(pl.multiple_of(chip * rows, rows), rows)
    other = pl.ds(pl.multiple_of((1 - chip) * rows, rows), rows)
    mine_ref[...] = (kept_ref[mine, :] + arrived_ref[mine, :]).astype(mine_ref.dtype)
    other_ref[...] = (kept_ref[other, :] + arrived_ref[other, :]).astype(other_ref.dtype)


def chip_sum_kernel(mine_ref, arrived_ref, *out_refs):
    docs = out_refs[0].shape[1]
    for spot, out_ref in enumerate(out_refs):
        columns = slice(spot * docs, (spot + 1) * docs)
        total = mine_ref[:, columns] + arrived_ref[:, columns].astype(jnp.float32)
        out_ref[...] = total.astype(out_ref.dtype)


def swap(value, distance):
    count = lax.axis_size("layer")
    return lax.ppermute(value, "layer", [(lay, lay ^ distance) for lay in range(count)])


def core_sum(kept, arrived, mine_type):
    rows, width = kept.shape[0] // 2, kept.shape[1]
    out_shape = [jax.ShapeDtypeStruct((rows, width), out_type) for out_type in (mine_type, jnp.bfloat16)]
    return small_call(core_sum_kernel, out_shape, kept, arrived)


def layer_sum(kept, sent, out_types):
    mine, other = core_sum(kept, swap(sent, 1), jnp.float32)
    rows, docs = mine.shape[0], mine.shape[1] // len(out_types)
    out_shape = [jax.ShapeDtypeStruct((rows, docs), out_type) for out_type in out_types]
    return small_call(chip_sum_kernel, out_shape, mine, swap(other, 2))


ROUND_ONE = ((0, 2), (2, 3), (3, 1), (1, 0))
ROUND_TWO = ((0, 1), (1, 3), (3, 2), (2, 0))
BLOCK_ONE = (1, 3, 0, 2)
BLOCK_TWO = (2, 0, 3, 1)
BLOCK_LAST = (3, 2, 1, 0)


def pick(table):
    def entry(row):
        value = jnp.int32(table[0])
        for index in range(1, len(table)):
            value = jnp.where(row == index, jnp.int32(table[index]), value)
        return value

    return entry


def step_of(table):
    return pick([(block - table.index(block)) % STEPS for block in range(STEPS)])


def assemble_kernel(own_ref, first_ref, second_ref, out_ref):
    out_ref[0] = own_ref[...]
    for ref, table in ((first_ref, BLOCK_ONE), (second_ref, BLOCK_TWO)):
        out_ref[step_of(table)(row_index())] = ref[...].astype(jnp.float32)


def core_share(rows, own):
    core = lax.rem(layer_index(), 2)
    return pl.ds(pl.multiple_of((core if own else 1 - core) * rows, rows), rows)


def other_share_kernel(mine_ref, out_ref):
    out_ref[...] = mine_ref[core_share(out_ref.shape[0], False), :]


def finish_kernel(mine_ref, arrived_ref, scores_hbm, out_hbm, total, copied):
    del scores_hbm
    mine = mine_ref[core_share(total.shape[0], True), :].astype(jnp.float32)
    total[...] = mine + arrived_ref[...].astype(jnp.float32)
    copy = pltpu.make_async_copy(total, out_hbm.at[step_of(BLOCK_LAST)(row_index())], copied)
    copy.start()
    copy.wait()


def finish(mine, arrived, scores):
    hbm = pl.BlockSpec(memory_space=pltpu.HBM)
    vmem = pl.BlockSpec(memory_space=pltpu.VMEM)
    return pl.pallas_call(
        finish_kernel,
        out_shape=jax.ShapeDtypeStruct(scores.shape, scores.dtype),
        in_specs=[vmem, vmem, hbm],
        out_specs=hbm,
        scratch_shapes=[pltpu.VMEM(scores.shape[1:], jnp.float32), pltpu.SemaphoreType.DMA],
        input_output_aliases={2: 0},
        compiler_params=pltpu.CompilerParams(vmem_limit_bytes=4 * MIB),
    )(mine, arrived, scores)


def along_line(documents, conditioned, query_ids):
    docs = documents.shape[0]
    half = (conditioned.shape[0] // 2, docs)

    def halves(block, block_of, front=()):
        width = docs * (1 + bool(front))
        out_shape = [jax.ShapeDtypeStruct((half[0], width), jnp.float32)] * 2
        scratch = [pltpu.VMEM((2 * half[0], docs), jnp.float32)]
        kernel = functools.partial(halves_kernel, block_of)
        return scoring(kernel, out_shape, conditioned, query_ids, block, front, scratch)

    def one_half(block, block_of, kept):
        kernel = functools.partial(half_kernel, block_of, kept)
        out_shape = [jax.ShapeDtypeStruct(half, jnp.float32 if kept else jnp.bfloat16)]
        weight = 5 if kept else 1
        return scoring(kernel, out_shape, conditioned, query_ids, block, weight=weight)[0]

    def back(total, table):
        return lax.ppermute(total, "rows", tuple(enumerate(table)))

    one = lax.ppermute(documents, "rows", ROUND_ONE)
    two = lax.ppermute(documents, "rows", ROUND_TWO)
    own = halves(documents, lambda row: row)
    one, own = lax.optimization_barrier((one, own))
    three = lax.ppermute(one, "rows", ROUND_ONE)

    own, first = layer_sum(*halves(one, pick(BLOCK_ONE), own), (jnp.float32, jnp.bfloat16))
    two, first = lax.optimization_barrier((two, first))
    (second,) = layer_sum(*halves(two, pick(BLOCK_TWO)), (jnp.bfloat16,))
    three, *_ = lax.optimization_barrier((three, first, second))
    first, second = back(first, BLOCK_ONE), back(second, BLOCK_TWO)

    arrived = swap(one_half(three, pick(BLOCK_LAST), False), 1)
    three, first, second = lax.optimization_barrier((three, first, second))
    kept = one_half(three, pick(BLOCK_LAST), True)
    (both,) = small_call(sum_kernel, [jax.ShapeDtypeStruct(half, jnp.bfloat16)], kept, arrived)
    shares = lax.axis_size("layer")
    pairs = [
        (row * shares + lay, BLOCK_LAST[row] * shares + 2 * ((lay // 2) ^ (lay % 2)) + lay % 2)
        for row in range(len(BLOCK_LAST))
        for lay in range(shares)
    ]
    mine = lax.ppermute(both, ("rows", "layer"), pairs)
    out_shape = [jax.ShapeDtypeStruct((STEPS,) + own.shape, jnp.float32)]
    (scores,) = small_call(assemble_kernel, out_shape, own, first, second)
    mine, scores = lax.optimization_barrier((mine, scores))
    (other,) = small_call(other_share_kernel, [jax.ShapeDtypeStruct(own.shape, jnp.bfloat16)], mine)
    return finish(mine, swap(other, 1), scores)


def around_ring(documents, conditioned, query_ids):
    n_rows, shares = lax.axis_size("rows"), lax.axis_size("layer")
    rows, docs = conditioned.shape[0], documents.shape[0]
    result = []
    for step in range(STEPS):
        behind = [(row, (row - step) % n_rows) for row in range(n_rows)]
        block = lax.ppermute(documents, "rows", behind) if step else documents

        def ahead(row, step=step):
            return lax.rem(row + step, n_rows)

        kernel = functools.partial(turned_kernel, shares, ahead)
        out_shape = [jax.ShapeDtypeStruct((rows // shares, docs), jnp.bfloat16)] * shares
        scratch = [pltpu.VMEM((rows, docs), jnp.float32)]
        total = direct_sum(scoring(kernel, out_shape, conditioned, query_ids, block, (), scratch))
        onward = [(row, (row + step) % n_rows) for row in range(n_rows)]
        result.append(lax.ppermute(total, "rows", onward) if step else total)
    return jnp.stack(result)


def local(train_grads, query_grads, eigenbases, eigenvalues, layer_offsets, query_doc_ids):
    conditioned = prepare(query_grads, eigenbases, eigenvalues, layer_offsets)
    on_line = lax.axis_size("rows") == 4 and lax.axis_size("layer") == 4
    plan = along_line if on_line else around_ring
    return plan(train_grads, conditioned, query_doc_ids[:, None])


def solution(mesh):
    in_specs = (
        P(("group", "rows"), "layer"),
        P(("group", "rows"), "layer"),
        P("layer", None, None),
        P("layer", None),
        P("layer"),
        P(("group", "rows")),
    )
    out_specs = P(None, "layer", ("group", "rows"))
    return jax.shard_map(local, mesh=mesh, in_specs=in_specs, out_specs=out_specs, check_vma=False)
```

```python
import functools

import jax
import jax.numpy as jnp
from jax import lax
from jax.experimental import pallas as pl
from jax.experimental.pallas import tpu as pltpu
from jax.sharding import PartitionSpec as P

LDIM = 512
LAY_DEV = 4
STEPS = 4
DAMPING = 0.05
NT = (((1,), (1,)), ((), ()))
MIB = 1024 * 1024


def layer_index():
    return lax.axis_index("layer").astype(jnp.int32)


def row_index():
    return lax.axis_index("rows").astype(jnp.int32)


def prepare_kernel(
    offsets, queries_hbm, bases_hbm, values_hbm, conditioned_ref, queries, bases, values, arrived
):
    copies = [pltpu.make_async_copy(values_hbm, values, arrived.at[0])]
    for layer in range(LAY_DEV):
        columns = queries_hbm.at[:, layer * LDIM : (layer + 1) * LDIM]
        copies.append(pltpu.make_async_copy(columns, queries.at[layer], arrived.at[1 + 2 * layer]))
        copies.append(pltpu.make_async_copy(bases_hbm.at[layer], bases.at[layer], arrived.at[2 + 2 * layer]))
    for copy in copies:
        copy.start()
    base_column = layer_index() * (LAY_DEV * LDIM)
    copies[0].wait()
    for layer in range(LAY_DEV):
        copies[1 + 2 * layer].wait()
        copies[2 + 2 * layer].wait()
        basis = bases[layer]
        projected = jnp.dot(queries[layer], basis, preferred_element_type=jnp.float32)
        scaled = (projected / (values[layer : layer + 1, :] + DAMPING)).astype(jnp.bfloat16)
        restored = lax.dot_general(scaled, basis, NT, preferred_element_type=jnp.float32)
        first = pl.multiple_of(offsets[layer] - base_column, LDIM)
        conditioned_ref[:, pl.ds(first, LDIM)] = restored.astype(jnp.bfloat16)


def prepare(queries, bases, values, offsets):
    rows, dims = queries.shape
    hbm = pl.BlockSpec(memory_space=pltpu.HBM)
    return pl.pallas_call(
        prepare_kernel,
        out_shape=jax.ShapeDtypeStruct((rows, dims), jnp.bfloat16),
        in_specs=[pl.BlockSpec(memory_space=pltpu.SMEM), hbm, hbm, hbm],
        out_specs=pl.BlockSpec(memory_space=pltpu.VMEM),
        scratch_shapes=[
            pltpu.VMEM((LAY_DEV, rows, LDIM), jnp.bfloat16),
            pltpu.VMEM(bases.shape, jnp.bfloat16),
            pltpu.VMEM(values.shape, jnp.float32),
            pltpu.SemaphoreType.DMA((1 + 2 * LAY_DEV,)),
        ],
        compiler_params=pltpu.CompilerParams(vmem_limit_bytes=48 * MIB),
        cost_estimate=pl.CostEstimate(
            flops=4 * rows * dims * LDIM, bytes_accessed=6 * MIB, transcendentals=0
        ),
    )(offsets, queries, bases, values)


def masked_tile(queries, documents, query_ids, block):
    tile = lax.dot_general(queries, documents, NT, preferred_element_type=jnp.float32)
    doc_ids = block * tile.shape[1] + lax.broadcasted_iota(jnp.int32, tile.shape, 1)
    return jnp.where(query_ids == doc_ids, 0.0, tile)


def scoring(kernel, out_shape, conditioned, query_ids, documents, extra=(), scratch=(), weight=1):
    dims = conditioned.shape[1]
    docs = documents.shape[0]
    rows = sum(shape.shape[0] for shape in out_shape)
    vmem = pl.BlockSpec(memory_space=pltpu.VMEM)
    return pl.pallas_call(
        kernel,
        out_shape=out_shape,
        in_specs=[vmem] * (3 + len(extra)),
        out_specs=[vmem] * len(out_shape),
        scratch_shapes=scratch,
        compiler_params=pltpu.CompilerParams(vmem_limit_bytes=12 * MIB),
        cost_estimate=pl.CostEstimate(
            flops=2 * rows * docs * dims * weight, bytes_accessed=2 * dims * (rows + docs) * weight, transcendentals=0
        ),
    )(conditioned, query_ids, documents, *extra)


def turned_kernel(shares, block_of, queries_ref, ids_ref, documents_ref, *refs):
    *out_refs, held = refs
    held[...] = masked_tile(queries_ref[...], documents_ref[...], ids_ref[...], block_of(row_index()))
    for turn, out_ref in enumerate(out_refs):
        share_rows = out_ref.shape[0]
        first = pl.multiple_of(lax.rem(layer_index() + turn, shares) * share_rows, share_rows)
        out_ref[...] = held[pl.ds(first, share_rows), :].astype(jnp.bfloat16)


def half_shares(share_rows, kept):
    core = lax.rem(layer_index(), 2)
    core = core if kept else 1 - core
    return [pl.multiple_of((2 * chip + core) * share_rows, share_rows) for chip in range(2)]


def halves_kernel(block_of, queries_ref, ids_ref, documents_ref, *refs):
    front_refs, out_refs, held = refs[:-3], refs[-3:-1], refs[-1]
    held[...] = masked_tile(queries_ref[...], documents_ref[...], ids_ref[...], block_of(row_index()))
    docs = documents_ref.shape[0]
    rows, width = out_refs[0].shape
    for side, kept in enumerate((True, False)):
        if front_refs:
            out_refs[side][:, : width - docs] = front_refs[side][...]
        for chip, first in enumerate(half_shares(rows // 2, kept)):
            spot = slice(chip * (rows // 2), (chip + 1) * (rows // 2))
            out_refs[side][spot, width - docs :] = held[pl.ds(first, rows // 2), :]


def target_chip():
    chip, core = lax.div(layer_index(), 2), lax.rem(layer_index(), 2)
    return jnp.where(chip == core, 0, 1)


def half_kernel(block_of, kept, queries_ref, ids_ref, documents_ref, out_ref):
    rows = out_ref.shape[0]
    chip = target_chip() if kept else 1 - target_chip()
    spot = pl.ds(pl.multiple_of(chip * rows, rows), rows)
    tile = masked_tile(queries_ref[spot, :], documents_ref[...], ids_ref[spot, :], block_of(row_index()))
    out_ref[...] = tile.astype(out_ref.dtype)


def total_of(refs):
    total = refs[0][...].astype(jnp.float32)
    for ref in refs[1:]:
        total += ref[...].astype(jnp.float32)
    return total


def sum_kernel(*refs):
    refs[-1][...] = total_of(refs[:-1]).astype(refs[-1].dtype)


def small_call(kernel, out_shape, *args):
    vmem = pl.BlockSpec(memory_space=pltpu.VMEM)
    return pl.pallas_call(
        kernel,
        out_shape=out_shape,
        in_specs=[vmem] * len(args),
        out_specs=[vmem] * len(out_shape),
        compiler_params=pltpu.CompilerParams(vmem_limit_bytes=4 * MIB),
    )(*args)


def direct_sum(tiles):
    shares = len(tiles)
    arrived = [tiles[0]]
    for turn in range(1, shares):
        pairs = [(lay, (lay + turn) % shares) for lay in range(shares)]
        arrived.append(lax.ppermute(tiles[turn], "layer", pairs))
    (total,) = small_call(sum_kernel, [jax.ShapeDtypeStruct(tiles[0].shape, jnp.float32)], *arrived)
    return total


def core_sum_kernel(kept_ref, arrived_ref, mine_ref, other_ref):
    rows = mine_ref.shape[0]
    chip = lax.div(layer_index(), 2)
    mine = pl.ds(pl.multiple_of(chip * rows, rows), rows)
    other = pl.ds(pl.multiple_of((1 - chip) * rows, rows), rows)
    mine_ref[...] = (kept_ref[mine, :] + arrived_ref[mine, :]).astype(mine_ref.dtype)
    other_ref[...] = (kept_ref[other, :] + arrived_ref[other, :]).astype(other_ref.dtype)


def chip_sum_kernel(mine_ref, arrived_ref, *out_refs):
    docs = out_refs[0].shape[1]
    for spot, out_ref in enumerate(out_refs):
        columns = slice(spot * docs, (spot + 1) * docs)
        total = mine_ref[:, columns] + arrived_ref[:, columns].astype(jnp.float32)
        out_ref[...] = total.astype(out_ref.dtype)


def swap(value, distance):
    count = lax.axis_size("layer")
    return lax.ppermute(value, "layer", [(lay, lay ^ distance) for lay in range(count)])


def core_sum(kept, arrived, mine_type):
    rows, width = kept.shape[0] // 2, kept.shape[1]
    out_shape = [jax.ShapeDtypeStruct((rows, width), out_type) for out_type in (mine_type, jnp.bfloat16)]
    return small_call(core_sum_kernel, out_shape, kept, arrived)


def layer_sum(kept, sent, out_types):
    mine, other = core_sum(kept, swap(sent, 1), jnp.float32)
    rows, docs = mine.shape[0], mine.shape[1] // len(out_types)
    out_shape = [jax.ShapeDtypeStruct((rows, docs), out_type) for out_type in out_types]
    return small_call(chip_sum_kernel, out_shape, mine, swap(other, 2))


ROUND_ONE = ((0, 2), (2, 3), (3, 1), (1, 0))
ROUND_TWO = ((0, 1), (1, 3), (3, 2), (2, 0))
BLOCK_ONE = (1, 3, 0, 2)
BLOCK_TWO = (2, 0, 3, 1)
BLOCK_LAST = (3, 2, 1, 0)


def pick(table):
    def entry(row):
        value = jnp.int32(table[0])
        for index in range(1, len(table)):
            value = jnp.where(row == index, jnp.int32(table[index]), value)
        return value

    return entry


def step_of(table):
    return pick([(block - table.index(block)) % STEPS for block in range(STEPS)])


def assemble_kernel(own_ref, first_ref, second_ref, out_ref):
    out_ref[0] = own_ref[...]
    for ref, table in ((first_ref, BLOCK_ONE), (second_ref, BLOCK_TWO)):
        out_ref[step_of(table)(row_index())] = ref[...].astype(jnp.float32)


def core_share(rows, own):
    core = lax.rem(layer_index(), 2)
    return pl.ds(pl.multiple_of((core if own else 1 - core) * rows, rows), rows)


def other_share_kernel(mine_ref, out_ref):
    out_ref[...] = mine_ref[core_share(out_ref.shape[0], False), :]


def finish_kernel(mine_ref, arrived_ref, scores_hbm, out_hbm, total, copied):
    del scores_hbm
    mine = mine_ref[core_share(total.shape[0], True), :].astype(jnp.float32)
    total[...] = mine + arrived_ref[...].astype(jnp.float32)
    copy = pltpu.make_async_copy(total, out_hbm.at[step_of(BLOCK_LAST)(row_index())], copied)
    copy.start()
    copy.wait()


def finish(mine, arrived, scores):
    hbm = pl.BlockSpec(memory_space=pltpu.HBM)
    vmem = pl.BlockSpec(memory_space=pltpu.VMEM)
    return pl.pallas_call(
        finish_kernel,
        out_shape=jax.ShapeDtypeStruct(scores.shape, scores.dtype),
        in_specs=[vmem, vmem, hbm],
        out_specs=hbm,
        scratch_shapes=[pltpu.VMEM(scores.shape[1:], jnp.float32), pltpu.SemaphoreType.DMA],
        input_output_aliases={2: 0},
        compiler_params=pltpu.CompilerParams(vmem_limit_bytes=4 * MIB),
    )(mine, arrived, scores)


def along_line(documents, conditioned, query_ids):
    docs = documents.shape[0]
    half = (conditioned.shape[0] // 2, docs)

    def halves(block, block_of, front=()):
        width = docs * (1 + bool(front))
        out_shape = [jax.ShapeDtypeStruct((half[0], width), jnp.float32)] * 2
        scratch = [pltpu.VMEM((2 * half[0], docs), jnp.float32)]
        kernel = functools.partial(halves_kernel, block_of)
        return scoring(kernel, out_shape, conditioned, query_ids, block, front, scratch)

    def one_half(block, block_of, kept):
        kernel = functools.partial(half_kernel, block_of, kept)
        out_shape = [jax.ShapeDtypeStruct(half, jnp.float32 if kept else jnp.bfloat16)]
        weight = 5 if kept else 1
        return scoring(kernel, out_shape, conditioned, query_ids, block, weight=weight)[0]

    def back(total, table):
        return lax.ppermute(total, "rows", tuple(enumerate(table)))

    one = lax.ppermute(documents, "rows", ROUND_ONE)
    two = lax.ppermute(documents, "rows", ROUND_TWO)
    own = halves(documents, lambda row: row)
    one, own = lax.optimization_barrier((one, own))
    three = lax.ppermute(one, "rows", ROUND_ONE)

    own, first = layer_sum(*halves(one, pick(BLOCK_ONE), own), (jnp.float32, jnp.bfloat16))
    two, first = lax.optimization_barrier((two, first))
    (second,) = layer_sum(*halves(two, pick(BLOCK_TWO)), (jnp.bfloat16,))
    three, *_ = lax.optimization_barrier((three, first, second))
    first, second = back(first, BLOCK_ONE), back(second, BLOCK_TWO)

    arrived = swap(one_half(three, pick(BLOCK_LAST), False), 1)
    three, first, second = lax.optimization_barrier((three, first, second))
    kept = one_half(three, pick(BLOCK_LAST), True)
    (both,) = small_call(sum_kernel, [jax.ShapeDtypeStruct(half, jnp.bfloat16)], kept, arrived)
    shares = lax.axis_size("layer")
    pairs = [
        (row * shares + lay, BLOCK_LAST[row] * shares + 2 * ((lay // 2) ^ (lay % 2)) + lay % 2)
        for row in range(len(BLOCK_LAST))
        for lay in range(shares)
    ]
    mine = lax.ppermute(both, ("rows", "layer"), pairs)
    out_shape = [jax.ShapeDtypeStruct((STEPS,) + own.shape, jnp.float32)]
    (scores,) = small_call(assemble_kernel, out_shape, own, first, second)
    mine, scores = lax.optimization_barrier((mine, scores))
    (other,) = small_call(other_share_kernel, [jax.ShapeDtypeStruct(own.shape, jnp.bfloat16)], mine)
    return finish(mine, swap(other, 1), scores)


def around_ring(documents, conditioned, query_ids):
    n_rows, shares = lax.axis_size("rows"), lax.axis_size("layer")
    rows, docs = conditioned.shape[0], documents.shape[0]
    result = []
    for step in range(STEPS):
        behind = [(row, (row - step) % n_rows) for row in range(n_rows)]
        block = lax.ppermute(documents, "rows", behind) if step else documents

        def ahead(row, step=step):
            return lax.rem(row + step, n_rows)

        kernel = functools.partial(turned_kernel, shares, ahead)
        out_shape = [jax.ShapeDtypeStruct((rows // shares, docs), jnp.bfloat16)] * shares
        scratch = [pltpu.VMEM((rows, docs), jnp.float32)]
        total = direct_sum(scoring(kernel, out_shape, conditioned, query_ids, block, (), scratch))
        onward = [(row, (row + step) % n_rows) for row in range(n_rows)]
        result.append(lax.ppermute(total, "rows", onward) if step else total)
    return jnp.stack(result)


def local(train_grads, query_grads, eigenbases, eigenvalues, layer_offsets, query_doc_ids):
    conditioned = prepare(query_grads, eigenbases, eigenvalues, layer_offsets)
    on_line = lax.axis_size("rows") == 4 and lax.axis_size("layer") == 4
    plan = along_line if on_line else around_ring
    return plan(train_grads, conditioned, query_doc_ids[:, None])


def solution(mesh):
    in_specs = (
        P(("group", "rows"), "layer"),
        P(("group", "rows"), "layer"),
        P("layer", None, None),
        P("layer", None),
        P("layer"),
        P(("group", "rows")),
    )
    out_specs = P(None, "layer", ("group", "rows"))
    return jax.shard_map(local, mesh=mesh, in_specs=in_specs, out_specs=out_specs, check_vma=False)
```

```python
import functools

import jax
import jax.numpy as jnp
from jax import lax
from jax.experimental import pallas as pl
from jax.experimental.pallas import tpu as pltpu
from jax.sharding import PartitionSpec as P

LDIM = 512
LAY_DEV = 4
STEPS = 4
DAMPING = 0.05
NT = (((1,), (1,)), ((), ()))
MIB = 1024 * 1024


def layer_index():
    return lax.axis_index("layer").astype(jnp.int32)


def row_index():
    return lax.axis_index("rows").astype(jnp.int32)


def prepare_kernel(
    offsets, queries_hbm, bases_hbm, values_hbm, conditioned_ref, queries, bases, values, arrived
):
    copies = [pltpu.make_async_copy(values_hbm, values, arrived.at[0])]
    for layer in range(LAY_DEV):
        columns = queries_hbm.at[:, layer * LDIM : (layer + 1) * LDIM]
        copies.append(pltpu.make_async_copy(columns, queries.at[layer], arrived.at[1 + 2 * layer]))
        copies.append(pltpu.make_async_copy(bases_hbm.at[layer], bases.at[layer], arrived.at[2 + 2 * layer]))
    for copy in copies:
        copy.start()
    base_column = layer_index() * (LAY_DEV * LDIM)
    copies[0].wait()
    for layer in range(LAY_DEV):
        copies[1 + 2 * layer].wait()
        copies[2 + 2 * layer].wait()
        basis = bases[layer]
        projected = jnp.dot(queries[layer], basis, preferred_element_type=jnp.float32)
        scaled = (projected / (values[layer : layer + 1, :] + DAMPING)).astype(jnp.bfloat16)
        restored = lax.dot_general(scaled, basis, NT, preferred_element_type=jnp.float32)
        first = pl.multiple_of(offsets[layer] - base_column, LDIM)
        conditioned_ref[:, pl.ds(first, LDIM)] = restored.astype(jnp.bfloat16)


def prepare(queries, bases, values, offsets):
    rows, dims = queries.shape
    hbm = pl.BlockSpec(memory_space=pltpu.HBM)
    return pl.pallas_call(
        prepare_kernel,
        out_shape=jax.ShapeDtypeStruct((rows, dims), jnp.bfloat16),
        in_specs=[pl.BlockSpec(memory_space=pltpu.SMEM), hbm, hbm, hbm],
        out_specs=pl.BlockSpec(memory_space=pltpu.VMEM),
        scratch_shapes=[
            pltpu.VMEM((LAY_DEV, rows, LDIM), jnp.bfloat16),
            pltpu.VMEM(bases.shape, jnp.bfloat16),
            pltpu.VMEM(values.shape, jnp.float32),
            pltpu.SemaphoreType.DMA((1 + 2 * LAY_DEV,)),
        ],
        compiler_params=pltpu.CompilerParams(vmem_limit_bytes=62 * MIB),
        cost_estimate=pl.CostEstimate(
            flops=4 * rows * dims * LDIM, bytes_accessed=6 * MIB, transcendentals=0
        ),
    )(offsets, queries, bases, values)


def masked_tile(queries, documents, query_ids, block):
    tile = lax.dot_general(queries, documents, NT, preferred_element_type=jnp.float32)
    doc_ids = block * tile.shape[1] + lax.broadcasted_iota(jnp.int32, tile.shape, 1)
    return jnp.where(query_ids == doc_ids, 0.0, tile)


def scoring(kernel, out_shape, conditioned, query_ids, documents, extra=(), scratch=(), weight=1):
    dims = conditioned.shape[1]
    docs = documents.shape[0]
    rows = sum(shape.shape[0] for shape in out_shape)
    vmem = pl.BlockSpec(memory_space=pltpu.VMEM)
    return pl.pallas_call(
        kernel,
        out_shape=out_shape,
        in_specs=[vmem] * (3 + len(extra)),
        out_specs=[vmem] * len(out_shape),
        scratch_shapes=scratch,
        compiler_params=pltpu.CompilerParams(vmem_limit_bytes=12 * MIB),
        cost_estimate=pl.CostEstimate(
            flops=2 * rows * docs * dims * weight, bytes_accessed=2 * dims * (rows + docs) * weight, transcendentals=0
        ),
    )(conditioned, query_ids, documents, *extra)


def turned_kernel(shares, block_of, queries_ref, ids_ref, documents_ref, *refs):
    *out_refs, held = refs
    held[...] = masked_tile(queries_ref[...], documents_ref[...], ids_ref[...], block_of(row_index()))
    for turn, out_ref in enumerate(out_refs):
        share_rows = out_ref.shape[0]
        first = pl.multiple_of(lax.rem(layer_index() + turn, shares) * share_rows, share_rows)
        out_ref[...] = held[pl.ds(first, share_rows), :].astype(jnp.bfloat16)


def half_shares(share_rows, kept):
    core = lax.rem(layer_index(), 2)
    core = core if kept else 1 - core
    return [pl.multiple_of((2 * chip + core) * share_rows, share_rows) for chip in range(2)]


def halves_kernel(block_of, queries_ref, ids_ref, documents_ref, *refs):
    front_refs, out_refs, held = refs[:-3], refs[-3:-1], refs[-1]
    held[...] = masked_tile(queries_ref[...], documents_ref[...], ids_ref[...], block_of(row_index()))
    docs = documents_ref.shape[0]
    rows, width = out_refs[0].shape
    for side, kept in enumerate((True, False)):
        if front_refs:
            out_refs[side][:, : width - docs] = front_refs[side][...]
        for chip, first in enumerate(half_shares(rows // 2, kept)):
            spot = slice(chip * (rows // 2), (chip + 1) * (rows // 2))
            out_refs[side][spot, width - docs :] = held[pl.ds(first, rows // 2), :]


def target_chip():
    chip, core = lax.div(layer_index(), 2), lax.rem(layer_index(), 2)
    return jnp.where(chip == core, 0, 1)


def half_kernel(block_of, kept, queries_ref, ids_ref, documents_ref, out_ref):
    rows = out_ref.shape[0]
    chip = target_chip() if kept else 1 - target_chip()
    spot = pl.ds(pl.multiple_of(chip * rows, rows), rows)
    tile = masked_tile(queries_ref[spot, :], documents_ref[...], ids_ref[spot, :], block_of(row_index()))
    out_ref[...] = tile.astype(out_ref.dtype)


def total_of(refs):
    total = refs[0][...].astype(jnp.float32)
    for ref in refs[1:]:
        total += ref[...].astype(jnp.float32)
    return total


def sum_kernel(*refs):
    refs[-1][...] = total_of(refs[:-1]).astype(refs[-1].dtype)


def small_call(kernel, out_shape, *args):
    vmem = pl.BlockSpec(memory_space=pltpu.VMEM)
    return pl.pallas_call(
        kernel,
        out_shape=out_shape,
        in_specs=[vmem] * len(args),
        out_specs=[vmem] * len(out_shape),
        compiler_params=pltpu.CompilerParams(vmem_limit_bytes=4 * MIB),
    )(*args)


def direct_sum(tiles):
    shares = len(tiles)
    arrived = [tiles[0]]
    for turn in range(1, shares):
        pairs = [(lay, (lay + turn) % shares) for lay in range(shares)]
        arrived.append(lax.ppermute(tiles[turn], "layer", pairs))
    (total,) = small_call(sum_kernel, [jax.ShapeDtypeStruct(tiles[0].shape, jnp.float32)], *arrived)
    return total


def core_sum_kernel(kept_ref, arrived_ref, mine_ref, other_ref):
    rows = mine_ref.shape[0]
    chip = lax.div(layer_index(), 2)
    mine = pl.ds(pl.multiple_of(chip * rows, rows), rows)
    other = pl.ds(pl.multiple_of((1 - chip) * rows, rows), rows)
    mine_ref[...] = (kept_ref[mine, :] + arrived_ref[mine, :]).astype(mine_ref.dtype)
    other_ref[...] = (kept_ref[other, :] + arrived_ref[other, :]).astype(other_ref.dtype)


def chip_sum_kernel(mine_ref, arrived_ref, *out_refs):
    docs = out_refs[0].shape[1]
    for spot, out_ref in enumerate(out_refs):
        columns = slice(spot * docs, (spot + 1) * docs)
        total = mine_ref[:, columns] + arrived_ref[:, columns].astype(jnp.float32)
        out_ref[...] = total.astype(out_ref.dtype)


def swap(value, distance):
    count = lax.axis_size("layer")
    return lax.ppermute(value, "layer", [(lay, lay ^ distance) for lay in range(count)])


def core_sum(kept, arrived, mine_type):
    rows, width = kept.shape[0] // 2, kept.shape[1]
    out_shape = [jax.ShapeDtypeStruct((rows, width), out_type) for out_type in (mine_type, jnp.bfloat16)]
    return small_call(core_sum_kernel, out_shape, kept, arrived)


def layer_sum(kept, sent, out_types):
    mine, other = core_sum(kept, swap(sent, 1), jnp.float32)
    rows, docs = mine.shape[0], mine.shape[1] // len(out_types)
    out_shape = [jax.ShapeDtypeStruct((rows, docs), out_type) for out_type in out_types]
    return small_call(chip_sum_kernel, out_shape, mine, swap(other, 2))


ROUND_ONE = ((0, 2), (2, 3), (3, 1), (1, 0))
ROUND_TWO = ((0, 1), (1, 3), (3, 2), (2, 0))
BLOCK_ONE = (1, 3, 0, 2)
BLOCK_TWO = (2, 0, 3, 1)
BLOCK_LAST = (3, 2, 1, 0)


def pick(table):
    def entry(row):
        value = jnp.int32(table[0])
        for index in range(1, len(table)):
            value = jnp.where(row == index, jnp.int32(table[index]), value)
        return value

    return entry


def step_of(table):
    return pick([(block - table.index(block)) % STEPS for block in range(STEPS)])


def assemble_kernel(own_ref, first_ref, second_ref, out_ref):
    out_ref[0] = own_ref[...]
    for ref, table in ((first_ref, BLOCK_ONE), (second_ref, BLOCK_TWO)):
        out_ref[step_of(table)(row_index())] = ref[...].astype(jnp.float32)


def core_share(rows, own):
    core = lax.rem(layer_index(), 2)
    return pl.ds(pl.multiple_of((core if own else 1 - core) * rows, rows), rows)


def other_share_kernel(mine_ref, out_ref):
    out_ref[...] = mine_ref[core_share(out_ref.shape[0], False), :]


def finish_kernel(mine_ref, arrived_ref, scores_hbm, out_hbm, total, copied):
    del scores_hbm
    mine = mine_ref[core_share(total.shape[0], True), :].astype(jnp.float32)
    total[...] = mine + arrived_ref[...].astype(jnp.float32)
    copy = pltpu.make_async_copy(total, out_hbm.at[step_of(BLOCK_LAST)(row_index())], copied)
    copy.start()
    copy.wait()


def finish(mine, arrived, scores):
    hbm = pl.BlockSpec(memory_space=pltpu.HBM)
    vmem = pl.BlockSpec(memory_space=pltpu.VMEM)
    return pl.pallas_call(
        finish_kernel,
        out_shape=jax.ShapeDtypeStruct(scores.shape, scores.dtype),
        in_specs=[vmem, vmem, hbm],
        out_specs=hbm,
        scratch_shapes=[pltpu.VMEM(scores.shape[1:], jnp.float32), pltpu.SemaphoreType.DMA],
        input_output_aliases={2: 0},
        compiler_params=pltpu.CompilerParams(vmem_limit_bytes=4 * MIB),
    )(mine, arrived, scores)


def along_line(documents, conditioned, query_ids):
    docs = documents.shape[0]
    half = (conditioned.shape[0] // 2, docs)

    def halves(block, block_of, front=()):
        width = docs * (1 + bool(front))
        out_shape = [jax.ShapeDtypeStruct((half[0], width), jnp.float32)] * 2
        scratch = [pltpu.VMEM((2 * half[0], docs), jnp.float32)]
        kernel = functools.partial(halves_kernel, block_of)
        return scoring(kernel, out_shape, conditioned, query_ids, block, front, scratch)

    def one_half(block, block_of, kept):
        kernel = functools.partial(half_kernel, block_of, kept)
        out_shape = [jax.ShapeDtypeStruct(half, jnp.float32 if kept else jnp.bfloat16)]
        weight = 5 if kept else 1
        return scoring(kernel, out_shape, conditioned, query_ids, block, weight=weight)[0]

    def back(total, table):
        return lax.ppermute(total, "rows", tuple(enumerate(table)))

    one = lax.ppermute(documents, "rows", ROUND_ONE)
    two = lax.ppermute(documents, "rows", ROUND_TWO)
    own = halves(documents, lambda row: row)
    three = lax.ppermute(one, "rows", ROUND_ONE)

    own, first = layer_sum(*halves(one, pick(BLOCK_ONE), own), (jnp.float32, jnp.bfloat16))
    two, first = lax.optimization_barrier((two, first))
    (second,) = layer_sum(*halves(two, pick(BLOCK_TWO)), (jnp.bfloat16,))
    three, *_ = lax.optimization_barrier((three, first, second))
    first, second = back(first, BLOCK_ONE), back(second, BLOCK_TWO)

    arrived = swap(one_half(three, pick(BLOCK_LAST), False), 1)
    three, first, second = lax.optimization_barrier((three, first, second))
    kept = one_half(three, pick(BLOCK_LAST), True)
    (both,) = small_call(sum_kernel, [jax.ShapeDtypeStruct(half, jnp.bfloat16)], kept, arrived)
    shares = lax.axis_size("layer")
    pairs = [
        (row * shares + lay, BLOCK_LAST[row] * shares + 2 * ((lay // 2) ^ (lay % 2)) + lay % 2)
        for row in range(len(BLOCK_LAST))
        for lay in range(shares)
    ]
    mine = lax.ppermute(both, ("rows", "layer"), pairs)
    out_shape = [jax.ShapeDtypeStruct((STEPS,) + own.shape, jnp.float32)]
    (scores,) = small_call(assemble_kernel, out_shape, own, first, second)
    (other,) = small_call(other_share_kernel, [jax.ShapeDtypeStruct(own.shape, jnp.bfloat16)], mine)
    return finish(mine, swap(other, 1), scores)


def around_ring(documents, conditioned, query_ids):
    n_rows, shares = lax.axis_size("rows"), lax.axis_size("layer")
    rows, docs = conditioned.shape[0], documents.shape[0]
    result = []
    for step in range(STEPS):
        behind = [(row, (row - step) % n_rows) for row in range(n_rows)]
        block = lax.ppermute(documents, "rows", behind) if step else documents

        def ahead(row, step=step):
            return lax.rem(row + step, n_rows)

        kernel = functools.partial(turned_kernel, shares, ahead)
        out_shape = [jax.ShapeDtypeStruct((rows // shares, docs), jnp.bfloat16)] * shares
        scratch = [pltpu.VMEM((rows, docs), jnp.float32)]
        total = direct_sum(scoring(kernel, out_shape, conditioned, query_ids, block, (), scratch))
        onward = [(row, (row + step) % n_rows) for row in range(n_rows)]
        result.append(lax.ppermute(total, "rows", onward) if step else total)
    return jnp.stack(result)


def local(train_grads, query_grads, eigenbases, eigenvalues, layer_offsets, query_doc_ids):
    conditioned = prepare(query_grads, eigenbases, eigenvalues, layer_offsets)
    on_line = lax.axis_size("rows") == 4 and lax.axis_size("layer") == 4
    plan = along_line if on_line else around_ring
    return plan(train_grads, conditioned, query_doc_ids[:, None])


def solution(mesh):
    in_specs = (
        P(("group", "rows"), "layer"),
        P(("group", "rows"), "layer"),
        P("layer", None, None),
        P("layer", None),
        P("layer"),
        P(("group", "rows")),
    )
    out_specs = P(None, "layer", ("group", "rows"))
    return jax.shard_map(local, mesh=mesh, in_specs=in_specs, out_specs=out_specs, check_vma=False)
```
